32 devices in a mesh: dp: 16 (over z, y, x), tensor: 2 (over core).
Axes of the slice: x: 2, y: 2, z: 4, core: 2. Of those that a mesh axis runs over, the one named last changes fastest.
Arguments:
- hidden_in: bfloat16 [32768, 768], P('dp'), may hold values from -6 to 6
- grad_out: bfloat16 [32768, 768], P('dp'), may hold values from -6 to 6
- lengths: int32 [128], P('dp'), may hold values from 16 to 256, as said below
- key_mask: int32 [128, 256], P('dp'), may hold values 0 or 1
- triple_weight: bfloat16 [3, 768, 768], P(None, None, 'tensor'), may hold values from -0.21875 to 0.21875
- outward_weight: bfloat16 [768, 768], P('tensor'), may hold values from -1.25 to 1.25
- expand_weight: bfloat16 [768, 3072], P(None, 'tensor'), may hold values from -0.21875 to 0.21875
- contract_weight: bfloat16 [3072, 768], P('tensor'), may hold values from -0.109375 to 0.109375
- triple_master: float32 [3, 768, 768], P(None, 'dp', 'tensor'), may hold values from -0.21875 to 0.21875
- triple_first: float32 [3, 768, 768], P(None, 'dp', 'tensor'), may hold values from -512 to 512
- triple_second: float32 [3, 768, 768], P(None, 'dp', 'tensor'), may hold values from 8192 to 32768
- outward_master: float32 [768, 768], P('tensor', 'dp'), may hold values from -1.25 to 1.25
- outward_first: float32 [768, 768], P('tensor', 'dp'), may hold values from -160 to 160
- outward_second: float32 [768, 768], P('tensor', 'dp'), may hold values from 737.28 to 2949.12
- expand_master: float32 [768, 3072], P('dp', 'tensor'), may hold values from -0.21875 to 0.21875
- expand_first: float32 [768, 3072], P('dp', 'tensor'), may hold values from -256 to 256
- expand_second: float32 [768, 3072], P('dp', 'tensor'), may hold values from 2048 to 8192
- contract_master: float32 [3072, 768], P('tensor', 'dp'), may hold values from -0.109375 to 0.109375
- contract_first: float32 [3072, 768], P('tensor', 'dp'), may hold values from -512 to 512
- contract_second: float32 [3072, 768], P('tensor', 'dp'), may hold values from 8192 to 32768
- pair_bias: float32 [2, 768], P(None, 'tensor'), may hold values from -3 to 3
- pair_first: float32 [2, 768], P(None, 'tensor'), may hold values from -512 to 512
- pair_second: float32 [2, 768], P(None, 'tensor'), may hold values from 8192 to 32768
- expand_bias: float32 [3072], P('tensor'), may hold values from -3 to 3
- expand_bias_first: float32 [3072], P('tensor'), may hold values from -256 to 256
- expand_bias_second: float32 [3072], P('tensor'), may hold values from 2048 to 8192
- norm_vectors: float32 [6, 768], replicated, may hold values from -0.9 to 1.45
- vectors_first: float32 [6, 768], replicated, may hold values from -896 to 896
- vectors_second: float32 [6, 768], replicated, may hold values from 20971.52 to 83886.08
Outputs:
- layer_out: bfloat16 [32768, 768], P('dp')
- input_grad: float32 [32768, 768], P('dp')
- triple_master_new: float32 [3, 768, 768], P(None, 'dp', 'tensor')
- triple_first_new: float32 [3, 768, 768], P(None, 'dp', 'tensor')
- triple_second_new: float32 [3, 768, 768], P(None, 'dp', 'tensor')
- triple_copy: bfloat16 [3, 768, 768], P(None, None, 'tensor')
- outward_master_new: float32 [768, 768], P('tensor', 'dp')
- outward_first_new: float32 [768, 768], P('tensor', 'dp')
- outward_second_new: float32 [768, 768], P('tensor', 'dp')
- outward_copy: bfloat16 [768, 768], P('tensor')
- expand_master_new: float32 [768, 3072], P('dp', 'tensor')
- expand_first_new: float32 [768, 3072], P('dp', 'tensor')
- expand_second_new: float32 [768, 3072], P('dp', 'tensor')
- expand_copy: bfloat16 [768, 3072], P(None, 'tensor')
- contract_master_new: float32 [3072, 768], P('tensor', 'dp')
- contract_first_new: float32 [3072, 768], P('tensor', 'dp')
- contract_second_new: float32 [3072, 768], P('tensor', 'dp')
- contract_copy: bfloat16 [3072, 768], P('tensor')
- pair_bias_new: float32 [2, 768], P(None, 'tensor')
- pair_first_new: float32 [2, 768], P(None, 'tensor')
- pair_second_new: float32 [2, 768], P(None, 'tensor')
- expand_bias_new: float32 [3072], P('tensor')
- expand_bias_first_new: float32 [3072], P('tensor')
- expand_bias_second_new: float32 [3072], P('tensor')
- vectors_new: float32 [6, 768], replicated
- vectors_first_new: float32 [6, 768], replicated
- vectors_second_new: float32 [6, 768], replicated
The draws below stay inside these ranges and needn't reach their ends.
Inputs may be any that keep to these rules, and one draw needn't show every extreme that they name: `lengths`: each sequence has at least 1 used slot, and some sequence of the batch uses all 256.
All inputs are finite; a program needn't handle non-finite values. No bound on the sum of `key_mask` on one device may be relied on, other than what follows from the above.
Results may differ from the reference program's by a relative error of at most 0.017.
The reference program's roundings to bfloat16 on the way count: a program that leaves them out, or rounds other values in their place, can miss the bound.
Values may be sent and summed in bfloat16 or wider, within the bound.
No kernel may reach another device: no remote copies, remote signals or barrier semaphores. Data moves between devices by JAX's collectives and lax.ppermute only.
A program may use at most 192 MiB of HBM per device.

```python
import math
import jax
import jax.numpy as jnp
from jax import lax

D = 768
HEADS = 12
FF = 3072
HEAD_DIM = 64
SEQ_LEN = 256
SEQS_DEV = 8
STEP = 7
SEQS = 128
TOKENS = 32768
N_DP = 16
N_TENSOR = 2


def draw_lengths(key, part):
    key = jax.random.fold_in(key, 11)
    pick_key, short_key, long_key, which_key = jax.random.split(key, 4)
    low_len = max(2, SEQ_LEN // 16)
    half_len = SEQ_LEN // 2
    short_len = jax.random.randint(short_key, (SEQS,), low_len, half_len + 1)
    long_len = jax.random.randint(long_key, (SEQS,), half_len, SEQ_LEN + 1)
    long_flag = jax.random.randint(pick_key, (SEQS,), 0, 4) == 0
    chosen = jnp.where(long_flag, long_len, short_len)
    forced = jax.random.randint(which_key, (), 0, SEQS)
    return jnp.where(jnp.arange(SEQS) == forced, SEQ_LEN, chosen).astype(jnp.int32)


def draw_norm_vectors(key, part):
    key = jax.random.fold_in(key, 12)
    base = jnp.clip(jax.random.normal(key, (6, D), jnp.float32), -3.0, 3.0)
    row_index = lax.broadcasted_iota(jnp.int32, (6, D), 0)
    gain_rows = (row_index == 2) | (row_index == 4)
    return jnp.where(gain_rows, 1.0 + 0.15 * base, 0.3 * base).astype(jnp.float32)


def with_ends(drawn, own_key, least, top_value):
    longest = drawn.shape.index(max(drawn.shape))
    spots = []
    for shift in (0, 1):
        where = [jax.random.randint(jax.random.fold_in(own_key, axis), (), 0, length) for axis, length in enumerate(drawn.shape)]
        where[longest] = (where[longest] + shift) % drawn.shape[longest]
        spots.append(tuple(where))
    return drawn.at[spots[0]].set(least).at[spots[1]].set(top_value)


def strengthened(result, key, source, target, parts, factor):
    owner, partner = [(jnp.arange(result.shape[axis_at]) // (result.shape[axis_at] // parts)).reshape([-1 if axis == axis_at else 1 for axis in range(result.ndim)]) for axis_at in (source, target)]
    chosen = jax.random.permutation(key, parts)[partner]
    strong = (owner == chosen) | (owner == (partner + parts // 2) % parts)
    return jnp.where(strong, factor * result, result)


def level_of(stream_key, extent, cuts, smallest, high):
    def one(axis_at, blocks):
        heights = jax.random.uniform(jax.random.fold_in(jax.random.fold_in(stream_key, 6), axis_at), (blocks,), jnp.float32, smallest / len(cuts), high / len(cuts))
        return jnp.repeat(jnp.exp(heights), extent[axis_at] // blocks).reshape((-1,) + (1,) * (len(extent) - axis_at - 1))

    loudness = one(*cuts[0])
    for cut in cuts[1:]:
        loudness = loudness * one(*cut)
    return loudness


def gaussian(own_key, shape, deviation, most, cuts=(), kind=jnp.bfloat16):
    result = deviation * jax.random.normal(own_key, shape, jnp.float32)
    if cuts:
        result = result * level_of(own_key, shape, cuts, -0.22, 0.18)
    return jnp.clip(result, -most, most).astype(kind)


def bell_draw_with(own_key, shape, scale, limit, shards, heavy, kind=jnp.bfloat16):
    drawn = scale * jax.random.normal(own_key, shape, jnp.float32)
    if shards:
        drawn = drawn * level_of(own_key, shape, shards, -0.22, 0.18)
    return jnp.clip(strengthened(drawn, jax.random.fold_in(own_key, 3), *heavy), -limit, limit).astype(kind)


def setup_inputs(seed: int = 0) -> dict:
    splits = jax.random.split(jax.random.key(seed), 30)
    hidden_in = bell_draw_with(splits[0], (TOKENS, D), 1.0, 6.0, ((0, 16),), (0, 1, 16, 2.0))
    grad_out = bell_draw_with(splits[1], (TOKENS, D), 1.0, 6.0, ((0, 16),), (0, 1, 16, 2.0))
    lengths = draw_lengths(jax.random.fold_in(splits[29], 71), 0)
    key_mask = with_ends((jax.random.randint(splits[3], (SEQS, SEQ_LEN), 0, 8) < 7).astype(jnp.int32), jax.random.fold_in(splits[3], 1), 0, 1)
    triple_weight = gaussian(splits[4], (3, D, D), D ** -0.5, 0.21875, ((2, 2),))
    outward_weight = gaussian(splits[5], (D, D), (D // 32) ** -0.5, 1.25, ((0, 2),))
    expand_weight = gaussian(splits[6], (D, FF), D ** -0.5, 0.21875, ((1, 2),))
    contract_weight = gaussian(splits[7], (FF, D), FF ** -0.5, 0.109375, ((0, 2),))
    triple_master = gaussian(splits[8], (3, D, D), D ** -0.5, 0.21875, ((1, 16), (2, 2)), jnp.float32)
    triple_first = gaussian(splits[9], (3, D, D), (0.5 * TOKENS ** 0.5), 512.0, ((1, 16), (2, 2)), jnp.float32)
    triple_second = jnp.clip(jnp.exp(math.log(32768.0) - 1.3862944 * jax.random.uniform(splits[10], (3, D, D), jnp.float32) ** level_of(splits[10], (3, D, D), ((1, 16), (2, 2)), -0.2, 0.2)), 8192.0, 32768.0)
    outward_master = gaussian(splits[11], (D, D), (D // 32) ** -0.5, 1.25, ((0, 2), (1, 16)), jnp.float32)
    outward_first = gaussian(splits[12], (D, D), (0.15 * TOKENS ** 0.5), 160.0, ((0, 2), (1, 16)), jnp.float32)
    outward_second = jnp.clip(jnp.exp(math.log(2949.12) - 1.3862944 * jax.random.uniform(splits[13], (D, D), jnp.float32) ** level_of(splits[13], (D, D), ((0, 2), (1, 16)), -0.2, 0.2)), 737.28, 2949.12)
    expand_master = gaussian(splits[14], (D, FF), D ** -0.5, 0.21875, ((0, 16), (1, 2)), jnp.float32)
    expand_first = gaussian(splits[15], (D, FF), (0.25 * TOKENS ** 0.5), 256.0, ((0, 16), (1, 2)), jnp.float32)
    expand_second = jnp.clip(jnp.exp(math.log(8192.0) - 1.3862944 * jax.random.uniform(splits[16], (D, FF), jnp.float32) ** level_of(splits[16], (D, FF), ((0, 16), (1, 2)), -0.2, 0.2)), 2048.0, 8192.0)
    contract_master = gaussian(splits[17], (FF, D), FF ** -0.5, 0.109375, ((0, 2), (1, 16)), jnp.float32)
    contract_first = gaussian(splits[18], (FF, D), (0.5 * TOKENS ** 0.5), 512.0, ((0, 2), (1, 16)), jnp.float32)
    contract_second = jnp.clip(jnp.exp(math.log(32768.0) - 1.3862944 * jax.random.uniform(splits[19], (FF, D), jnp.float32) ** level_of(splits[19], (FF, D), ((0, 2), (1, 16)), -0.2, 0.2)), 8192.0, 32768.0)
    pair_bias = gaussian(splits[20], (2, D), 0.3, 3.0, ((1, 2),), jnp.float32)
    pair_first = gaussian(splits[21], (2, D), (0.5 * TOKENS ** 0.5), 512.0, ((1, 2),), jnp.float32)
    pair_second = jnp.clip(jnp.exp(math.log(32768.0) - 1.3862944 * jax.random.uniform(splits[22], (2, D), jnp.float32) ** level_of(splits[22], (2, D), ((1, 2),), -0.2, 0.2)), 8192.0, 32768.0)
    expand_bias = gaussian(splits[23], (FF,), 0.3, 3.0, ((0, 2),), jnp.float32)
    expand_bias_first = gaussian(splits[24], (FF,), (0.25 * TOKENS ** 0.5), 256.0, ((0, 2),), jnp.float32)
    expand_bias_second = jnp.clip(jnp.exp(math.log(8192.0) - 1.3862944 * jax.random.uniform(splits[25], (FF,), jnp.float32) ** level_of(splits[25], (FF,), ((0, 2),), -0.2, 0.2)), 2048.0, 8192.0)
    norm_vectors = draw_norm_vectors(jax.random.fold_in(splits[29], 71), 0)
    vectors_first = gaussian(splits[27], (6, D), (0.8 * TOKENS ** 0.5), 896.0, (), jnp.float32)
    vectors_second = jnp.clip(jnp.exp(jax.random.uniform(splits[28], (6, D), jnp.float32, math.log(20971.52), math.log(83886.08))), 20971.52, 83886.08)
    return {"hidden_in": hidden_in, "grad_out": grad_out, "lengths": lengths, "key_mask": key_mask, "triple_weight": triple_weight, "outward_weight": outward_weight, "expand_weight": expand_weight, "contract_weight": contract_weight, "triple_master": triple_master, "triple_first": triple_first, "triple_second": triple_second, "outward_master": outward_master, "outward_first": outward_first, "outward_second": outward_second, "expand_master": expand_master, "expand_first": expand_first, "expand_second": expand_second, "contract_master": contract_master, "contract_first": contract_first, "contract_second": contract_second, "pair_bias": pair_bias, "pair_first": pair_first, "pair_second": pair_second, "expand_bias": expand_bias, "expand_bias_first": expand_bias_first, "expand_bias_second": expand_bias_second, "norm_vectors": norm_vectors, "vectors_first": vectors_first, "vectors_second": vectors_second}


@jax.custom_vjp
def low(v):
    return lax.optimization_barrier(v.astype(jnp.bfloat16)).astype(jnp.float32)

@jax.custom_vjp
def low_back(v):
    return v

def low_keep(v):
    return (low(v), None)

def low_pass(kept, grad):
    return (grad,)

def back_keep(v):
    return (v, None)

def back_low(kept, grad):
    return (low(grad),)
low.defvjp(low_keep, low_pass)
low_back.defvjp(back_keep, back_low)
HIGHEST = lax.Precision.HIGHEST
MASK_FILL = -1e+30
NORM_EPSILON = 1e-05
FIRST_DECAY = 0.5
SECOND_DECAY = 0.5
LEARN_RATE = 0.1
WEIGHT_DECAY = 0.01
EPSILON = 1e-08

def norm_rows(inputs):
    row_mean = lax.optimization_barrier(jnp.mean(inputs, axis=-1, keepdims=True))
    centred = inputs - row_mean
    spread = lax.optimization_barrier(jnp.mean(centred * centred, axis=-1, keepdims=True))
    return centred * lax.rsqrt(spread + NORM_EPSILON)

def attend(pieces):
    queries, key_rows, values, valid_block = pieces
    scores = low_back(jnp.einsum('sqhd,skhd->shqk', queries, key_rows, precision=HIGHEST) * HEAD_DIM ** (-0.5))
    mask_rows = valid_block[:, None, None, :]
    masked = jnp.where(mask_rows, scores, MASK_FILL)
    row_top = lax.optimization_barrier(jnp.max(masked, axis=-1, keepdims=True))
    exp_terms = jnp.where(mask_rows, jnp.exp(masked - row_top), 0.0)
    probs_full = exp_terms / lax.optimization_barrier(jnp.sum(exp_terms, axis=-1, keepdims=True))
    context = jnp.einsum('shqk,skhd->sqhd', low(probs_full), values, precision=HIGHEST)
    return low_back(low(context))

def sum_groups(left_side, right_side, group_width):
    running = jnp.zeros((left_side.shape[0], right_side.shape[1]), left_side.dtype)
    for group_index in range(N_TENSOR):
        lower = group_index * group_width
        upper = lower + group_width
        running = running + low(jnp.dot(left_side[:, lower:upper], right_side[lower:upper], precision=HIGHEST))
    return running

def adamw_step(master, first_moment, second_moment, gradient, decay_rate):
    first_new = FIRST_DECAY * first_moment + (1.0 - FIRST_DECAY) * gradient
    second_new = SECOND_DECAY * second_moment + (1.0 - SECOND_DECAY) * gradient * gradient
    first_fixed = first_new / (1.0 - FIRST_DECAY ** STEP)
    second_fixed = second_new / (1.0 - SECOND_DECAY ** STEP)
    direction = first_fixed / (jnp.sqrt(second_fixed) + EPSILON)
    master_new = master - LEARN_RATE * (direction + decay_rate * master)
    return (master_new, first_new, second_new)

def reference(hidden_in, grad_out, lengths, key_mask, triple_weight, outward_weight, expand_weight, contract_weight, triple_master, triple_first, triple_second, outward_master, outward_first, outward_second, expand_master, expand_first, expand_second, contract_master, contract_first, contract_second, pair_bias, pair_first, pair_second, expand_bias, expand_bias_first, expand_bias_second, norm_vectors, vectors_first, vectors_second):
    positions = jnp.arange(SEQ_LEN, dtype=jnp.int32)[None, :]
    valid_keys = (positions < lengths[:, None]) & ((key_mask == 1) | (positions == 0))
    valid_groups = valid_keys.reshape(N_DP, SEQS_DEV, SEQ_LEN)

    def layer(inputs, triple, outward, expand, contract, pair_vec, widen_bias, vectors):
        projected = jnp.einsum('td,jdc->jtc', inputs, triple, precision=HIGHEST)
        offsets = jnp.stack([pair_vec[0], jnp.zeros_like(pair_vec[0]), pair_vec[1]])
        projected = low_back(low(projected + offsets[:, None, :]))
        head_split = projected.reshape(3, N_DP, SEQS_DEV, SEQ_LEN, HEADS, HEAD_DIM)
        context = lax.map(jax.checkpoint(attend), (head_split[0], head_split[1], head_split[2], valid_groups))
        context = context.reshape(TOKENS, D)
        attention_sum = low_back(sum_groups(context, outward, D // N_TENSOR))
        pre_one = inputs + attention_sum + vectors[0]
        hidden_one = norm_rows(pre_one) * vectors[2] + vectors[3]
        widened = low_back(jnp.dot(low(hidden_one), expand, precision=HIGHEST) + widen_bias)
        activated = low(jax.nn.gelu(widened, approximate=False))
        ffn_sum = low_back(sum_groups(activated, contract, FF // N_TENSOR))
        pre_two = hidden_one + ffn_sum + vectors[1]
        return norm_rows(pre_two) * vectors[4] + vectors[5]
    primals = (hidden_in.astype(jnp.float32), triple_weight.astype(jnp.float32), outward_weight.astype(jnp.float32), expand_weight.astype(jnp.float32), contract_weight.astype(jnp.float32), pair_bias, expand_bias, norm_vectors)
    layer_value, pullback = jax.vjp(layer, *primals)
    gradients = pullback(grad_out.astype(jnp.float32))
    triple_new = adamw_step(triple_master, triple_first, triple_second, gradients[1], WEIGHT_DECAY)
    outward_new = adamw_step(outward_master, outward_first, outward_second, gradients[2], WEIGHT_DECAY)
    expand_new = adamw_step(expand_master, expand_first, expand_second, gradients[3], WEIGHT_DECAY)
    contract_new = adamw_step(contract_master, contract_first, contract_second, gradients[4], WEIGHT_DECAY)
    pair_new = adamw_step(pair_bias, pair_first, pair_second, gradients[5], 0.0)
    widen_new = adamw_step(expand_bias, expand_bias_first, expand_bias_second, gradients[6], 0.0)
    vectors_new = adamw_step(norm_vectors, vectors_first, vectors_second, gradients[7], 0.0)
    return (layer_value.astype(jnp.bfloat16), gradients[0], triple_new[0], triple_new[1], triple_new[2], triple_new[0].astype(jnp.bfloat16), outward_new[0], outward_new[1], outward_new[2], outward_new[0].astype(jnp.bfloat16), expand_new[0], expand_new[1], expand_new[2], expand_new[0].astype(jnp.bfloat16), contract_new[0], contract_new[1], contract_new[2], contract_new[0].astype(jnp.bfloat16), pair_new[0], pair_new[1], pair_new[2], widen_new[0], widen_new[1], widen_new[2], vectors_new[0], vectors_new[1], vectors_new[2])
```

```python
from functools import partial

import jax
import jax.numpy as jnp
from jax import lax
from jax.sharding import PartitionSpec as P

HEAD_DIM = 64
STEP = 7


MASK_FILL = -1e30
NORM_EPSILON = 1e-05
FIRST_DECAY = 0.5
SECOND_DECAY = 0.5
LEARN_RATE = 0.1
WEIGHT_DECAY = 0.01
EPSILON = 1e-08
LOW = jnp.bfloat16
WIDE = jnp.float32


def norm_rows(inputs):
    row_mean = jnp.mean(inputs, axis=-1, keepdims=True)
    centred = inputs - row_mean
    spread = jnp.mean(centred * centred, axis=-1, keepdims=True)
    inverse = lax.rsqrt(spread + NORM_EPSILON)
    return (centred * inverse, inverse[:, 0])


def norm_back(upstream, normed, inverse, gain_row):
    scaled = upstream * gain_row
    first_mean = jnp.mean(scaled, axis=-1, keepdims=True)
    cross_mean = jnp.mean(scaled * normed, axis=-1, keepdims=True)
    return inverse[:, None] * (scaled - first_mean - normed * cross_mean)


def adamw_step(master, first_moment, second_moment, gradient, decay_rate):
    first_new = FIRST_DECAY * first_moment + (1.0 - FIRST_DECAY) * gradient
    second_new = SECOND_DECAY * second_moment + (1.0 - SECOND_DECAY) * gradient * gradient
    first_fixed = first_new / (1.0 - FIRST_DECAY**STEP)
    second_fixed = second_new / (1.0 - SECOND_DECAY**STEP)
    direction = first_fixed / (jnp.sqrt(second_fixed) + EPSILON)
    master_new = master - LEARN_RATE * (direction + decay_rate * master)
    return (master_new, first_new, second_new)


def swap(value):
    return lax.ppermute(value, "tensor", [(0, 1), (1, 0)])


def across(value, bit, count):
    return lax.ppermute(value, "dp", [(i, i ^ (1 << bit)) for i in range(count)])


def bit_orders(count):
    bits = list(range(count.bit_length() - 1))
    return (bits, bits[1::-1] + bits[2:])


def scatter_rows(grad, order, rank, count):
    rows, width = grad.shape
    left = sorted(order, reverse=True)
    held = grad.reshape((2,) * len(left) + (rows // count, width))
    for bit in order:
        axis = left.index(bit)
        mine = (rank >> bit) & 1
        kept = lax.dynamic_index_in_dim(held, mine, axis, keepdims=False)
        sent = lax.dynamic_index_in_dim(held, 1 - mine, axis, keepdims=False)
        came = across(sent, bit, count)
        held = (kept.astype(WIDE) + came.astype(WIDE)).astype(LOW)
        left.remove(bit)
    return held


def gather_rows(shard, order, rank, count):
    rows, width = shard.shape
    have = []
    held = shard
    for bit in reversed(order):
        came = across(held, bit, count)
        have = sorted(have + [bit], reverse=True)
        axis = have.index(bit)
        low_side = ((rank >> bit) & 1) == 0
        held = jnp.stack(
            [jnp.where(low_side, held, came), jnp.where(low_side, came, held)], axis=axis
        )
    return held.reshape(count * rows, width)


def local(
    n_dp,
    hidden_in,
    grad_out,
    lengths,
    key_mask,
    triple_weight,
    outward_weight,
    expand_weight,
    contract_weight,
    triple_master,
    triple_first,
    triple_second,
    outward_master,
    outward_first,
    outward_second,
    expand_master,
    expand_first,
    expand_second,
    contract_master,
    contract_first,
    contract_second,
    pair_bias,
    pair_first,
    pair_second,
    expand_bias,
    expand_bias_first,
    expand_bias_second,
    norm_vectors,
    vectors_first,
    vectors_second,
):
    core = lax.axis_index("tensor")
    rank = lax.axis_index("dp")
    orders = bit_orders(n_dp)

    def own_half(value):
        size = value.shape[0] // 2
        return lax.dynamic_slice_in_dim(value, core * size, size, 0)

    def whole_tokens(value):
        other = swap(value)
        return jnp.where(
            core == 0, jnp.concatenate([value, other]), jnp.concatenate([other, value])
        )

    triple_all = jnp.concatenate([triple_weight, swap(triple_weight)], axis=2)
    outward_all = jnp.concatenate([outward_weight, swap(outward_weight)], axis=0)
    expand_all = jnp.concatenate([expand_weight, swap(expand_weight)], axis=1)
    contract_all = jnp.concatenate([contract_weight, swap(contract_weight)], axis=0)
    bias_bundle = jnp.concatenate([pair_bias[0], pair_bias[1], expand_bias])
    other_bundle = swap(bias_bundle)
    n_pair = pair_bias.shape[1]
    n_bias = expand_bias.shape[0]
    query_bias = jnp.concatenate([pair_bias[0], other_bundle[:n_pair]])
    value_bias = jnp.concatenate([pair_bias[1], other_bundle[n_pair : 2 * n_pair]])
    expand_bias_all = jnp.concatenate([expand_bias, other_bundle[2 * n_pair :]])

    hidden = own_half(hidden_in)
    upstream = own_half(grad_out).astype(WIDE)
    lengths = own_half(lengths)
    key_mask = own_half(key_mask)
    seqs_here = lengths.shape[0]
    seq_len = key_mask.shape[1]
    tokens_here = hidden.shape[0]
    width = triple_all.shape[2]
    heads = width // HEAD_DIM
    score_scale = HEAD_DIM ** (-0.5)
    split_shape = (seqs_here, seq_len, heads, HEAD_DIM)
    positions = lax.broadcasted_iota(jnp.int32, (seqs_here, seq_len), 1)
    valid_keys = (positions < lengths[:, None]) & ((key_mask == 1) | (positions == 0))
    key_valid = valid_keys[:, None, None, :]
    projected = jnp.einsum("td,jdc->jtc", hidden, triple_all, preferred_element_type=WIDE)
    offsets = jnp.stack([query_bias, jnp.zeros_like(query_bias), value_bias])
    projected_low = (projected + offsets[:, None, :]).astype(LOW)
    queries = projected_low[0].reshape(split_shape)
    key_rows = projected_low[1].reshape(split_shape)
    values = projected_low[2].reshape(split_shape)
    scores = (
        jnp.einsum("sqhd,skhd->shqk", queries, key_rows, preferred_element_type=WIDE) * score_scale
    )
    masked = jnp.where(key_valid, scores, MASK_FILL)
    row_top = jnp.max(masked, axis=-1, keepdims=True)
    exp_terms = jnp.where(key_valid, jnp.exp(masked - row_top), 0.0)
    totals = jnp.sum(exp_terms, axis=-1, keepdims=True)
    log_total = row_top + jnp.log(totals)
    weights_low = (exp_terms / totals).astype(LOW)
    context = jnp.einsum("shqk,skhd->sqhd", weights_low, values, preferred_element_type=WIDE)
    context = context.astype(LOW).reshape(tokens_here, width)
    attn_total = jnp.dot(context, outward_all, preferred_element_type=WIDE)
    residual_one = hidden.astype(WIDE) + norm_vectors[0]
    normed_one, inverse_one = norm_rows(residual_one + attn_total)
    hidden_one = normed_one * norm_vectors[2] + norm_vectors[3]
    hidden_low = hidden_one.astype(LOW)
    widened = jnp.dot(hidden_low, expand_all, preferred_element_type=WIDE) + expand_bias_all
    active_low = jax.nn.gelu(widened, approximate=False).astype(LOW)
    ffn_total = jnp.dot(active_low, contract_all, preferred_element_type=WIDE)
    residual_two = hidden_one + norm_vectors[1]
    normed_two, inverse_two = norm_rows(residual_two + ffn_total)
    layer_own = (normed_two * norm_vectors[4] + norm_vectors[5]).astype(LOW)
    layer_out = whole_tokens(layer_own)

    def to_owner(grad):
        half = grad.shape[1] // 2
        return (grad[:, :half] + swap(grad[:, half:].astype(LOW)).astype(WIDE)).astype(LOW)

    def to_shard(grad):
        half = grad.shape[1] // 2
        parts = [
            scatter_rows(grad[:, i * half : (i + 1) * half], orders[i], rank, n_dp)
            for i in range(2)
        ]
        return jnp.concatenate(parts, axis=1).astype(WIDE)

    def to_all(shard):
        half = shard.shape[1] // 2
        parts = [
            gather_rows(shard[:, i * half : (i + 1) * half], orders[i], rank, n_dp)
            for i in range(2)
        ]
        return jnp.concatenate(parts, axis=1)

    gain_two_grad = jnp.sum(upstream * normed_two, axis=0)
    shift_two_grad = jnp.sum(upstream, axis=0)
    pre_two_grad = norm_back(upstream, normed_two, inverse_two, norm_vectors[4])
    bias_two_grad = jnp.sum(pre_two_grad, axis=0)
    branch_grad = pre_two_grad.astype(LOW)
    contract_grad = jnp.einsum("td,tf->df", branch_grad, active_low, preferred_element_type=WIDE)
    contract_share = to_shard(to_owner(contract_grad))
    active_grad = jnp.einsum("td,fd->tf", branch_grad, contract_all, preferred_element_type=WIDE)
    _, gelu_back = jax.vjp(partial(jax.nn.gelu, approximate=False), widened)
    widened_grad = gelu_back(active_grad)[0].astype(LOW)
    expand_bias_grad = jnp.sum(widened_grad, axis=0, dtype=WIDE)
    expand_grad = jnp.einsum("td,tf->df", hidden_low, widened_grad, preferred_element_type=WIDE)
    expand_share = to_shard(to_owner(expand_grad))
    hidden_part = jnp.einsum("tf,df->td", widened_grad, expand_all, preferred_element_type=WIDE)
    hidden_grad = pre_two_grad + hidden_part
    gain_one_grad = jnp.sum(hidden_grad * normed_one, axis=0)
    shift_one_grad = jnp.sum(hidden_grad, axis=0)
    pre_one_grad = norm_back(hidden_grad, normed_one, inverse_one, norm_vectors[2])
    bias_one_grad = jnp.sum(pre_one_grad, axis=0)
    attention_grad = pre_one_grad.astype(LOW)
    outward_grad = jnp.einsum("td,tc->dc", attention_grad, context, preferred_element_type=WIDE)
    context_grad = jnp.einsum(
        "td,cd->tc", attention_grad, outward_all, preferred_element_type=WIDE
    )
    context_grad = context_grad.astype(LOW).reshape(split_shape)
    recomputed = (
        jnp.einsum("sqhd,skhd->shqk", queries, key_rows, preferred_element_type=WIDE) * score_scale
    )
    attention = jnp.where(key_valid, jnp.exp(recomputed - log_total), 0.0)
    attention_low = attention.astype(LOW)
    probs_grad = jnp.einsum("sqhd,skhd->shqk", context_grad, values, preferred_element_type=WIDE)
    values_grad = jnp.einsum(
        "shqk,sqhd->skhd", attention_low, context_grad, preferred_element_type=WIDE
    )
    row_dot = jnp.sum(probs_grad * attention, axis=-1, keepdims=True)
    score_grad = (attention * (probs_grad - row_dot)).astype(LOW)
    queries_grad = (
        jnp.einsum("shqk,skhd->sqhd", score_grad, key_rows, preferred_element_type=WIDE)
        * score_scale
    )
    keys_grad = (
        jnp.einsum("shqk,sqhd->skhd", score_grad, queries, preferred_element_type=WIDE)
        * score_scale
    )
    projected_grad = [
        g.astype(LOW).reshape(tokens_here, width) for g in (queries_grad, keys_grad, values_grad)
    ]
    pair_grad = jnp.stack(
        [
            jnp.sum(projected_grad[0], axis=0, dtype=WIDE),
            jnp.sum(projected_grad[2], axis=0, dtype=WIDE),
        ]
    )
    triple_grad = [
        jnp.einsum("td,tc->dc", hidden, g, preferred_element_type=WIDE) for g in projected_grad
    ]
    own = n_pair
    attn_grad = jnp.concatenate(
        [g[:, :own] for g in triple_grad]
        + [outward_grad[:, :own]]
        + [g[:, own:] for g in triple_grad]
        + [outward_grad[:, own:]],
        axis=1,
    )
    attn_share = to_shard(to_owner(attn_grad))
    input_part = sum(
        jnp.einsum("tc,dc->td", projected_grad[j], triple_all[j], preferred_element_type=WIDE)
        for j in range(3)
    )
    input_grad = whole_tokens((pre_one_grad + input_part).astype(LOW)).astype(WIDE)

    vector_grad = jnp.stack(
        [bias_one_grad, bias_two_grad, gain_one_grad, shift_one_grad, gain_two_grad, shift_two_grad]
    )
    own_side = jnp.concatenate([pair_grad[:, :own].reshape(-1), expand_bias_grad[:n_bias]])
    other_side = jnp.concatenate([pair_grad[:, own:].reshape(-1), expand_bias_grad[n_bias:]])
    vector_flat = vector_grad.reshape(-1)
    vector_sum = jnp.concatenate([vector_flat, own_side]) + swap(
        jnp.concatenate([vector_flat, other_side])
    )
    for bit in orders[0]:
        vector_sum = vector_sum + across(vector_sum, bit, n_dp)
    n_vec = vector_flat.shape[0]
    vector_total = vector_sum[:n_vec].reshape(norm_vectors.shape)
    pair_total = vector_sum[n_vec : n_vec + 2 * own].reshape(2, own)
    widen_total = vector_sum[n_vec + 2 * own :]

    contract_new = adamw_step(
        contract_master.T, contract_first.T, contract_second.T, contract_share, WEIGHT_DECAY
    )
    contract_copy = to_all(contract_new[0].astype(LOW)).T
    expand_new = adamw_step(expand_master, expand_first, expand_second, expand_share, WEIGHT_DECAY)
    expand_copy = to_all(expand_new[0].astype(LOW))
    triple_share = jnp.stack([attn_share[:, j * own : (j + 1) * own] for j in range(3)])
    triple_new = adamw_step(triple_master, triple_first, triple_second, triple_share, WEIGHT_DECAY)
    outward_new = adamw_step(
        outward_master.T, outward_first.T, outward_second.T, attn_share[:, 3 * own :], WEIGHT_DECAY
    )
    attn_copy = to_all(
        jnp.concatenate([triple_new[0][j] for j in range(3)] + [outward_new[0]], axis=1).astype(LOW)
    )
    triple_copy = jnp.stack([attn_copy[:, j * own : (j + 1) * own] for j in range(3)])
    outward_copy = attn_copy[:, 3 * own :].T
    pair_new = adamw_step(pair_bias, pair_first, pair_second, pair_total, 0.0)
    widen_new = adamw_step(expand_bias, expand_bias_first, expand_bias_second, widen_total, 0.0)
    vectors_new = adamw_step(norm_vectors, vectors_first, vectors_second, vector_total, 0.0)
    return (
        layer_out,
        input_grad,
        triple_new[0],
        triple_new[1],
        triple_new[2],
        triple_copy,
        outward_new[0].T,
        outward_new[1].T,
        outward_new[2].T,
        outward_copy,
        expand_new[0],
        expand_new[1],
        expand_new[2],
        expand_copy,
        contract_new[0].T,
        contract_new[1].T,
        contract_new[2].T,
        contract_copy,
        pair_new[0],
        pair_new[1],
        pair_new[2],
        widen_new[0],
        widen_new[1],
        widen_new[2],
        vectors_new[0],
        vectors_new[1],
        vectors_new[2],
    )


def solution(mesh):
    matrix_specs = (
        P(None, "dp", "tensor"),
        P("tensor", "dp"),
        P("dp", "tensor"),
        P("tensor", "dp"),
    )
    copy_specs = (P(None, None, "tensor"), P("tensor", None), P(None, "tensor"), P("tensor", None))
    vector_specs = (P(None, "tensor"),) * 3 + (P("tensor"),) * 3 + (P(),) * 3
    in_specs = (
        (P("dp", None), P("dp", None), P("dp"), P("dp", None))
        + copy_specs
        + tuple(spec for spec in matrix_specs for _ in range(3))
        + vector_specs
    )
    out_specs = (P("dp", None), P("dp", None))
    for spec, copied in zip(matrix_specs, copy_specs):
        out_specs += (spec,) * 3 + (copied,)
    out_specs += vector_specs
    return jax.shard_map(
        partial(local, mesh.shape["dp"]),
        mesh=mesh,
        in_specs=in_specs,
        out_specs=out_specs,
        check_vma=False,
    )
```

```python
from functools import partial

import jax
import jax.numpy as jnp
from jax import lax
from jax.experimental import pallas as pl
from jax.experimental.pallas import tpu as pltpu
from jax.sharding import PartitionSpec as P

HEAD_DIM = 64
STEP = 7


MASK_FILL = -1e30
NORM_EPSILON = 1e-05
FIRST_DECAY = 0.5
SECOND_DECAY = 0.5
LEARN_RATE = 0.1
WEIGHT_DECAY = 0.01
EPSILON = 1e-08
LOW = jnp.bfloat16
WIDE = jnp.float32


def adamw_step(master, first_moment, second_moment, gradient, decay_rate):
    first_new = FIRST_DECAY * first_moment + (1.0 - FIRST_DECAY) * gradient
    second_new = SECOND_DECAY * second_moment + (1.0 - SECOND_DECAY) * gradient * gradient
    first_fixed = first_new / (1.0 - FIRST_DECAY**STEP)
    second_fixed = second_new / (1.0 - SECOND_DECAY**STEP)
    direction = first_fixed / (jnp.sqrt(second_fixed) + EPSILON)
    master_new = master - LEARN_RATE * (direction + decay_rate * master)
    return (master_new, first_new, second_new)


BLOCK_FF = 512
VMEM = pltpu.CompilerParams(vmem_limit_bytes=58 * 2**20)
ROOT_HALF = 0.7071067811865476
BELL_TOP = 0.3989422804014327


def dot(left, right):
    return jnp.dot(left, right, preferred_element_type=WIDE)


def dot_nt(left, right):
    return lax.dot_general(left, right, (((1,), (1,)), ((), ())), preferred_element_type=WIDE)


def dot_tn(left, right):
    return lax.dot_general(left, right, (((0,), (0,)), ((), ())), preferred_element_type=WIDE)


def gelu_pair(x):
    cdf = 0.5 * lax.erf(x * ROOT_HALF) + 0.5
    return x * cdf, cdf + x * (jnp.exp(x * x * -0.5) * BELL_TOP)


def mean_rows(value):
    return jnp.mean(value, axis=-1, keepdims=True)


def norm_parts(pre):
    centred = pre - mean_rows(pre)
    inverse = lax.rsqrt(mean_rows(centred * centred) + NORM_EPSILON)
    return centred * inverse, inverse


def norm_grad(upstream, normed, inverse, gain):
    scaled = upstream * gain
    return inverse * (scaled - mean_rows(scaled) - normed * mean_rows(scaled * normed))


def col_sum(value):
    return jnp.sum(value, axis=0, keepdims=True)


def fold_rows(value):
    return jnp.sum(value.reshape(-1, 8, value.shape[1]), axis=0)


def by_rows(count, body, start, unroll=1):
    at = lambda r: pl.ds(pl.multiple_of(r * TILE, TILE), TILE)
    return lax.fori_loop(0, count // TILE, lambda r, c: body(at(r), c), start, unroll=unroll)


def lane_half(shape, e):
    lane = lax.broadcasted_iota(jnp.int32, shape, 1)
    return (lane < HEAD_DIM) if e == 0 else (lane >= HEAD_DIM)


TILE = 256


def attend_kernel(
    place, lengths, x_ref, mask_ref, w0_ref, w1_ref, o0_ref, o1_ref, p0_ref, p1_ref, nv_ref,
    qkv_ref, probs_ref, ctx_ref, pre_ref, score_s,
):
    x = x_ref[...]
    row = place[0] * pl.num_programs(0) + pl.program_id(0)
    slot = lax.broadcasted_iota(jnp.int32, (1, x.shape[0]), 1)
    present = (mask_ref[pl.ds(row, 1)] == 1) | (slot == 0)
    valid = jnp.where((slot < lengths[row]) & present, 1.0, 0.0)
    valid = jnp.broadcast_to(valid, (16, x.shape[0])).astype(LOW)
    bias = (1.0 - dot_tn(valid, jnp.full((16, 128), 0.0625, LOW))) * MASK_FILL
    width = w0_ref.shape[2]
    pairs = width // 128
    scale = jnp.asarray(HEAD_DIM ** (-0.5), LOW)
    for half, (w_ref, p_ref) in enumerate(((w0_ref, p0_ref), (w1_ref, p1_ref))):
        base = 3 * width * half
        q = dot(x, w_ref[0]) + p_ref[0:1]
        qkv_ref[:, base : base + width] = q.astype(LOW)
        qkv_ref[:, base + width : base + 2 * width] = dot(x, w_ref[1]).astype(LOW)
        v = dot(x, w_ref[2]) + p_ref[1:2]
        qkv_ref[:, base + 2 * width : base + 3 * width] = v.astype(LOW)
    for half in range(2):
        base = 3 * width * half
        for pair in range(pairs):
            at = base + 128 * pair
            kp = qkv_ref[:, at + width : at + width + 128] * scale
            for e in range(2):
                ke = jnp.where(lane_half(kp.shape, e), kp, jnp.zeros_like(kp))
                score_s[2 * pair + e] = dot_nt(ke, qkv_ref[:, at : at + 128])
        for head in range(2 * pairs):
            for left in range(0, x.shape[0], 128):
                masked = score_s[head, :, left : left + 128] + bias
                top = jnp.max(masked, axis=0, keepdims=True)
                ex = jnp.exp(masked - top)
                total = jnp.sum(ex, axis=0, keepdims=True)
                low = (ex * (1.0 / total)).astype(LOW)
                probs_ref[0, half * 2 * pairs + head, :, left : left + 128] = low
        vt = qkv_ref[:, base + 2 * width : base + 3 * width].T
        for pair in range(pairs):
            outs = []
            for e in range(2):
                low = 128 * pair + HEAD_DIM * e
                outs.append(
                    dot(vt[low : low + HEAD_DIM], probs_ref[0, half * 2 * pairs + 2 * pair + e])
                )
            ctx = jnp.concatenate(outs, axis=0).T.astype(LOW)
            ctx_ref[:, half * width + 128 * pair : half * width + 128 * pair + 128] = ctx
    attn = dot(ctx_ref[:, :width], o0_ref[...]) + dot(ctx_ref[:, width:], o1_ref[...])
    pre_ref[...] = x.astype(WIDE) + nv_ref[0:1] + attn


def attend(place, lengths, hidden_in, key_mask, w0, w1, o0, o1, p0, p1, nv):
    seqs, seq_len = key_mask.shape[0] // 2, key_mask.shape[1]
    d = hidden_in.shape[1]
    width = w0.shape[2]
    heads = 2 * width // HEAD_DIM
    tokens = seqs * seq_len
    full = lambda a: pl.BlockSpec(a.shape, lambda s, c, n: (0,) * a.ndim)
    rows = lambda cols: pl.BlockSpec((seq_len, cols), lambda s, c, n: (s, 0))
    return pl.pallas_call(
        attend_kernel,
        out_shape=(
            jax.ShapeDtypeStruct((tokens, 6 * width), LOW),
            jax.ShapeDtypeStruct((seqs, heads, seq_len, seq_len), LOW),
            jax.ShapeDtypeStruct((tokens, 2 * width), LOW),
            jax.ShapeDtypeStruct((tokens, d), WIDE),
        ),
        grid_spec=pltpu.PrefetchScalarGridSpec(
            num_scalar_prefetch=2,
            grid=(seqs,),
            in_specs=[
                pl.BlockSpec((seq_len, d), lambda s, c, n: (c[0] * seqs + s, 0)),
                *(full(a) for a in (key_mask, w0, w1, o0, o1, p0, p1, nv)),
            ],
            out_specs=[
                rows(6 * width),
                pl.BlockSpec((1, heads, seq_len, seq_len), lambda s, c, n: (s, 0, 0, 0)),
                rows(2 * width),
                rows(d),
            ],
            scratch_shapes=[pltpu.VMEM((heads // 2, seq_len, seq_len), WIDE)],
        ),
        compiler_params=VMEM,
        name="attend",
        cost_estimate=pl.CostEstimate(flops=8 * 10**9, bytes_accessed=25 * 10**6, transcendentals=3 * 10**6),
    )(place, lengths, hidden_in, key_mask, w0, w1, o0, o1, p0, p1, nv)


ROWS = 512


def ffn_fwd_kernel(
    core, pre_ref, up_ref, e0_ref, e1_ref, c0_ref, c1_ref, b0_ref, b1_ref, nv_ref,
    act_ref, slope_ref, out_ref, grad_ref, low_ref, hl_ref, sums_ref, whole_ref,
    acc_s, wide_s,
):
    j = pl.program_id(0)
    last = pl.num_programs(0) - 1
    tokens = pre_ref.shape[0]

    @pl.when(j == 0)
    def _():
        def one(rows, _):
            normed, _ = norm_parts(pre_ref[rows])
            hidden_one = normed * nv_ref[2:3] + nv_ref[3:4]
            hl_ref[rows] = hidden_one.astype(LOW)
            acc_s[rows] = hidden_one + nv_ref[1:2]
            return 0

        by_rows(tokens, one, 0)

    def step(e_ref, c_ref, b_ref):
        for top in range(0, tokens, ROWS):
            wide_s[top : top + ROWS] = dot(hl_ref[top : top + ROWS], e_ref[...])
        for top in range(0, tokens, ROWS):
            for at in range(top, top + ROWS, 16):
                rows = slice(at, at + 16)
                act, slope = gelu_pair(wide_s[rows] + b_ref[...])
                act_ref[rows] = act.astype(LOW)
                slope_ref[rows] = slope.astype(LOW)
            acc_s[top : top + ROWS] += dot(act_ref[top : top + ROWS], c_ref[...])

    @pl.when(j < (last + 1) // 2)
    def _():
        step(e0_ref, c0_ref, b0_ref)

    @pl.when(j >= (last + 1) // 2)
    def _():
        step(e1_ref, c1_ref, b1_ref)

    @pl.when(j == last)
    def _():
        def one(rows, sums):
            normed, inverse = norm_parts(acc_s[rows])
            out = (normed * nv_ref[4:5] + nv_ref[5:6]).astype(LOW)
            out_ref[rows] = out
            whole_ref[rows] = out
            up = up_ref[rows].astype(WIDE)
            grad = norm_grad(up, normed, inverse, nv_ref[4:5])
            grad_ref[rows] = grad
            low_ref[rows] = grad.astype(LOW)
            new = (fold_rows(grad), fold_rows(up * normed), fold_rows(up))
            return tuple(a + b for a, b in zip(sums, new))

        zero = jnp.zeros((8, pre_ref.shape[1]), WIDE)
        sums = by_rows(tokens, one, (zero,) * 3, unroll=1)
        for i in range(3):
            sums_ref[i : i + 1] = col_sum(sums[i])
        sums_ref[3:8] = jnp.zeros((5, sums_ref.shape[1]), WIDE)


def ffn_fwd(core, pre, grad_out, e0, e1, c0, c1, b0, b1, nv):
    tokens, d = pre.shape
    width = e0.shape[1]
    steps = width // BLOCK_FF
    full = lambda shape: pl.BlockSpec(shape, lambda j, c: (0,) * len(shape))
    lower = lambda j: jnp.minimum(j, steps - 1)
    upper = lambda j: jnp.maximum(j - steps, 0)
    return pl.pallas_call(
        ffn_fwd_kernel,
        out_shape=(
            jax.ShapeDtypeStruct((tokens, 2 * width), LOW),
            jax.ShapeDtypeStruct((tokens, 2 * width), LOW),
            jax.ShapeDtypeStruct((tokens, d), LOW),
            jax.ShapeDtypeStruct((tokens, d), WIDE),
            jax.ShapeDtypeStruct((tokens, d), LOW),
            jax.ShapeDtypeStruct((tokens, d), LOW),
            jax.ShapeDtypeStruct((8, d), WIDE),
            jax.ShapeDtypeStruct((2 * tokens, d), LOW),
        ),
        grid_spec=pltpu.PrefetchScalarGridSpec(
            num_scalar_prefetch=1,
            grid=(2 * steps,),
            in_specs=[
                full((tokens, d)),
                pl.BlockSpec((tokens, d), lambda j, c: (c[0], 0)),
                pl.BlockSpec((d, BLOCK_FF), lambda j, c: (0, lower(j))),
                pl.BlockSpec((d, BLOCK_FF), lambda j, c: (0, upper(j))),
                pl.BlockSpec((BLOCK_FF, d), lambda j, c: (lower(j), 0)),
                pl.BlockSpec((BLOCK_FF, d), lambda j, c: (upper(j), 0)),
                pl.BlockSpec((1, BLOCK_FF), lambda j, c: (0, lower(j))),
                pl.BlockSpec((1, BLOCK_FF), lambda j, c: (0, upper(j))),
                full(nv.shape),
            ],
            out_specs=[
                pl.BlockSpec((tokens, BLOCK_FF), lambda j, c: (0, j)),
                pl.BlockSpec((tokens, BLOCK_FF), lambda j, c: (0, j)),
                full((tokens, d)),
                full((tokens, d)),
                full((tokens, d)),
                full((tokens, d)),
                full((8, d)),
                pl.BlockSpec((tokens, d), lambda j, c: (c[0], 0)),
            ],
            scratch_shapes=[pltpu.VMEM((tokens, d), WIDE), pltpu.VMEM((tokens, BLOCK_FF), WIDE)],
        ),
        compiler_params=VMEM,
        name="ffn_fwd",
        cost_estimate=pl.CostEstimate(flops=11 * 10**9, bytes_accessed=40 * 10**6, transcendentals=4 * 10**6),
    )(core, pre, grad_out, e0, e1, c0, c1, b0, b1, nv)


def place_rows(out_ref, value, rank, count, left=0):
    rows = value.shape[0] // count
    cols = slice(left, left + value.shape[1])
    if rows % 16:
        out_ref[:, cols] = value
        return
    for i in range(count):
        apart = jnp.bitwise_xor(rank, i)
        at = (apart & 3) * (count // 4) + (apart >> 2)
        there = pl.ds(pl.multiple_of(at * rows, 16), rows)
        out_ref[there, cols] = value[i * rows : (i + 1) * rows]


def placed(grad, rank, count):
    rows = grad.shape[0] // count
    if rows % 16 == 0:
        return grad
    at = jnp.arange(count)
    apart = (at // (count // 4)) | ((at % (count // 4)) << 2)
    return grad.reshape(count, rows, -1)[apart ^ rank].reshape(grad.shape)


ANY = pl.BlockSpec(memory_space=pl.ANY)


def with_deps(body, lead, inputs, deps):
    def kernel(*refs):
        body(*refs[: lead + inputs], *refs[lead + inputs + len(deps) :])

    return kernel


def weight_kernel(count, place, left_ref, right_ref, out_ref):
    place_rows(out_ref, dot_tn(left_ref[...], right_ref[...]).astype(LOW), place[1], count)


def weight_grad(place, n_dp, left, right, first, count, block, deps=()):
    tokens = right.shape[0]
    d = left.shape[1]
    halves = left.shape[0] // tokens
    out = pl.pallas_call(
        with_deps(partial(weight_kernel, n_dp), 1, 2, deps),
        out_shape=jax.ShapeDtypeStruct((d, count * block), LOW),
        grid_spec=pltpu.PrefetchScalarGridSpec(
            num_scalar_prefetch=1,
            grid=(count,),
            in_specs=[
                pl.BlockSpec((tokens, d), lambda j, c: (c[0] if halves == 2 else 0, 0)),
                pl.BlockSpec((tokens, block), lambda j, c: (0, first + j)),
            ]
            + [ANY] * len(deps),
            out_specs=pl.BlockSpec((d, block), lambda j, c: (0, j)),
        ),
        compiler_params=VMEM,
        name="weight_grad",
        cost_estimate=pl.CostEstimate(
            flops=2 * d * tokens * count * block, bytes_accessed=6 * 10**6, transcendentals=0
        ),
    )(place, left, right, *deps)
    return placed(out, place[1], n_dp)


def ffn_bwd_kernel(
    final, n_dp, place, low_ref, slope_ref, e_ref, c_ref, sofar_ref, pre_ref, hl_ref, ctx_ref, nv_ref,
    we_ref, bias_ref, one_ref, *rest,
):
    if final:
        ag_ref, sums_ref, wo_ref, acc_s, wg_s, wide_s = rest
    else:
        acc_s, wg_s, wide_s = rest
    j = pl.program_id(0)
    last = pl.num_programs(0) - 1
    tokens = low_ref.shape[0]

    @pl.when(j == 0)
    def _():
        acc_s[...] = sofar_ref[...]

    for top in range(0, tokens, ROWS):
        wide_s[top : top + ROWS] = dot_nt(low_ref[top : top + ROWS], c_ref[...])
    bias = jnp.zeros((8, BLOCK_FF), WIDE)
    for top in range(0, tokens, ROWS):
        for at in range(top, top + ROWS, 16):
            rows = slice(at, at + 16)
            wg = (wide_s[rows] * slope_ref[rows].astype(WIDE)).astype(LOW)
            wg_s[rows] = wg
            bias = bias + fold_rows(wg.astype(WIDE))
        acc_s[top : top + ROWS] += dot_nt(wg_s[top : top + ROWS], e_ref[...])
    bias_ref[...] = col_sum(bias)
    grad = dot_tn(hl_ref[...], wg_s[...]).astype(LOW)
    if final:
        for i in range(we_ref.shape[1] // BLOCK_FF):

            @pl.when(j == i)
            def _():
                place_rows(we_ref, grad, place[1], n_dp, i * BLOCK_FF)
    else:
        place_rows(we_ref, grad, place[1], n_dp)

    @pl.when(j == last)
    def _():
        if not final:
            one_ref[...] = acc_s[...]
            return

        def one(rows, sums):
            normed, inverse = norm_parts(pre_ref[rows])
            up = acc_s[rows]
            grad = norm_grad(up, normed, inverse, nv_ref[2:3])
            one_ref[rows] = grad
            ag_ref[rows] = grad.astype(LOW)
            new = (fold_rows(grad), fold_rows(up * normed), fold_rows(up))
            return tuple(a + b for a, b in zip(sums, new))

        zero = jnp.zeros((8, pre_ref.shape[1]), WIDE)
        sums = by_rows(tokens, one, (zero,) * 3, unroll=1)
        for i in range(3):
            sums_ref[i : i + 1] = col_sum(sums[i])
        sums_ref[3:8] = jnp.zeros((5, sums_ref.shape[1]), WIDE)
        half = wo_ref.shape[1]
        grad = dot_tn(ag_ref[...], ctx_ref[:, :half]).astype(LOW)
        place_rows(we_ref, grad, place[1], n_dp, we_ref.shape[1] - half)
        place_rows(wo_ref, dot_tn(ag_ref[...], ctx_ref[:, half:]).astype(LOW), place[1], n_dp)


def ffn_bwd(place, n_dp, final, low, slope, e, c, sofar, pre, hl, ctx, nv, deps=()):
    tokens, d = low.shape
    width = e.shape[1]
    steps = width // BLOCK_FF
    first = 0 if final else steps
    full = lambda shape: pl.BlockSpec(shape, lambda j, c: (0,) * len(shape))
    half = ctx.shape[1] // 2
    if final:
        both = (d, width + half)
        outs = [(jax.ShapeDtypeStruct(both, LOW), full(both))]
    else:
        outs = [
            (jax.ShapeDtypeStruct((d, width), LOW), pl.BlockSpec((d, BLOCK_FF), lambda j, c: (0, j)))
        ]
    outs += [
        (jax.ShapeDtypeStruct((1, width), WIDE), pl.BlockSpec((1, BLOCK_FF), lambda j, c: (0, j))),
        (jax.ShapeDtypeStruct((tokens, d), WIDE), full((tokens, d))),
    ]
    if final:
        outs += [
            (jax.ShapeDtypeStruct((tokens, d), LOW), full((tokens, d))),
            (jax.ShapeDtypeStruct((8, d), WIDE), full((8, d))),
            (jax.ShapeDtypeStruct((d, half), LOW), full((d, half))),
        ]
    out = pl.pallas_call(
        with_deps(partial(ffn_bwd_kernel, final, n_dp), 1, 9, deps),
        out_shape=tuple(o[0] for o in outs),
        grid_spec=pltpu.PrefetchScalarGridSpec(
            num_scalar_prefetch=1,
            grid=(steps,),
            in_specs=[
                full((tokens, d)),
                pl.BlockSpec((tokens, BLOCK_FF), lambda j, c: (0, first + j)),
                pl.BlockSpec((d, BLOCK_FF), lambda j, c: (0, j)),
                pl.BlockSpec((BLOCK_FF, d), lambda j, c: (j, 0)),
                full((tokens, d)),
                full((tokens, d)) if final else ANY,
                full((tokens, d)),
                full(ctx.shape) if final else ANY,
                full(nv.shape),
            ]
            + [ANY] * len(deps),
            out_specs=[o[1] for o in outs],
            scratch_shapes=[
                pltpu.VMEM((tokens, d), WIDE),
                pltpu.VMEM((tokens, BLOCK_FF), LOW),
                pltpu.VMEM((tokens, BLOCK_FF), WIDE),
            ],
        ),
        compiler_params=VMEM,
        name="ffn_bwd",
        cost_estimate=pl.CostEstimate(flops=8 * 10**9, bytes_accessed=20 * 10**6, transcendentals=0),
    )(place, low, slope, e, c, sofar, pre, hl, ctx, nv, *deps)
    out = list(out)
    for i in (0, 5) if final else (0,):
        out[i] = placed(out[i], place[1], n_dp)
    return out


def attend_back_kernel(
    ag_ref, probs_ref, qkv_ref, o0_ref, o1_ref, grad_ref, sums_ref, dp_s, ds_s, cg_s
):
    width = o0_ref.shape[0]
    pairs = width // 128
    scale = jnp.asarray(HEAD_DIM ** (-0.5), LOW)
    keep = [lane_half((ag_ref.shape[0], 128), e) for e in range(2)]
    side = lambda value, e: jnp.where(keep[e], value, jnp.zeros_like(value))
    for half, o_ref in enumerate((o0_ref, o1_ref)):
        cg_s[...] = dot_nt(ag_ref[...], o_ref[...]).astype(LOW)
        first = half * 2 * pairs
        for pair in range(pairs):
            at = 3 * width * half + 128 * pair
            do = cg_s[:, 128 * pair : 128 * pair + 128]
            vp = qkv_ref[:, at + 2 * width : at + 2 * width + 128]
            for e in range(2):
                dp_s[2 * pair + e] = dot_nt(side(vp, e), do)
            dv = dot(probs_ref[0, first + 2 * pair], side(do, 0))
            dv = (dv + dot(probs_ref[0, first + 2 * pair + 1], side(do, 1))).astype(LOW)
            grad_ref[:, at + 2 * width : at + 2 * width + 128] = dv
            to = half * width + 128 * pair
            sums_ref[0, 1:2, to : to + 128] = col_sum(dv.astype(WIDE))
        for head in range(2 * pairs):
            for left in range(0, ag_ref.shape[0], 128):
                cols = slice(left, left + 128)
                dp = dp_s[head, :, cols]
                probs = probs_ref[0, first + head, :, cols].astype(WIDE)
                inner = jnp.sum(dp * probs, axis=0, keepdims=True)
                ds_s[head, :, cols] = (probs * (dp - inner)).astype(LOW)
        for pair in range(pairs):
            at = 3 * width * half + 128 * pair
            qp = qkv_ref[:, at : at + 128] * scale
            kp = qkv_ref[:, at + width : at + width + 128] * scale
            dk = dot(ds_s[2 * pair], side(qp, 0)) + dot(ds_s[2 * pair + 1], side(qp, 1))
            dq = dot_tn(ds_s[2 * pair], side(kp, 0)) + dot_tn(ds_s[2 * pair + 1], side(kp, 1))
            dq = dq.astype(LOW)
            grad_ref[:, at : at + 128] = dq
            grad_ref[:, at + width : at + width + 128] = dk.astype(LOW)
            to = half * width + 128 * pair
            sums_ref[0, 0:1, to : to + 128] = col_sum(dq.astype(WIDE))


def attend_back(ag, probs, qkv, o0, o1, first, count, before=None, deps=()):
    seqs, heads, seq_len, _ = probs.shape
    tokens, d = ag.shape
    width = o0.shape[0]
    full = lambda a: pl.BlockSpec(a.shape, lambda s: (0,) * a.ndim)
    rows = lambda cols: pl.BlockSpec((seq_len, cols), lambda s: (first + s, 0))
    if before is not None:
        deps = tuple(before) + tuple(deps)
    return pl.pallas_call(
        with_deps(attend_back_kernel, 0, 5, deps),
        out_shape=(
            jax.ShapeDtypeStruct((tokens, 6 * width), LOW),
            jax.ShapeDtypeStruct((seqs, 8, 2 * width), WIDE),
        ),
        grid=(count,),
        in_specs=[
            rows(d),
            pl.BlockSpec((1, heads, seq_len, seq_len), lambda s: (first + s, 0, 0, 0)),
            rows(6 * width),
            full(o0),
            full(o1),
        ]
        + [ANY] * len(deps),
        out_specs=[
            rows(6 * width),
            pl.BlockSpec((1, 8, 2 * width), lambda s: (first + s, 0, 0)),
        ],
        input_output_aliases={} if before is None else {5: 0, 6: 1},
        scratch_shapes=[
            pltpu.VMEM((heads // 2, seq_len, seq_len), WIDE),
            pltpu.VMEM((heads // 2, seq_len, seq_len), LOW),
            pltpu.VMEM((seq_len, width), LOW),
        ],
        compiler_params=VMEM,
        name="attend_back",
        cost_estimate=pl.CostEstimate(
            flops=3 * count * 10**9, bytes_accessed=5 * count * 10**6, transcendentals=0
        ),
    )(ag, probs, qkv, o0, o1, *deps)


def input_kernel(place, grad_ref, w0_ref, w1_ref, one_ref, out_ref, whole_ref):
    width = w0_ref.shape[2]
    total = one_ref[...]
    for i in range(6):
        w = (w0_ref, w1_ref)[i // 3][i % 3]
        total = total + dot_nt(grad_ref[:, i * width : (i + 1) * width], w)
    out_ref[...] = total.astype(LOW)
    whole_ref[...] = total.astype(LOW).astype(WIDE)


def input_side(place, grad, w0, w1, one, deps=()):
    tokens, d = one.shape
    block = min(ROWS, tokens)
    full = lambda a: pl.BlockSpec(a.shape, lambda s, c: (0,) * a.ndim)
    rows = lambda cols: pl.BlockSpec((block, cols), lambda s, c: (s, 0))
    return pl.pallas_call(
        with_deps(input_kernel, 1, 4, deps),
        out_shape=(
            jax.ShapeDtypeStruct((tokens, d), LOW),
            jax.ShapeDtypeStruct((2 * tokens, d), WIDE),
        ),
        grid_spec=pltpu.PrefetchScalarGridSpec(
            num_scalar_prefetch=1,
            grid=(tokens // block,),
            in_specs=[rows(grad.shape[1]), full(w0), full(w1), rows(d)] + [ANY] * len(deps),
            out_specs=[
                rows(d),
                pl.BlockSpec((block, d), lambda s, c: (c[0] * (tokens // block) + s, 0)),
            ],
        ),
        compiler_params=VMEM,
        name="input_side",
        cost_estimate=pl.CostEstimate(flops=4 * 10**9, bytes_accessed=14 * 10**6, transcendentals=0),
    )(place, grad, w0, w1, one, *deps)


def put_kernel(place, other_ref, whole_ref, out_ref):
    out_ref[...] = other_ref[...].astype(out_ref.dtype)


def put_other(place, other, whole, deps=()):
    tokens, d = other.shape
    block = tokens // 4
    return pl.pallas_call(
        with_deps(put_kernel, 1, 2, deps),
        out_shape=jax.ShapeDtypeStruct(whole.shape, whole.dtype),
        grid_spec=pltpu.PrefetchScalarGridSpec(
            num_scalar_prefetch=1,
            grid=(4,),
            in_specs=[pl.BlockSpec((block, d), lambda s, c: (s, 0)), ANY] + [ANY] * len(deps),
            out_specs=pl.BlockSpec((block, d), lambda s, c: ((1 - c[0]) * 4 + s, 0)),
        ),
        input_output_aliases={2: 0},
        compiler_params=VMEM,
        name="put_other",
        cost_estimate=pl.CostEstimate(flops=0, bytes_accessed=4 * tokens * d, transcendentals=0),
    )(place, other, whole, *deps)


def gather_kernel(count, layout, wide, place, z_ref, x_ref, y_ref, da_ref, db_ref, *refs):
    outs, held = refs[: len(layout)], refs[len(layout)]
    block = z_ref.shape[0] // (count // 4)
    step = pl.program_id(0)

    def blocks():
        for apart in range(count):
            first = (apart >> 2) * block
            ref = (z_ref, x_ref, y_ref, da_ref)[apart & 3]
            if apart & 3 == 3 and first >= da_ref.shape[0]:
                ref, first = db_ref, first - da_ref.shape[0]
            yield jnp.bitwise_xor(place[1], apart), ref[first : first + block]

    for (kind, first, end), out in zip(layout, outs):

        @pl.when((step >= first) & (step < end))
        def _():
            for at, value in blocks():
                if kind == "deep":
                    rows = block // out.shape[0]
                    there = pl.ds(pl.multiple_of(at * rows, 16), rows)
                    for i in range(out.shape[0]):
                        out[i, there] = value[i * rows : i * rows + rows]
                else:
                    to = held if kind == "flip" else out
                    to[pl.ds(pl.multiple_of(at * block, 16), block)] = value
            if kind == "flip":
                out[...] = held[...].T


def gather_place(place, n_dp, layout, z, x, y, da, db, deps=()):
    rows, cols = z.shape[0] * 4, z.shape[1]
    block = rows // n_dp
    deep = layout[0][0] == "deep"
    wide = 128 if deep else 384
    shapes, specs, steps = [], [], []
    for kind, left, right in layout:
        full = right - left
        if deep:
            left, right = 0, cols
            shapes.append((full // cols, rows * cols // full, cols))
        else:
            shapes.append((full, rows) if kind == "flip" else (rows, full))
        first, end = left // wide, right // wide
        steps.append((kind, first, end))
        at = lambda j, first=first, end=end: jnp.clip(j - first, 0, end - first - 1)
        if deep:
            specs.append(pl.BlockSpec(shapes[-1][:2] + (wide,), lambda j, c, at=at: (0, 0, at(j))))
        elif kind == "flip":
            specs.append(pl.BlockSpec((wide, rows), lambda j, c, at=at: (at(j), 0)))
        else:
            specs.append(pl.BlockSpec((rows, wide), lambda j, c, at=at: (0, at(j))))
    if (block // (shapes[0][0] if deep else 1)) % 16:
        plane = jnp.stack([z, x, y, jnp.concatenate([da, db])])
        blocks = plane.reshape(4, n_dp // 4, block, cols).transpose(1, 0, 2, 3)
        blocks = blocks.reshape(n_dp, block, cols)[jnp.arange(n_dp) ^ place[1]]
        outs = []
        for (kind, left, right), shape in zip(layout, shapes):
            if deep:
                outs.append(
                    blocks.reshape(n_dp, shape[0], -1, cols).transpose(1, 0, 2, 3).reshape(shape)
                )
            else:
                whole = blocks.reshape(rows, cols)[:, left:right]
                outs.append(whole.T if kind == "flip" else whole)
        return outs
    spec = lambda a: pl.BlockSpec((a.shape[0], wide), lambda j, c: (0, j))
    return pl.pallas_call(
        with_deps(partial(gather_kernel, n_dp, steps, wide), 1, 5, deps),
        out_shape=[jax.ShapeDtypeStruct(shape, LOW) for shape in shapes],
        grid_spec=pltpu.PrefetchScalarGridSpec(
            num_scalar_prefetch=1,
            grid=(cols // wide,),
            in_specs=[spec(a) for a in (z, x, y, da, db)] + [ANY] * len(deps),
            out_specs=specs,
            scratch_shapes=[pltpu.VMEM((rows, wide), LOW)],
        ),
        compiler_params=VMEM,
        name="gather_place",
        cost_estimate=pl.CostEstimate(flops=0, bytes_accessed=4 * rows * cols, transcendentals=0),
    )(place, z, x, y, da, db, *deps)


def swap(value):
    return lax.ppermute(value, "tensor", [(0, 1), (1, 0)])


def across(value, apart, count):
    return lax.ppermute(value, "dp", [(i, i ^ apart) for i in range(count)])


def far_groups(count):
    groups, weight = [], 4
    while weight < count:
        members = min(4, count // weight)
        groups.append((weight, members))
        weight *= members
    return groups


def scatter_flow(mine, came, count):
    rows, width = mine.shape
    shape = lambda a: a.reshape(2, 2, 2, rows // 8, a.shape[1])
    mine, came = shape(mine), [shape(c) for c in came]

    def part(*at):
        other = [c[at].astype(WIDE) for c in came]
        return mine[at].astype(WIDE) + (jnp.concatenate(other, axis=-1) if other[1:] else other[0])

    every = slice(None)
    to_x, to_y = part(every, 1, 0).astype(LOW), part(1, every, 1).astype(LOW)
    from_x, from_y = yield [to_x, to_y], lambda v: [across(v[0], 1, count), across(v[1], 2, count)]
    to_y = (part(1, 0, 0) + from_x[1].astype(WIDE)).astype(LOW)
    to_x = (part(0, 1, 1) + from_y[1].astype(WIDE)).astype(LOW)
    last_x, last_y = yield [to_x, to_y], lambda v: [across(v[0], 1, count), across(v[1], 2, count)]
    upper = part(0, 0, 0) + from_x[0].astype(WIDE) + last_y.astype(WIDE)
    lower = part(0, 0, 1) + from_y[0].astype(WIDE) + last_x.astype(WIDE)
    held = jnp.concatenate([upper, lower], axis=0)
    for weight, members in reversed(far_groups(count)):
        pieces = held.reshape(members, -1, width)
        sends = [pieces[m].astype(LOW) for m in range(1, members)]
        came = yield (
            sends,
            lambda v, w=weight: [across(p, (m + 1) * w, count) for m, p in enumerate(v)],
        )
        held = pieces[0]
        for piece in came:
            held = held + piece.astype(WIDE)
    return held


def gather_flow(shard, count):
    held = shard
    for weight, members in far_groups(count):
        came = yield (
            [held],
            lambda v, w=weight, n=members: [across(v[0], m * w, count) for m in range(1, n)],
        )
        held = jnp.concatenate([held] + list(came), axis=0)
    half = held.shape[0] // 2
    x, y = yield [held], lambda v: [across(v[0], 1, count), across(v[0], 2, count)]
    upper, lower = x[:half], y[half:]
    both = yield [upper, lower], lambda v: [across(v[0], 2, count), across(v[1], 1, count)]
    return held, x, y, both[0], both[1]


def total_flow(mine, others, count):
    (came,) = yield [others], lambda v: [swap(v[0])]
    total = mine + came
    apart = 1
    while apart < count:
        (came,) = yield [total], lambda v, apart=apart: [across(v[0], apart, count)]
        total = total + came
        apart *= 2
    return total


def behind(value, after):
    return lax.optimization_barrier((value, after))[0]


class Flow:
    def __init__(self, steps, then=None):
        self.steps, self.then = steps, then
        self.came, self.result, self.done = None, None, False
        self.sends = ()

    def advance(self, after=None):
        if after is not None and self.came is not None:
            self.came = behind(list(self.came), after)
        while not self.done:
            try:
                sends, send = self.steps.send(self.came)
            except StopIteration as stop:
                if self.then is None:
                    self.result, self.done = stop.value, True
                    return []
                self.steps, self.then = self.then(stop.value)
                self.came = None
                continue
            self.came, self.sends = send(sends), list(sends)
            return self.sends
        return []

    def finish(self):
        while not self.done:
            self.advance()
        return self.result


def local(
    n_dp,
    hidden_in,
    grad_out,
    lengths,
    key_mask,
    triple_weight,
    outward_weight,
    expand_weight,
    contract_weight,
    triple_master,
    triple_first,
    triple_second,
    outward_master,
    outward_first,
    outward_second,
    expand_master,
    expand_first,
    expand_second,
    contract_master,
    contract_first,
    contract_second,
    pair_bias,
    pair_first,
    pair_second,
    expand_bias,
    expand_bias_first,
    expand_bias_second,
    norm_vectors,
    vectors_first,
    vectors_second,
):
    core = lax.axis_index("tensor")
    rank = lax.axis_index("dp")

    own = pair_bias.shape[1]
    n_bias = expand_bias.shape[0]
    place = jnp.stack([core, rank]).astype(jnp.int32)
    bias_row = expand_bias[None]
    triple_other = swap(triple_weight)
    pair_other = swap(pair_bias)
    outward_other = swap(outward_weight)
    expand_here, contract_here, bias_here = behind(
        [expand_weight, contract_weight, bias_row], [triple_other, pair_other, outward_other]
    )
    bias_other = swap(bias_here)
    expand_other = swap(expand_here)
    contract_other = swap(contract_here)
    updates = {}

    def contract_then(share):
        new = adamw_step(
            contract_master.T, contract_first.T, contract_second.T, share, WEIGHT_DECAY
        )
        updates["contract"] = new
        return gather_flow(new[0].astype(LOW), n_dp), None

    def expand_then(share):
        new = adamw_step(
            expand_master, expand_first, expand_second, share[:, :n_bias], WEIGHT_DECAY
        )
        out = adamw_step(
            outward_master.T, outward_first.T, outward_second.T, share[:, n_bias:], WEIGHT_DECAY
        )
        updates["expand"], updates["outward"] = new, out
        return gather_flow(jnp.concatenate([new[0], out[0]], axis=1).astype(LOW), n_dp), None

    def triple_then(share):
        share = jnp.stack([share[:, j * own : (j + 1) * own] for j in range(3)])
        new = adamw_step(triple_master, triple_first, triple_second, share, WEIGHT_DECAY)
        updates["triple"] = new
        return gather_flow(new[0].astype(LOW).reshape(-1, own), n_dp), None

    qkv, probs, context, pre_one = attend(
        place, lengths, hidden_in, key_mask, triple_weight, triple_other, outward_weight,
        outward_other, pair_bias, pair_other, norm_vectors,
    )
    active, slope, layer_own, pre_two_grad, branch_grad, hidden_low, sums_two, layer_out = ffn_fwd(
        place, pre_one, grad_out, expand_weight, expand_other, contract_weight, contract_other,
        bias_row, bias_other, norm_vectors,
    )
    layer_other = swap(layer_own)

    steps = n_bias // BLOCK_FF
    weight = partial(weight_grad, place, n_dp)
    contract_theirs = weight(branch_grad, active, steps, steps, BLOCK_FF)
    contract_mine = weight(branch_grad, active, 0, steps, BLOCK_FF, deps=(contract_theirs,))
    contract_flow = Flow(scatter_flow(contract_mine, [swap(contract_theirs)], n_dp), contract_then)
    sends = contract_flow.advance()
    expand_theirs, bias_theirs, hidden_sofar = ffn_bwd(
        place, n_dp, False, branch_grad, slope, expand_other, contract_other, pre_two_grad,
        pre_two_grad, hidden_low, context, norm_vectors, deps=sends,
    )
    expand_came = swap(expand_theirs)
    sends = contract_flow.advance(bias_theirs)
    expand_mine, bias_mine, pre_one_grad, attention_grad, sums_one, outward_theirs = ffn_bwd(
        place, n_dp, True, branch_grad, slope, expand_weight, contract_weight, hidden_sofar,
        pre_one, hidden_low, context, norm_vectors, deps=sends,
    )
    expand_flow = Flow(
        scatter_flow(expand_mine, [expand_came, swap(outward_theirs)], n_dp), expand_then
    )
    sends = contract_flow.advance(sums_one) + expand_flow.advance()
    projected_grad, sums_pair = attend_back(
        attention_grad, probs, qkv, outward_weight, outward_other, 0, lengths.shape[0] // 2,
        deps=sends,
    )
    sends = contract_flow.advance(sums_pair) + expand_flow.advance(sums_pair)
    triple_theirs = weight(hidden_in, projected_grad, 1, 1, 3 * own, deps=sends)
    triple_mine = weight(hidden_in, projected_grad, 0, 1, 3 * own, deps=(triple_theirs,))
    triple_flow = Flow(scatter_flow(triple_mine, [swap(triple_theirs)], n_dp), triple_then)
    sends = triple_flow.advance() + expand_flow.advance(triple_mine)
    input_own, input_grad = input_side(
        place, projected_grad, triple_weight, triple_other, pre_one_grad, deps=sends
    )

    triple_flow.advance(input_own)
    contract_flow.advance(triple_flow.sends)
    expand_flow.advance(triple_flow.sends)
    layer_out = put_other(place, layer_other, layer_out, deps=triple_flow.sends)

    d = norm_vectors.shape[1]
    sums_pair, bias_mine, bias_theirs = behind([sums_pair, bias_mine, bias_theirs], layer_out)
    pair_grad = jnp.sum(sums_pair, axis=0)[:2]
    spare = jnp.zeros((8 - (2 * own + n_bias) // d, d), WIDE)
    bundle = lambda left, right, bias: jnp.concatenate(
        [
            sums_one,
            sums_two,
            pair_grad[:, left:right].reshape(-1, d),
            bias.reshape(-1, d),
            spare,
        ]
    )
    vector_flow = Flow(
        total_flow(bundle(0, own, bias_mine), bundle(own, 2 * own, bias_theirs), n_dp)
    )
    vector_flow.advance()
    triple_flow.advance(layer_out)
    contract_flow.advance(triple_flow.sends)
    input_grad = put_other(place, swap(input_own), input_grad, deps=triple_flow.sends)
    vector_flow.advance(input_grad)
    expand_flow.advance(input_grad)
    triple_flow.advance(input_grad)
    gather = partial(gather_place, place, n_dp)
    contract_flow.finish()
    (contract_copy,) = gather(
        (("flip", 0, n_bias),), *contract_flow.result, deps=triple_flow.sends
    )
    vector_flow.advance(contract_copy)
    expand_flow.advance(contract_copy)
    triple_flow.advance(contract_copy)
    vector_flow.advance(triple_flow.sends)
    expand_flow.finish()
    expand_copy, outward_copy = gather(
        (("plain", 0, n_bias), ("flip", n_bias, n_bias + own)),
        *expand_flow.result,
        deps=triple_flow.sends,
    )
    triple_flow.advance(expand_copy)
    vector_sum = vector_flow.finish()
    triple_flow.finish()
    (triple_copy,) = gather((("deep", 0, 3 * own),), *triple_flow.result)
    vector_total = jnp.stack([vector_sum[i] for i in (0, 8, 1, 2, 9, 10)])
    pair_total = vector_sum[16 : 16 + 2 * own // d].reshape(2, own)
    widen_total = vector_sum[16 + 2 * own // d :].reshape(-1)[:n_bias]
    contract_new, expand_new = updates["contract"], updates["expand"]
    outward_new, triple_new = updates["outward"], updates["triple"]
    pair_new = adamw_step(pair_bias, pair_first, pair_second, pair_total, 0.0)
    widen_new = adamw_step(expand_bias, expand_bias_first, expand_bias_second, widen_total, 0.0)
    vectors_new = adamw_step(norm_vectors, vectors_first, vectors_second, vector_total, 0.0)
    return (
        layer_out,
        input_grad,
        triple_new[0],
        triple_new[1],
        triple_new[2],
        triple_copy,
        outward_new[0].T,
        outward_new[1].T,
        outward_new[2].T,
        outward_copy,
        expand_new[0],
        expand_new[1],
        expand_new[2],
        expand_copy,
        contract_new[0].T,
        contract_new[1].T,
        contract_new[2].T,
        contract_copy,
        pair_new[0],
        pair_new[1],
        pair_new[2],
        widen_new[0],
        widen_new[1],
        widen_new[2],
        vectors_new[0],
        vectors_new[1],
        vectors_new[2],
    )


def solution(mesh):
    matrix_specs = (
        P(None, "dp", "tensor"),
        P("tensor", "dp"),
        P("dp", "tensor"),
        P("tensor", "dp"),
    )
    copy_specs = (P(None, None, "tensor"), P("tensor", None), P(None, "tensor"), P("tensor", None))
    vector_specs = (P(None, "tensor"),) * 3 + (P("tensor"),) * 3 + (P(),) * 3
    in_specs = (
        (P("dp", None), P("dp", None), P("dp"), P("dp", None))
        + copy_specs
        + tuple(spec for spec in matrix_specs for _ in range(3))
        + vector_specs
    )
    out_specs = (P("dp", None), P("dp", None))
    for spec, copied in zip(matrix_specs, copy_specs):
        out_specs += (spec,) * 3 + (copied,)
    out_specs += vector_specs
    return jax.shard_map(
        partial(local, mesh.shape["dp"]),
        mesh=mesh,
        in_specs=in_specs,
        out_specs=out_specs,
        check_vma=False,
    )
```

```python
from functools import partial

import jax
import jax.numpy as jnp
from jax import lax
from jax.experimental import pallas as pl
from jax.experimental.pallas import tpu as pltpu
from jax.sharding import PartitionSpec as P

HEAD_DIM = 64
STEP = 7


MASK_FILL = -1e30
NORM_EPSILON = 1e-05
FIRST_DECAY = 0.5
SECOND_DECAY = 0.5
LEARN_RATE = 0.1
WEIGHT_DECAY = 0.01
EPSILON = 1e-08
LOW = jnp.bfloat16
WIDE = jnp.float32


BLOCK_FF = 512
NO_COST = pl.CostEstimate(flops=0, bytes_accessed=0, transcendentals=0)
LONG = pl.CostEstimate(flops=5 * 10**10, bytes_accessed=10**8, transcendentals=0)
VMEM = pltpu.CompilerParams(vmem_limit_bytes=64 * 2**20)
ROOT_HALF = 0.7071067811865476
BELL_TOP = 0.3989422804014327


def dot(left, right):
    return jnp.dot(left, right, preferred_element_type=WIDE)


def dot_nt(left, right):
    return lax.dot_general(left, right, (((1,), (1,)), ((), ())), preferred_element_type=WIDE)


def dot_tn(left, right):
    return lax.dot_general(left, right, (((0,), (0,)), ((), ())), preferred_element_type=WIDE)


def gelu_pair(x):
    cdf = 0.5 * lax.erf(x * ROOT_HALF) + 0.5
    return x * cdf, cdf + x * (jnp.exp(x * x * -0.5) * BELL_TOP)


def mean_rows(value):
    return jnp.mean(value, axis=-1, keepdims=True)


def norm_parts(pre):
    centred = pre - mean_rows(pre)
    inverse = lax.rsqrt(mean_rows(centred * centred) + NORM_EPSILON)
    return centred * inverse, inverse


def norm_grad(upstream, normed, inverse, gain):
    scaled = upstream * gain
    return inverse * (scaled - mean_rows(scaled) - normed * mean_rows(scaled * normed))


def col_sum(value):
    return jnp.sum(value, axis=0, keepdims=True)


def fold_rows(value):
    return jnp.sum(value.reshape(-1, 8, value.shape[1]), axis=0)


def by_rows(count, body, start, unroll=1):
    at = lambda r: pl.ds(pl.multiple_of(r * TILE, TILE), TILE)
    return lax.fori_loop(0, count // TILE, lambda r, c: body(at(r), c), start, unroll=unroll)


def lane_half(shape, e):
    lane = lax.broadcasted_iota(jnp.int32, shape, 1)
    return (lane < HEAD_DIM) if e == 0 else (lane >= HEAD_DIM)


TILE = 256


def attend_kernel(
    place, lengths, x_ref, mask_ref, w0_ref, w1_ref, o0_ref, o1_ref, p0_ref, p1_ref, nv_ref,
    qkv_ref, probs_ref, ctx_ref, pre_ref, score_s,
):
    x = x_ref[...]
    row = place[0] * pl.num_programs(0) + pl.program_id(0)
    slot = lax.broadcasted_iota(jnp.int32, (1, x.shape[0]), 1)
    present = (mask_ref[pl.ds(row, 1)] == 1) | (slot == 0)
    valid = jnp.where((slot < lengths[row]) & present, 1.0, 0.0)
    valid = jnp.broadcast_to(valid, (16, x.shape[0])).astype(LOW)
    bias = (1.0 - dot_tn(valid, jnp.full((16, 128), 0.0625, LOW))) * MASK_FILL
    width = w0_ref.shape[2]
    pairs = width // 128
    scale = jnp.asarray(HEAD_DIM ** (-0.5), LOW)
    for half, (w_ref, p_ref) in enumerate(((w0_ref, p0_ref), (w1_ref, p1_ref))):
        base = 3 * width * half
        q = dot(x, w_ref[0]) + p_ref[0:1]
        qkv_ref[:, base : base + width] = q.astype(LOW)
        qkv_ref[:, base + width : base + 2 * width] = dot(x, w_ref[1]).astype(LOW)
        v = dot(x, w_ref[2]) + p_ref[1:2]
        qkv_ref[:, base + 2 * width : base + 3 * width] = v.astype(LOW)
    for half in range(2):
        base = 3 * width * half
        for pair in range(pairs):
            at = base + 128 * pair
            kp = qkv_ref[:, at + width : at + width + 128] * scale
            for e in range(2):
                ke = jnp.where(lane_half(kp.shape, e), kp, jnp.zeros_like(kp))
                score_s[2 * pair + e] = dot_nt(ke, qkv_ref[:, at : at + 128])
        for head in range(2 * pairs):
            for left in range(0, x.shape[0], 128):
                masked = score_s[head, :, left : left + 128] + bias
                top = jnp.max(masked, axis=0, keepdims=True)
                ex = jnp.exp(masked - top)
                total = jnp.sum(ex, axis=0, keepdims=True)
                low = (ex * (1.0 / total)).astype(LOW)
                probs_ref[0, half * 2 * pairs + head, :, left : left + 128] = low
        vt = qkv_ref[:, base + 2 * width : base + 3 * width].T
        for pair in range(pairs):
            outs = []
            for e in range(2):
                low = 128 * pair + HEAD_DIM * e
                outs.append(
                    dot(vt[low : low + HEAD_DIM], probs_ref[0, half * 2 * pairs + 2 * pair + e])
                )
            ctx = jnp.concatenate(outs, axis=0).T.astype(LOW)
            ctx_ref[:, half * width + 128 * pair : half * width + 128 * pair + 128] = ctx
    attn = dot(ctx_ref[:, :width], o0_ref[...]) + dot(ctx_ref[:, width:], o1_ref[...])
    pre_ref[...] = x.astype(WIDE) + nv_ref[0:1] + attn


def attend(place, lengths, hidden_in, key_mask, w0, w1, o0, o1, p0, p1, nv):
    seqs, seq_len = key_mask.shape[0] // 2, key_mask.shape[1]
    d = hidden_in.shape[1]
    width = w0.shape[2]
    heads = 2 * width // HEAD_DIM
    tokens = seqs * seq_len
    full = lambda a: pl.BlockSpec(a.shape, lambda s, c, n: (0,) * a.ndim)
    rows = lambda cols: pl.BlockSpec((seq_len, cols), lambda s, c, n: (s, 0))
    return pl.pallas_call(
        attend_kernel,
        out_shape=(
            jax.ShapeDtypeStruct((tokens, 6 * width), LOW),
            jax.ShapeDtypeStruct((seqs, heads, seq_len, seq_len), LOW),
            jax.ShapeDtypeStruct((tokens, 2 * width), LOW),
            jax.ShapeDtypeStruct((tokens, d), WIDE),
        ),
        grid_spec=pltpu.PrefetchScalarGridSpec(
            num_scalar_prefetch=2,
            grid=(seqs,),
            in_specs=[
                pl.BlockSpec((seq_len, d), lambda s, c, n: (c[0] * seqs + s, 0)),
                *(full(a) for a in (key_mask, w0, w1, o0, o1, p0, p1, nv)),
            ],
            out_specs=[
                rows(6 * width),
                pl.BlockSpec((1, heads, seq_len, seq_len), lambda s, c, n: (s, 0, 0, 0)),
                rows(2 * width),
                rows(d),
            ],
            scratch_shapes=[pltpu.VMEM((heads // 2, seq_len, seq_len), WIDE)],
        ),
        compiler_params=VMEM,
        name="attend",
        cost_estimate=LONG,
    )(place, lengths, hidden_in, key_mask, w0, w1, o0, o1, p0, p1, nv)


ROWS = 512


def ffn_fwd_kernel(
    core, pre_ref, up_ref, e0_ref, e1_ref, c0_ref, c1_ref, b0_ref, b1_ref, nv_ref,
    act_ref, slope_ref, out_ref, grad_ref, low_ref, hl_ref, sums_ref, whole_ref,
    acc_s, wide_s,
):
    j = pl.program_id(0)
    last = pl.num_programs(0) - 1
    tokens = pre_ref.shape[0]

    @pl.when(j == 0)
    def _():
        def one(rows, _):
            normed, _ = norm_parts(pre_ref[rows])
            hidden_one = normed * nv_ref[2:3] + nv_ref[3:4]
            hl_ref[rows] = hidden_one.astype(LOW)
            acc_s[rows] = hidden_one + nv_ref[1:2]
            return 0

        by_rows(tokens, one, 0)

    def step(e_ref, c_ref, b_ref):
        for top in range(0, tokens, ROWS):
            wide_s[top : top + ROWS] = dot(hl_ref[top : top + ROWS], e_ref[...])
        for top in range(0, tokens, ROWS):
            for at in range(top, top + ROWS, 16):
                rows = slice(at, at + 16)
                act, slope = gelu_pair(wide_s[rows] + b_ref[...])
                act_ref[rows] = act.astype(LOW)
                slope_ref[rows] = slope.astype(LOW)
            acc_s[top : top + ROWS] += dot(act_ref[top : top + ROWS], c_ref[...])

    @pl.when(j < (last + 1) // 2)
    def _():
        step(e0_ref, c0_ref, b0_ref)

    @pl.when(j >= (last + 1) // 2)
    def _():
        step(e1_ref, c1_ref, b1_ref)

    @pl.when(j == last)
    def _():
        def one(rows, sums):
            normed, inverse = norm_parts(acc_s[rows])
            out = (normed * nv_ref[4:5] + nv_ref[5:6]).astype(LOW)
            out_ref[rows] = out
            whole_ref[rows] = out
            up = up_ref[rows].astype(WIDE)
            grad = norm_grad(up, normed, inverse, nv_ref[4:5])
            grad_ref[rows] = grad
            low_ref[rows] = grad.astype(LOW)
            new = (fold_rows(grad), fold_rows(up * normed), fold_rows(up))
            return tuple(a + b for a, b in zip(sums, new))

        zero = jnp.zeros((8, pre_ref.shape[1]), WIDE)
        sums = by_rows(tokens, one, (zero,) * 3, unroll=1)
        for i in range(3):
            sums_ref[i : i + 1] = col_sum(sums[i])
        sums_ref[3:8] = jnp.zeros((5, sums_ref.shape[1]), WIDE)


def ffn_fwd(core, pre, grad_out, e0, e1, c0, c1, b0, b1, nv):
    tokens, d = pre.shape
    width = e0.shape[1]
    steps = width // BLOCK_FF
    full = lambda shape: pl.BlockSpec(shape, lambda j, c: (0,) * len(shape))
    lower = lambda j: jnp.minimum(j, steps - 1)
    upper = lambda j: jnp.maximum(j - steps, 0)
    return pl.pallas_call(
        ffn_fwd_kernel,
        out_shape=(
            jax.ShapeDtypeStruct((tokens, 2 * width), LOW),
            jax.ShapeDtypeStruct((tokens, 2 * width), LOW),
            jax.ShapeDtypeStruct((tokens, d), LOW),
            jax.ShapeDtypeStruct((tokens, d), WIDE),
            jax.ShapeDtypeStruct((tokens, d), LOW),
            jax.ShapeDtypeStruct((tokens, d), LOW),
            jax.ShapeDtypeStruct((8, d), WIDE),
            jax.ShapeDtypeStruct((2 * tokens, d), LOW),
        ),
        grid_spec=pltpu.PrefetchScalarGridSpec(
            num_scalar_prefetch=1,
            grid=(2 * steps,),
            in_specs=[
                full((tokens, d)),
                pl.BlockSpec((tokens, d), lambda j, c: (c[0], 0)),
                pl.BlockSpec((d, BLOCK_FF), lambda j, c: (0, lower(j))),
                pl.BlockSpec((d, BLOCK_FF), lambda j, c: (0, upper(j))),
                pl.BlockSpec((BLOCK_FF, d), lambda j, c: (lower(j), 0)),
                pl.BlockSpec((BLOCK_FF, d), lambda j, c: (upper(j), 0)),
                pl.BlockSpec((1, BLOCK_FF), lambda j, c: (0, lower(j))),
                pl.BlockSpec((1, BLOCK_FF), lambda j, c: (0, upper(j))),
                full(nv.shape),
            ],
            out_specs=[
                pl.BlockSpec((tokens, BLOCK_FF), lambda j, c: (0, j)),
                pl.BlockSpec((tokens, BLOCK_FF), lambda j, c: (0, j)),
                full((tokens, d)),
                full((tokens, d)),
                full((tokens, d)),
                full((tokens, d)),
                full((8, d)),
                pl.BlockSpec((tokens, d), lambda j, c: (c[0], 0)),
            ],
            scratch_shapes=[pltpu.VMEM((tokens, d), WIDE), pltpu.VMEM((tokens, BLOCK_FF), WIDE)],
        ),
        compiler_params=VMEM,
        name="ffn_fwd",
        cost_estimate=LONG,
    )(core, pre, grad_out, e0, e1, c0, c1, b0, b1, nv)


def reverse(value, count):
    out = value & 0
    for bit in range(count.bit_length() - 1):
        out = out * 2 + ((value >> bit) & 1)
    return out


def spot(apart, count):
    return (apart & 3) * (count // 4) + reverse(apart >> 2, count // 4)


def place_rows(out_ref, value, rank, count, left=0):
    rows = value.shape[0] // count
    cols = slice(left, left + value.shape[1])
    if rows % 16:
        out_ref[:, cols] = value
        return
    for i in range(count):
        at = spot(jnp.bitwise_xor(rank, i), count)
        there = pl.ds(pl.multiple_of(at * rows, 16), rows)
        out_ref[there, cols] = value[i * rows : (i + 1) * rows]


def placed(grad, rank, count):
    rows = grad.shape[0] // count
    if rows % 16 == 0:
        return grad
    blocks = grad.reshape(count, rows, -1)
    apart = jnp.arange(count)
    return jnp.zeros_like(blocks).at[spot(apart ^ rank, count)].set(blocks).reshape(grad.shape)


ANY = pl.BlockSpec(memory_space=pl.ANY)


def with_deps(body, lead, inputs, deps):
    def kernel(*refs):
        body(*refs[: lead + inputs], *refs[lead + inputs + len(deps) :])

    return kernel


def weight_kernel(count, place, left_ref, right_ref, out_ref):
    place_rows(out_ref, dot_tn(left_ref[...], right_ref[...]).astype(LOW), place[1], count)


def weight_grad(place, n_dp, left, right, first, count, block, deps=()):
    tokens = right.shape[0]
    d = left.shape[1]
    halves = left.shape[0] // tokens
    out = pl.pallas_call(
        with_deps(partial(weight_kernel, n_dp), 1, 2, deps),
        out_shape=jax.ShapeDtypeStruct((d, count * block), LOW),
        grid_spec=pltpu.PrefetchScalarGridSpec(
            num_scalar_prefetch=1,
            grid=(count,),
            in_specs=[
                pl.BlockSpec((tokens, d), lambda j, c: (c[0] if halves == 2 else 0, 0)),
                pl.BlockSpec((tokens, block), lambda j, c: (0, first + j)),
            ]
            + [ANY] * len(deps),
            out_specs=pl.BlockSpec((d, block), lambda j, c: (0, j)),
        ),
        compiler_params=VMEM,
        name="weight_grad",
        cost_estimate=LONG,
    )(place, left, right, *deps)
    return placed(out, place[1], n_dp)


def ffn_bwd_kernel(
    final, n_dp, place, low_ref, slope_ref, e_ref, c_ref, sofar_ref, pre_ref, hl_ref, ctx_ref, nv_ref,
    we_ref, bias_ref, one_ref, *rest,
):
    if final:
        ag_ref, sums_ref, wo_ref, acc_s, wg_s, wide_s = rest
    else:
        acc_s, wg_s, wide_s = rest
    j = pl.program_id(0)
    last = pl.num_programs(0) - 1
    tokens = low_ref.shape[0]

    @pl.when(j == 0)
    def _():
        acc_s[...] = sofar_ref[...]

    for top in range(0, tokens, ROWS):
        wide_s[top : top + ROWS] = dot_nt(low_ref[top : top + ROWS], c_ref[...])
    bias = jnp.zeros((8, BLOCK_FF), WIDE)
    for top in range(0, tokens, ROWS):
        for at in range(top, top + ROWS, 16):
            rows = slice(at, at + 16)
            wg = (wide_s[rows] * slope_ref[rows].astype(WIDE)).astype(LOW)
            wg_s[rows] = wg
            bias = bias + fold_rows(wg.astype(WIDE))
        acc_s[top : top + ROWS] += dot_nt(wg_s[top : top + ROWS], e_ref[...])
    bias_ref[...] = col_sum(bias)
    grad = dot_tn(hl_ref[...], wg_s[...]).astype(LOW)
    if final:
        for i in range(we_ref.shape[1] // BLOCK_FF):

            @pl.when(j == i)
            def _():
                place_rows(we_ref, grad, place[1], n_dp, i * BLOCK_FF)
    else:
        place_rows(we_ref, grad, place[1], n_dp)

    @pl.when(j == last)
    def _():
        if not final:
            one_ref[...] = acc_s[...]
            return

        def one(rows, sums):
            normed, inverse = norm_parts(pre_ref[rows])
            up = acc_s[rows]
            grad = norm_grad(up, normed, inverse, nv_ref[2:3])
            one_ref[rows] = grad
            ag_ref[rows] = grad.astype(LOW)
            new = (fold_rows(grad), fold_rows(up * normed), fold_rows(up))
            return tuple(a + b for a, b in zip(sums, new))

        zero = jnp.zeros((8, pre_ref.shape[1]), WIDE)
        sums = by_rows(tokens, one, (zero,) * 3, unroll=1)
        for i in range(3):
            sums_ref[i : i + 1] = col_sum(sums[i])
        sums_ref[3:8] = jnp.zeros((5, sums_ref.shape[1]), WIDE)
        half = wo_ref.shape[1]
        grad = dot_tn(ag_ref[...], ctx_ref[:, :half]).astype(LOW)
        place_rows(we_ref, grad, place[1], n_dp, we_ref.shape[1] - half)
        place_rows(wo_ref, dot_tn(ag_ref[...], ctx_ref[:, half:]).astype(LOW), place[1], n_dp)


def ffn_bwd(place, n_dp, final, low, slope, e, c, sofar, pre, hl, ctx, nv, deps=()):
    tokens, d = low.shape
    width = e.shape[1]
    steps = width // BLOCK_FF
    first = 0 if final else steps
    full = lambda shape: pl.BlockSpec(shape, lambda j, c: (0,) * len(shape))
    half = ctx.shape[1] // 2
    if final:
        both = (d, width + half)
        outs = [(jax.ShapeDtypeStruct(both, LOW), full(both))]
    else:
        outs = [
            (jax.ShapeDtypeStruct((d, width), LOW), pl.BlockSpec((d, BLOCK_FF), lambda j, c: (0, j)))
        ]
    outs += [
        (jax.ShapeDtypeStruct((1, width), WIDE), pl.BlockSpec((1, BLOCK_FF), lambda j, c: (0, j))),
        (jax.ShapeDtypeStruct((tokens, d), WIDE), full((tokens, d))),
    ]
    if final:
        outs += [
            (jax.ShapeDtypeStruct((tokens, d), LOW), full((tokens, d))),
            (jax.ShapeDtypeStruct((8, d), WIDE), full((8, d))),
            (jax.ShapeDtypeStruct((d, half), LOW), full((d, half))),
        ]
    out = pl.pallas_call(
        with_deps(partial(ffn_bwd_kernel, final, n_dp), 1, 9, deps),
        out_shape=tuple(o[0] for o in outs),
        grid_spec=pltpu.PrefetchScalarGridSpec(
            num_scalar_prefetch=1,
            grid=(steps,),
            in_specs=[
                full((tokens, d)),
                pl.BlockSpec((tokens, BLOCK_FF), lambda j, c: (0, first + j)),
                pl.BlockSpec((d, BLOCK_FF), lambda j, c: (0, j)),
                pl.BlockSpec((BLOCK_FF, d), lambda j, c: (j, 0)),
                full((tokens, d)),
                full((tokens, d)) if final else ANY,
                full((tokens, d)),
                full(ctx.shape) if final else ANY,
                full(nv.shape),
            ]
            + [ANY] * len(deps),
            out_specs=[o[1] for o in outs],
            scratch_shapes=[
                pltpu.VMEM((tokens, d), WIDE),
                pltpu.VMEM((tokens, BLOCK_FF), LOW),
                pltpu.VMEM((tokens, BLOCK_FF), WIDE),
            ],
        ),
        compiler_params=VMEM,
        name="ffn_bwd",
        cost_estimate=LONG,
    )(place, low, slope, e, c, sofar, pre, hl, ctx, nv, *deps)
    out = list(out)
    for i in (0, 5) if final else (0,):
        out[i] = placed(out[i], place[1], n_dp)
    return out


def attend_back_kernel(
    start, ag_ref, probs_ref, qkv_ref, o0_ref, o1_ref, sofar_ref, grad_ref, sums_ref,
    dp_s, ds_s, cg_s,
):
    @pl.when(pl.program_id(0) == 0)
    def _():
        sums_ref[...] = jnp.zeros_like(sums_ref) if start else sofar_ref[...]

    width = o0_ref.shape[0]
    pairs = width // 128
    scale = jnp.asarray(HEAD_DIM ** (-0.5), LOW)
    keep = [lane_half((ag_ref.shape[0], 128), e) for e in range(2)]
    side = lambda value, e: jnp.where(keep[e], value, jnp.zeros_like(value))
    for half, o_ref in enumerate((o0_ref, o1_ref)):
        cg_s[...] = dot_nt(ag_ref[...], o_ref[...]).astype(LOW)
        first = half * 2 * pairs
        for pair in range(pairs):
            at = 3 * width * half + 128 * pair
            do = cg_s[:, 128 * pair : 128 * pair + 128]
            vp = qkv_ref[:, at + 2 * width : at + 2 * width + 128]
            for e in range(2):
                dp_s[2 * pair + e] = dot_nt(side(vp, e), do)
            dv = dot(probs_ref[0, first + 2 * pair], side(do, 0))
            dv = (dv + dot(probs_ref[0, first + 2 * pair + 1], side(do, 1))).astype(LOW)
            grad_ref[:, at + 2 * width : at + 2 * width + 128] = dv
            to = half * width + 128 * pair
            sums_ref[1:2, to : to + 128] += col_sum(dv.astype(WIDE))
        for head in range(2 * pairs):
            for left in range(0, ag_ref.shape[0], 128):
                cols = slice(left, left + 128)
                dp = dp_s[head, :, cols]
                probs = probs_ref[0, first + head, :, cols].astype(WIDE)
                inner = jnp.sum(dp * probs, axis=0, keepdims=True)
                ds_s[head, :, cols] = (probs * (dp - inner)).astype(LOW)
        for pair in range(pairs):
            at = 3 * width * half + 128 * pair
            qp = qkv_ref[:, at : at + 128] * scale
            kp = qkv_ref[:, at + width : at + width + 128] * scale
            dk = dot(ds_s[2 * pair], side(qp, 0)) + dot(ds_s[2 * pair + 1], side(qp, 1))
            dq = dot_tn(ds_s[2 * pair], side(kp, 0)) + dot_tn(ds_s[2 * pair + 1], side(kp, 1))
            dq = dq.astype(LOW)
            grad_ref[:, at : at + 128] = dq
            grad_ref[:, at + width : at + width + 128] = dk.astype(LOW)
            to = half * width + 128 * pair
            sums_ref[0:1, to : to + 128] += col_sum(dq.astype(WIDE))


def attend_back(ag, probs, qkv, o0, o1, first, count, before=None, deps=()):
    seqs, heads, seq_len, _ = probs.shape
    tokens, d = ag.shape
    width = o0.shape[0]
    full = lambda shape: pl.BlockSpec(shape, lambda s: (0,) * len(shape))
    rows = lambda cols: pl.BlockSpec((seq_len, cols), lambda s: (first + s, 0))
    sums = (8, 2 * width)
    start = before is None
    if not start:
        deps = (before[0],) + tuple(deps)
    return pl.pallas_call(
        with_deps(partial(attend_back_kernel, start), 0, 6, deps),
        out_shape=(
            jax.ShapeDtypeStruct((tokens, 6 * width), LOW),
            jax.ShapeDtypeStruct(sums, WIDE),
        ),
        grid=(count,),
        in_specs=[
            rows(d),
            pl.BlockSpec((1, heads, seq_len, seq_len), lambda s: (first + s, 0, 0, 0)),
            rows(6 * width),
            full(o0.shape),
            full(o1.shape),
            ANY if start else full(sums),
        ]
        + [ANY] * len(deps),
        out_specs=[rows(6 * width), full(sums)],
        input_output_aliases={} if start else {6: 0},
        scratch_shapes=[
            pltpu.VMEM((heads // 2, seq_len, seq_len), WIDE),
            pltpu.VMEM((heads // 2, seq_len, seq_len), LOW),
            pltpu.VMEM((seq_len, width), LOW),
        ],
        compiler_params=VMEM,
        name="attend_back",
        cost_estimate=LONG,
    )(ag, probs, qkv, o0, o1, ag if start else before[1], *deps)


def input_kernel(place, grad_ref, w0_ref, w1_ref, one_ref, out_ref, whole_ref):
    width = w0_ref.shape[2]
    total = one_ref[...]
    for i in range(6):
        w = (w0_ref, w1_ref)[i // 3][i % 3]
        total = total + dot_nt(grad_ref[:, i * width : (i + 1) * width], w)
    out_ref[...] = total.astype(LOW)
    whole_ref[...] = total.astype(LOW).astype(WIDE)


def input_side(place, grad, w0, w1, one, deps=()):
    tokens, d = one.shape
    block = min(ROWS, tokens)
    full = lambda a: pl.BlockSpec(a.shape, lambda s, c: (0,) * a.ndim)
    rows = lambda cols: pl.BlockSpec((block, cols), lambda s, c: (s, 0))
    return pl.pallas_call(
        with_deps(input_kernel, 1, 4, deps),
        out_shape=(
            jax.ShapeDtypeStruct((tokens, d), LOW),
            jax.ShapeDtypeStruct((2 * tokens, d), WIDE),
        ),
        grid_spec=pltpu.PrefetchScalarGridSpec(
            num_scalar_prefetch=1,
            grid=(tokens // block,),
            in_specs=[rows(grad.shape[1]), full(w0), full(w1), rows(d)] + [ANY] * len(deps),
            out_specs=[
                rows(d),
                pl.BlockSpec((block, d), lambda s, c: (c[0] * (tokens // block) + s, 0)),
            ],
        ),
        compiler_params=VMEM,
        name="input_side",
        cost_estimate=LONG,
    )(place, grad, w0, w1, one, *deps)


def bundle_kernel(one_ref, two_ref, pair_ref, b0_ref, b1_ref, mine_ref, theirs_ref):
    half = pair_ref.shape[1] // 2
    d = one_ref.shape[1]
    for i, (ref, b_ref) in enumerate(((mine_ref, b0_ref), (theirs_ref, b1_ref))):
        ref[...] = jnp.zeros_like(ref)
        ref[0:8] = one_ref[...]
        ref[8:16] = two_ref[...]
        for j in range(2):
            ref[16:17, j * half : (j + 1) * half] = pair_ref[j : j + 1, i * half : (i + 1) * half]
        for j in range(b_ref.shape[1] // d):
            ref[17 + j : 18 + j] = b_ref[:, j * d : (j + 1) * d]


def bundle(one, two, pair, mine, theirs, deps=()):
    out = jax.ShapeDtypeStruct((24, one.shape[1]), WIDE)
    spec = lambda a: pl.BlockSpec(a.shape, lambda: (0, 0))
    return pl.pallas_call(
        with_deps(bundle_kernel, 0, 5, deps),
        out_shape=(out, out),
        in_specs=[spec(a) for a in (one, two, pair, mine, theirs)] + [ANY] * len(deps),
        out_specs=(spec(out), spec(out)),
        name="bundle",
    )(one, two, pair, mine, theirs, *deps)


def gather_kernel(count, layout, place, z_ref, x_ref, y_ref, da_ref, db_ref, *refs):
    outs, scratch = refs[: len(layout)], list(refs[len(layout) :])
    tos = [scratch.pop(0) if kind == "flip" else out for (kind, _, _), out in zip(layout, outs)]
    block = z_ref.shape[0] // (count // 4)
    for apart in range(count):
        at = jnp.bitwise_xor(place[1], apart)
        first = reverse(apart >> 2, count // 4) * block
        ref = (z_ref, x_ref, y_ref, da_ref)[apart & 3]
        if apart & 3 == 3 and first >= da_ref.shape[0]:
            ref, first = db_ref, first - da_ref.shape[0]
        for (kind, left, right), to in zip(layout, tos):
            if kind == "deep":
                rows = block // to.shape[0]
                for i in range(to.shape[0]):
                    here = slice(first + i * rows, first + i * rows + rows)
                    to[i, pl.ds(pl.multiple_of(at * rows, 16), rows)] = ref[here]
            else:
                there = pl.ds(pl.multiple_of(at * block, 16), block)
                to[there] = ref[first : first + block, left:right]
    for (kind, _, _), out, to in zip(layout, outs, tos):
        if kind == "flip":
            out[...] = to[...].T


def gather_place(place, n_dp, layout, z, x, y, da, db, deps=()):
    rows, cols = z.shape[0] * 4, z.shape[1]
    block = rows // n_dp
    deep = [right - left for kind, left, right in layout if kind == "deep"]
    shapes = []
    for kind, left, right in layout:
        wide = right - left
        if kind == "deep":
            shapes.append((wide // cols, rows * cols // wide, cols))
        else:
            shapes.append((wide, rows) if kind == "flip" else (rows, wide))
    if (block // (shapes[0][0] if deep else 1)) % 16:
        plane = jnp.stack([z, x, y, jnp.concatenate([da, db])])
        blocks = plane.reshape(n_dp, block, cols)[spot(jnp.arange(n_dp) ^ place[1], n_dp)]
        outs = []
        for (kind, left, right), shape in zip(layout, shapes):
            if kind == "deep":
                outs.append(blocks.reshape(n_dp, shape[0], -1, cols).transpose(1, 0, 2, 3).reshape(shape))
            else:
                whole = blocks.reshape(rows, cols)[:, left:right]
                outs.append(whole.T if kind == "flip" else whole)
        return outs
    spec = lambda a: pl.BlockSpec(a.shape, lambda s, c: (0, 0))
    return pl.pallas_call(
        with_deps(partial(gather_kernel, n_dp, layout), 1, 5, deps),
        out_shape=[jax.ShapeDtypeStruct(shape, LOW) for shape in shapes],
        grid_spec=pltpu.PrefetchScalarGridSpec(
            num_scalar_prefetch=1,
            grid=(1,),
            in_specs=[spec(a) for a in (z, x, y, da, db)] + [ANY] * len(deps),
            out_specs=[pl.BlockSpec(s, lambda i, c, n=len(s): (0,) * n) for s in shapes],
            scratch_shapes=[
                pltpu.VMEM(shape[::-1], LOW)
                for (kind, _, _), shape in zip(layout, shapes)
                if kind == "flip"
            ],
        ),
        compiler_params=VMEM,
        name="gather_place",
        cost_estimate=LONG,
    )(place, z, x, y, da, db, *deps)


def combine_kernel(plan, *refs):
    outs = refs[len(refs) - len(plan) :]
    for parts, out in zip(plan, outs):
        rows = out.shape[0] // len(parts)
        for i, terms in enumerate(parts):
            sides = []
            for inputs in terms:
                pieces = [refs[r][...].astype(WIDE) for r in inputs]
                sides.append(pieces[0] if not pieces[1:] else jnp.concatenate(pieces, axis=1))
            out[i * rows : (i + 1) * rows] = sum(sides[1:], sides[0]).astype(LOW)


def cut(terms, rows):
    take = lambda a, n: a[n * rows : (n + 1) * rows].astype(WIDE)
    sides = [jnp.concatenate([take(a, n) for a, n in term], axis=1) for term in terms]
    return sum(sides[1:], sides[0])


class Blocks:
    def __init__(self, rows):
        self.rows, self.arrays, self.specs = rows, [], []

    def add(self, terms):
        plan = []
        for term in terms:
            plan.append([])
            for array, number in term:
                plan[-1].append(len(self.arrays))
                self.arrays.append(array)
                self.specs.append(
                    pl.BlockSpec((self.rows, array.shape[1]), lambda i, number=number: (number, 0))
                )
        return plan


def combine(results, rows, deps=()):
    if rows % 16:
        return [
            jnp.concatenate([cut(terms, rows) for terms in parts]).astype(LOW) for parts in results
        ]
    blocks = Blocks(rows)
    plan = [[blocks.add(terms) for terms in parts] for parts in results]
    shapes = [
        (rows * len(parts), sum(a.shape[1] for a, _ in parts[0][0])) for parts in results
    ]
    return pl.pallas_call(
        with_deps(partial(combine_kernel, plan), 0, len(blocks.arrays), deps),
        out_shape=[jax.ShapeDtypeStruct(s, LOW) for s in shapes],
        grid=(1,),
        in_specs=blocks.specs + [ANY] * len(deps),
        out_specs=[pl.BlockSpec(s, lambda i: (0, 0)) for s in shapes],
        compiler_params=VMEM,
        name="combine",
        cost_estimate=NO_COST,
    )(*blocks.arrays, *deps)


def adamw_step(master, first_moment, second_moment, gradient, decay_rate):
    first_new = FIRST_DECAY * first_moment + (1.0 - FIRST_DECAY) * gradient
    second_new = SECOND_DECAY * second_moment + (1.0 - SECOND_DECAY) * gradient * gradient
    first_fixed = first_new / (1.0 - FIRST_DECAY**STEP)
    second_fixed = second_new / (1.0 - SECOND_DECAY**STEP)
    direction = first_fixed / (jnp.sqrt(second_fixed) + EPSILON)
    master_new = master - LEARN_RATE * (direction + decay_rate * master)
    return (master_new, first_new, second_new)


def update_kernel(plan, widths, deep, *refs):
    inputs, rest = refs[: len(refs) - 6 * len(widths) - 1], refs[len(refs) - 6 * len(widths) - 1 :]
    states, outs, copy_ref = rest[: 3 * len(widths)], rest[3 * len(widths) : -1], rest[-1]
    gradient = 0.0
    for term in plan:
        pieces = [inputs[r][...].astype(WIDE) for r in term]
        gradient = gradient + (pieces[0] if not pieces[1:] else jnp.concatenate(pieces, axis=1))
    rows, at = gradient.shape[0], 0
    for i, width in enumerate(widths):
        mine, to = states[3 * i : 3 * i + 3], outs[3 * i : 3 * i + 3]
        groups = deep or 1
        for j in range(groups):
            part = gradient[:, at : at + width // groups]
            old = [ref[j] if deep else ref[...] for ref in mine]
            new = adamw_step(*old, part, WEIGHT_DECAY)
            for ref, value in zip(to, new):
                if deep:
                    ref[j] = value
                else:
                    ref[...] = value
            if deep:
                copy_ref[j * rows : (j + 1) * rows] = new[0].astype(LOW)
            else:
                copy_ref[:, at : at + width] = new[0].astype(LOW)
            at += width // groups


def update(terms, rows, states, deep=0):
    count = lambda s: s[0].shape[0] * s[0].shape[2] if deep else s[0].shape[1]
    widths = [count(s) for s in states]
    total = sum(widths)
    if rows % 16:
        gradient, at, news = cut(terms, rows), 0, []
        for state, width in zip(states, widths):
            part = gradient[:, at : at + width]
            if deep:
                part = jnp.stack(jnp.split(part, deep, axis=1))
            news.append(adamw_step(*state, part, WEIGHT_DECAY))
            at += width
        copies = [n[0].astype(LOW) for n in news]
        if deep:
            return news, copies[0].reshape(-1, copies[0].shape[2])
        return news, jnp.concatenate(copies, axis=1)
    blocks = Blocks(rows)
    plan = blocks.add(terms)
    spec = lambda a: pl.BlockSpec(a.shape, lambda i: (0,) * a.ndim)
    flat = [a for state in states for a in state]
    copy = jax.ShapeDtypeStruct((rows * deep, total // deep) if deep else (rows, total), LOW)
    outs = [jax.ShapeDtypeStruct(a.shape, WIDE) for a in flat] + [copy]
    out = pl.pallas_call(
        partial(update_kernel, plan, widths, deep),
        out_shape=outs,
        grid=(1,),
        in_specs=blocks.specs + [spec(a) for a in flat],
        out_specs=[spec(a) for a in outs],
        compiler_params=VMEM,
        name="update",
        cost_estimate=NO_COST,
    )(*blocks.arrays, *flat)
    return [out[3 * i : 3 * i + 3] for i in range(len(states))], out[-1]


def put_kernel(place, other_ref, whole_ref, out_ref):
    out_ref[...] = other_ref[...].astype(out_ref.dtype)


def put_other(place, other, whole, deps=()):
    tokens, d = other.shape
    return pl.pallas_call(
        with_deps(put_kernel, 1, 2, deps),
        out_shape=jax.ShapeDtypeStruct(whole.shape, whole.dtype),
        grid_spec=pltpu.PrefetchScalarGridSpec(
            num_scalar_prefetch=1,
            grid=(1,),
            in_specs=[pl.BlockSpec((tokens, d), lambda s, c: (0, 0)), ANY] + [ANY] * len(deps),
            out_specs=pl.BlockSpec((tokens, d), lambda s, c: (1 - c[0], 0)),
        ),
        input_output_aliases={2: 0},
        compiler_params=VMEM,
        name="put_other",
        cost_estimate=LONG,
    )(place, other, whole, *deps)


def swap(value):
    return lax.ppermute(value, "tensor", [(0, 1), (1, 0)])


def across(value, apart, count):
    return lax.ppermute(value, "dp", [(i, i ^ apart) for i in range(count)])


def far_digits(count, direct):
    weights = [1 << bit for bit in range(2, count.bit_length() - 1)]
    size = 2 if direct else 1
    return [weights[i : i + size] for i in range(0, len(weights), size)]


def distances(digit):
    out = [0]
    for weight in digit:
        out = [d + e for d in out for e in (0, weight)]
    return out


def scatter_flow(mine, came, count, direct=False):
    rows, width = mine.shape
    block = rows // 8

    def part(y, x, half):
        at = (y * 2 + x) * 2 + half
        return [[(mine, at)], [(c, at) for c in came]]

    to_x, to_y = combine(
        [[part(0, 1, 0), part(1, 1, 0)], [part(1, 0, 1), part(1, 1, 1)]], block
    )
    send_both = lambda v: [across(v[0], 1, count), across(v[1], 2, count)]
    from_x, from_y = yield [to_x, to_y], send_both
    to_y, to_x = combine(
        [[part(1, 0, 0) + [[(from_x, 1)]]], [part(0, 1, 1) + [[(from_y, 1)]]]], block
    )
    last_x, last_y = yield [to_x, to_y], send_both
    upper = part(0, 0, 0) + [[(from_x, 0)], [(last_y, 0)]]
    lower = part(0, 0, 1) + [[(from_y, 0)], [(last_x, 0)]]

    half = block
    terms = None
    for digit in far_digits(count, direct):
        apart = distances(digit)
        if terms is None:
            half = half * 2 // len(apart)
            pieces = [upper, lower]
            if len(apart) == 4:
                pieces = [divide(p, 2, i) for p in pieces for i in range(2)]
        else:
            half = half // len(apart)
            pieces = [divide(terms, len(apart), i) for i in range(len(apart))]
        sends = combine([[piece] for piece in pieces[1:]], half)
        came = yield (
            sends,
            lambda v, apart=apart: [across(p, d, count) for p, d in zip(v, apart[1:])],
        )
        terms = pieces[0] + [[(c, 0)] for c in came]
    return terms, half


def divide(terms, members, number):
    return [[(a, n * members + number) for a, n in term] for term in terms]


def gather_flow(shard, count, direct=False):
    held = shard
    for digit in reversed(far_digits(count, direct)):
        apart = distances(digit)
        came = yield (
            [held],
            lambda v, apart=apart: [across(v[0], d, count) for d in apart[1:]],
        )
        (held,) = combine([[[[(h, 0)]] for h in [held] + list(came)]], held.shape[0])
    half = held.shape[0] // 2
    x, y = yield [held], lambda v: [across(v[0], 1, count), across(v[0], 2, count)]
    upper, lower = combine([[[[(x, 0)]]], [[[(y, 1)]]]], half)
    both = yield [upper, lower], lambda v: [across(v[0], 2, count), across(v[1], 1, count)]
    return held, x, y, both[0], both[1]


def total_flow(mine, others, count):
    (came,) = yield [others], lambda v: [swap(v[0])]
    total = mine + came
    apart = 1
    while apart < count:
        (came,) = yield [total], lambda v, apart=apart: [across(v[0], apart, count)]
        total = total + came
        apart *= 2
    return total


def behind(value, after):
    return lax.optimization_barrier((value, after))[0]


class Flow:
    def __init__(self, steps, then=None):
        self.steps, self.then = steps, then
        self.came, self.result, self.done = None, None, False
        self.sends = ()

    def advance(self, after=None):
        if after is not None and self.came is not None:
            self.came = behind(list(self.came), after)
        while not self.done:
            try:
                sends, send = self.steps.send(self.came)
            except StopIteration as stop:
                if self.then is None:
                    self.result, self.done = stop.value, True
                    return []
                self.steps, self.then = self.then(stop.value)
                self.came = None
                continue
            self.came, self.sends = send(sends), list(sends)
            return self.sends
        return []

    def finish(self):
        while not self.done:
            self.advance()
        return self.result


def local(
    n_dp,
    hidden_in,
    grad_out,
    lengths,
    key_mask,
    triple_weight,
    outward_weight,
    expand_weight,
    contract_weight,
    triple_master,
    triple_first,
    triple_second,
    outward_master,
    outward_first,
    outward_second,
    expand_master,
    expand_first,
    expand_second,
    contract_master,
    contract_first,
    contract_second,
    pair_bias,
    pair_first,
    pair_second,
    expand_bias,
    expand_bias_first,
    expand_bias_second,
    norm_vectors,
    vectors_first,
    vectors_second,
):
    core = lax.axis_index("tensor")
    rank = lax.axis_index("dp")

    own = pair_bias.shape[1]
    n_bias = expand_bias.shape[0]
    place = jnp.stack([core, rank]).astype(jnp.int32)
    bias_row = expand_bias[None]
    triple_other = swap(triple_weight)
    pair_other = swap(pair_bias)
    outward_other = swap(outward_weight)
    expand_here, contract_here, bias_here = behind(
        [expand_weight, contract_weight, bias_row], [triple_other, pair_other, outward_other]
    )
    bias_other = swap(bias_here)
    expand_other = swap(expand_here)
    contract_other = swap(contract_here)
    updates = {}

    def contract_then(summed):
        state = (contract_master.T, contract_first.T, contract_second.T)
        (updates["contract"],), copy = update(*summed, [state])
        return gather_flow(copy, n_dp), None

    def expand_then(summed):
        states = [
            (expand_master, expand_first, expand_second),
            (outward_master.T, outward_first.T, outward_second.T),
        ]
        (updates["expand"], updates["outward"]), copy = update(*summed, states)
        return gather_flow(copy, n_dp), None

    def triple_then(summed):
        state = (triple_master, triple_first, triple_second)
        (updates["triple"],), copy = update(*summed, [state], 3)
        return gather_flow(copy, n_dp, True), None

    qkv, probs, context, pre_one = attend(
        place, lengths, hidden_in, key_mask, triple_weight, triple_other, outward_weight,
        outward_other, pair_bias, pair_other, norm_vectors,
    )
    active, slope, layer_own, pre_two_grad, branch_grad, hidden_low, sums_two, layer_out = ffn_fwd(
        place, pre_one, grad_out, expand_weight, expand_other, contract_weight, contract_other,
        bias_row, bias_other, norm_vectors,
    )

    steps = n_bias // BLOCK_FF
    weight = partial(weight_grad, place, n_dp)
    contract_theirs = weight(branch_grad, active, steps, steps, BLOCK_FF)
    contract_mine = weight(branch_grad, active, 0, steps, BLOCK_FF, deps=(contract_theirs,))
    contract_flow = Flow(scatter_flow(contract_mine, [swap(contract_theirs)], n_dp, True), contract_then)
    sends = contract_flow.advance()
    expand_theirs, bias_theirs, hidden_sofar = ffn_bwd(
        place, n_dp, False, branch_grad, slope, expand_other, contract_other, pre_two_grad,
        pre_two_grad, hidden_low, context, norm_vectors, deps=sends,
    )
    sends = contract_flow.advance(bias_theirs)
    expand_came = swap(behind(expand_theirs, sends))
    expand_mine, bias_mine, pre_one_grad, attention_grad, sums_one, outward_theirs = ffn_bwd(
        place, n_dp, True, branch_grad, slope, expand_weight, contract_weight, hidden_sofar,
        pre_one, hidden_low, context, norm_vectors, deps=sends,
    )
    sends = contract_flow.advance(sums_one)
    outward_came = swap(behind(outward_theirs, sends))
    expand_flow = Flow(scatter_flow(expand_mine, [expand_came, outward_came], n_dp), expand_then)
    sends = sends + expand_flow.advance()
    projected_grad, sums_pair = attend_back(
        attention_grad, probs, qkv, outward_weight, outward_other, 0, lengths.shape[0] // 2,
        deps=sends,
    )
    layer_other = swap(behind(layer_own, sends))
    sends = contract_flow.advance(sums_pair)
    sends = sends + expand_flow.advance(sends)
    vectors = bundle(sums_one, sums_two, sums_pair, bias_mine, bias_theirs)
    vector_flow = Flow(total_flow(*vectors, n_dp))
    sends = sends + vector_flow.advance()
    triple_theirs = weight(hidden_in, projected_grad, 1, 1, 3 * own, deps=sends)
    sends = expand_flow.advance(triple_theirs) + vector_flow.advance(triple_theirs)
    sends = sends + contract_flow.advance(triple_theirs)
    triple_mine = weight(hidden_in, projected_grad, 0, 1, 3 * own, deps=sends)
    triple_came = swap(behind(triple_theirs, sends))
    triple_flow = Flow(scatter_flow(triple_mine, [triple_came], n_dp, True), triple_then)
    sends = triple_flow.advance()
    sends = sends + expand_flow.advance(triple_mine) + contract_flow.advance(triple_mine)
    input_own, input_grad = input_side(
        place, projected_grad, triple_weight, triple_other, pre_one_grad, deps=sends
    )
    triple_flow.advance(input_own)
    expand_flow.advance(triple_flow.sends)
    layer_out = put_other(place, layer_other, layer_out, deps=expand_flow.sends)
    contract_flow.advance(layer_out)
    triple_flow.advance(contract_flow.sends)
    expand_flow.advance(triple_flow.sends)
    vector_flow.advance(expand_flow.sends)
    input_other = swap(behind(input_own, expand_flow.sends))
    input_grad = put_other(place, input_other, input_grad, deps=expand_flow.sends)
    vector_flow.advance(input_grad)
    gather = partial(gather_place, place, n_dp)
    contract_flow.finish()
    (contract_copy,) = gather((("flip", 0, n_bias),), *contract_flow.result, deps=(input_grad,))
    triple_flow.advance(contract_copy)
    expand_flow.advance(triple_flow.sends)
    vector_flow.advance(triple_flow.sends)
    triple_flow.advance(expand_flow.sends)
    expand_flow.advance(triple_flow.sends)
    vector_sum = vector_flow.finish()
    triple_flow.advance(expand_flow.sends)
    expand_flow.finish()
    expand_copy, outward_copy = gather(
        (("plain", 0, n_bias), ("flip", n_bias, n_bias + own)),
        *expand_flow.result,
        deps=triple_flow.sends,
    )
    triple_flow.finish()
    (triple_copy,) = gather((("deep", 0, 3 * own),), *triple_flow.result, deps=(expand_copy,))
    vector_total = jnp.stack([vector_sum[i] for i in (0, 8, 1, 2, 9, 10)])
    pair_total = vector_sum[16].reshape(2, own)
    widen_total = vector_sum[17:].reshape(-1)[:n_bias]
    contract_new, expand_new = updates["contract"], updates["expand"]
    outward_new, triple_new = updates["outward"], updates["triple"]
    pair_new = adamw_step(pair_bias, pair_first, pair_second, pair_total, 0.0)
    widen_new = adamw_step(expand_bias, expand_bias_first, expand_bias_second, widen_total, 0.0)
    vectors_new = adamw_step(norm_vectors, vectors_first, vectors_second, vector_total, 0.0)
    return (
        layer_out,
        input_grad,
        triple_new[0],
        triple_new[1],
        triple_new[2],
        triple_copy,
        outward_new[0].T,
        outward_new[1].T,
        outward_new[2].T,
        outward_copy,
        expand_new[0],
        expand_new[1],
        expand_new[2],
        expand_copy,
        contract_new[0].T,
        contract_new[1].T,
        contract_new[2].T,
        contract_copy,
        pair_new[0],
        pair_new[1],
        pair_new[2],
        widen_new[0],
        widen_new[1],
        widen_new[2],
        vectors_new[0],
        vectors_new[1],
        vectors_new[2],
    )


def solution(mesh):
    matrix_specs = (
        P(None, "dp", "tensor"),
        P("tensor", "dp"),
        P("dp", "tensor"),
        P("tensor", "dp"),
    )
    copy_specs = (P(None, None, "tensor"), P("tensor", None), P(None, "tensor"), P("tensor", None))
    vector_specs = (P(None, "tensor"),) * 3 + (P("tensor"),) * 3 + (P(),) * 3
    in_specs = (
        (P("dp", None), P("dp", None), P("dp"), P("dp", None))
        + copy_specs
        + tuple(spec for spec in matrix_specs for _ in range(3))
        + vector_specs
    )
    out_specs = (P("dp", None), P("dp", None))
    for spec, copied in zip(matrix_specs, copy_specs):
        out_specs += (spec,) * 3 + (copied,)
    out_specs += vector_specs
    return jax.shard_map(
        partial(local, mesh.shape["dp"]),
        mesh=mesh,
        in_specs=in_specs,
        out_specs=out_specs,
        check_vma=False,
    )
```

```python
from functools import partial

import jax
import jax.numpy as jnp
from jax import lax
from jax.experimental import pallas as pl
from jax.experimental.pallas import tpu as pltpu
from jax.sharding import PartitionSpec as P

HEAD_DIM = 64
STEP = 7


MASK_FILL = -1e30
NORM_EPSILON = 1e-05
FIRST_DECAY = 0.5
SECOND_DECAY = 0.5
LEARN_RATE = 0.1
WEIGHT_DECAY = 0.01
EPSILON = 1e-08
LOW = jnp.bfloat16
WIDE = jnp.float32


BLOCK_FF = 512
NO_COST = pl.CostEstimate(flops=0, bytes_accessed=0, transcendentals=0)
LONG = pl.CostEstimate(flops=5 * 10**10, bytes_accessed=10**8, transcendentals=0)
VMEM = pltpu.CompilerParams(vmem_limit_bytes=64 * 2**20)
ROOT_HALF = 0.7071067811865476
BELL_TOP = 0.3989422804014327


def dot(left, right):
    return jnp.dot(left, right, preferred_element_type=WIDE)


def dot_nt(left, right):
    return lax.dot_general(left, right, (((1,), (1,)), ((), ())), preferred_element_type=WIDE)


def dot_tn(left, right):
    return lax.dot_general(left, right, (((0,), (0,)), ((), ())), preferred_element_type=WIDE)


def gelu_pair(x):
    cdf = 0.5 * lax.erf(x * ROOT_HALF) + 0.5
    return x * cdf, cdf + x * (jnp.exp(x * x * -0.5) * BELL_TOP)


def mean_rows(value):
    return jnp.mean(value, axis=-1, keepdims=True)


def norm_parts(pre):
    centred = pre - mean_rows(pre)
    inverse = lax.rsqrt(mean_rows(centred * centred) + NORM_EPSILON)
    return centred * inverse, inverse


def norm_grad(upstream, normed, inverse, gain):
    scaled = upstream * gain
    return inverse * (scaled - mean_rows(scaled) - normed * mean_rows(scaled * normed))


def col_sum(value):
    return jnp.sum(value, axis=0, keepdims=True)


def fold_rows(value):
    return jnp.sum(value.reshape(-1, 8, value.shape[1]), axis=0)


def by_rows(count, body, start, unroll=1):
    at = lambda r: pl.ds(pl.multiple_of(r * TILE, TILE), TILE)
    return lax.fori_loop(0, count // TILE, lambda r, c: body(at(r), c), start, unroll=unroll)


def lane_half(shape, e):
    lane = lax.broadcasted_iota(jnp.int32, shape, 1)
    return (lane < HEAD_DIM) if e == 0 else (lane >= HEAD_DIM)


TILE = 256


def attend_kernel(
    place, lengths, x_ref, mask_ref, w0_ref, w1_ref, o0_ref, o1_ref, p0_ref, p1_ref, nv_ref,
    qkv_ref, probs_ref, ctx_ref, pre_ref, score_s,
):
    x = x_ref[...]
    row = place[0] * pl.num_programs(0) + pl.program_id(0)
    slot = lax.broadcasted_iota(jnp.int32, (1, x.shape[0]), 1)
    present = (mask_ref[pl.ds(row, 1)] == 1) | (slot == 0)
    valid = jnp.where((slot < lengths[row]) & present, 1.0, 0.0)
    valid = jnp.broadcast_to(valid, (16, x.shape[0])).astype(LOW)
    bias = (1.0 - dot_tn(valid, jnp.full((16, 128), 0.0625, LOW))) * MASK_FILL
    width = w0_ref.shape[2]
    pairs = width // 128
    scale = jnp.asarray(HEAD_DIM ** (-0.5), LOW)
    for half, (w_ref, p_ref) in enumerate(((w0_ref, p0_ref), (w1_ref, p1_ref))):
        base = 3 * width * half
        q = dot(x, w_ref[0]) + p_ref[0:1]
        qkv_ref[:, base : base + width] = q.astype(LOW)
        qkv_ref[:, base + width : base + 2 * width] = dot(x, w_ref[1]).astype(LOW)
        v = dot(x, w_ref[2]) + p_ref[1:2]
        qkv_ref[:, base + 2 * width : base + 3 * width] = v.astype(LOW)
    for half in range(2):
        base = 3 * width * half
        for pair in range(pairs):
            at = base + 128 * pair
            kp = qkv_ref[:, at + width : at + width + 128] * scale
            for e in range(2):
                ke = jnp.where(lane_half(kp.shape, e), kp, jnp.zeros_like(kp))
                score_s[2 * pair + e] = dot_nt(ke, qkv_ref[:, at : at + 128])
        for head in range(2 * pairs):
            for left in range(0, x.shape[0], 128):
                masked = score_s[head, :, left : left + 128] + bias
                top = jnp.max(masked, axis=0, keepdims=True)
                ex = jnp.exp(masked - top)
                total = jnp.sum(ex, axis=0, keepdims=True)
                low = (ex * (1.0 / total)).astype(LOW)
                probs_ref[0, half * 2 * pairs + head, :, left : left + 128] = low
        vt = qkv_ref[:, base + 2 * width : base + 3 * width].T
        for pair in range(pairs):
            outs = []
            for e in range(2):
                low = 128 * pair + HEAD_DIM * e
                outs.append(
                    dot(vt[low : low + HEAD_DIM], probs_ref[0, half * 2 * pairs + 2 * pair + e])
                )
            ctx = jnp.concatenate(outs, axis=0).T.astype(LOW)
            ctx_ref[:, half * width + 128 * pair : half * width + 128 * pair + 128] = ctx
    attn = dot(ctx_ref[:, :width], o0_ref[...]) + dot(ctx_ref[:, width:], o1_ref[...])
    pre_ref[...] = x.astype(WIDE) + nv_ref[0:1] + attn


def attend(place, lengths, hidden_in, key_mask, w0, w1, o0, o1, p0, p1, nv):
    seqs, seq_len = key_mask.shape[0] // 2, key_mask.shape[1]
    d = hidden_in.shape[1]
    width = w0.shape[2]
    heads = 2 * width // HEAD_DIM
    tokens = seqs * seq_len
    full = lambda a: pl.BlockSpec(a.shape, lambda s, c, n: (0,) * a.ndim)
    rows = lambda cols: pl.BlockSpec((seq_len, cols), lambda s, c, n: (s, 0))
    return pl.pallas_call(
        attend_kernel,
        out_shape=(
            jax.ShapeDtypeStruct((tokens, 6 * width), LOW),
            jax.ShapeDtypeStruct((seqs, heads, seq_len, seq_len), LOW),
            jax.ShapeDtypeStruct((tokens, 2 * width), LOW),
            jax.ShapeDtypeStruct((tokens, d), WIDE),
        ),
        grid_spec=pltpu.PrefetchScalarGridSpec(
            num_scalar_prefetch=2,
            grid=(seqs,),
            in_specs=[
                pl.BlockSpec((seq_len, d), lambda s, c, n: (c[0] * seqs + s, 0)),
                *(full(a) for a in (key_mask, w0, w1, o0, o1, p0, p1, nv)),
            ],
            out_specs=[
                rows(6 * width),
                pl.BlockSpec((1, heads, seq_len, seq_len), lambda s, c, n: (s, 0, 0, 0)),
                rows(2 * width),
                rows(d),
            ],
            scratch_shapes=[pltpu.VMEM((heads // 2, seq_len, seq_len), WIDE)],
        ),
        compiler_params=VMEM,
        name="attend",
        cost_estimate=LONG,
    )(place, lengths, hidden_in, key_mask, w0, w1, o0, o1, p0, p1, nv)


ROWS = 512


def ffn_fwd_kernel(
    core, pre_ref, up_ref, e0_ref, e1_ref, c0_ref, c1_ref, b0_ref, b1_ref, nv_ref,
    act_ref, slope_ref, out_ref, grad_ref, low_ref, hl_ref, sums_ref, whole_ref,
    acc_s, wide_s,
):
    j = pl.program_id(0)
    last = pl.num_programs(0) - 1
    tokens = pre_ref.shape[0]

    @pl.when(j == 0)
    def _():
        def one(rows, _):
            normed, _ = norm_parts(pre_ref[rows])
            hidden_one = normed * nv_ref[2:3] + nv_ref[3:4]
            hl_ref[rows] = hidden_one.astype(LOW)
            acc_s[rows] = hidden_one + nv_ref[1:2]
            return 0

        by_rows(tokens, one, 0)

    def step(e_ref, c_ref, b_ref):
        for top in range(0, tokens, ROWS):
            wide_s[top : top + ROWS] = dot(hl_ref[top : top + ROWS], e_ref[...])
        for top in range(0, tokens, ROWS):
            for at in range(top, top + ROWS, 16):
                rows = slice(at, at + 16)
                act, slope = gelu_pair(wide_s[rows] + b_ref[...])
                act_ref[rows] = act.astype(LOW)
                slope_ref[rows] = slope.astype(LOW)
            acc_s[top : top + ROWS] += dot(act_ref[top : top + ROWS], c_ref[...])

    @pl.when(j < (last + 1) // 2)
    def _():
        step(e0_ref, c0_ref, b0_ref)

    @pl.when(j >= (last + 1) // 2)
    def _():
        step(e1_ref, c1_ref, b1_ref)

    @pl.when(j == last)
    def _():
        def one(rows, sums):
            normed, inverse = norm_parts(acc_s[rows])
            out = (normed * nv_ref[4:5] + nv_ref[5:6]).astype(LOW)
            out_ref[rows] = out
            whole_ref[rows] = out
            up = up_ref[rows].astype(WIDE)
            grad = norm_grad(up, normed, inverse, nv_ref[4:5])
            grad_ref[rows] = grad
            low_ref[rows] = grad.astype(LOW)
            new = (fold_rows(grad), fold_rows(up * normed), fold_rows(up))
            return tuple(a + b for a, b in zip(sums, new))

        zero = jnp.zeros((8, pre_ref.shape[1]), WIDE)
        sums = by_rows(tokens, one, (zero,) * 3, unroll=1)
        for i in range(3):
            sums_ref[i : i + 1] = col_sum(sums[i])
        sums_ref[3:8] = jnp.zeros((5, sums_ref.shape[1]), WIDE)


def ffn_fwd(core, pre, grad_out, e0, e1, c0, c1, b0, b1, nv):
    tokens, d = pre.shape
    width = e0.shape[1]
    steps = width // BLOCK_FF
    full = lambda shape: pl.BlockSpec(shape, lambda j, c: (0,) * len(shape))
    lower = lambda j: jnp.minimum(j, steps - 1)
    upper = lambda j: jnp.maximum(j - steps, 0)
    return pl.pallas_call(
        ffn_fwd_kernel,
        out_shape=(
            jax.ShapeDtypeStruct((tokens, 2 * width), LOW),
            jax.ShapeDtypeStruct((tokens, 2 * width), LOW),
            jax.ShapeDtypeStruct((tokens, d), LOW),
            jax.ShapeDtypeStruct((tokens, d), WIDE),
            jax.ShapeDtypeStruct((tokens, d), LOW),
            jax.ShapeDtypeStruct((tokens, d), LOW),
            jax.ShapeDtypeStruct((8, d), WIDE),
            jax.ShapeDtypeStruct((2 * tokens, d), LOW),
        ),
        grid_spec=pltpu.PrefetchScalarGridSpec(
            num_scalar_prefetch=1,
            grid=(2 * steps,),
            in_specs=[
                full((tokens, d)),
                pl.BlockSpec((tokens, d), lambda j, c: (c[0], 0)),
                pl.BlockSpec((d, BLOCK_FF), lambda j, c: (0, lower(j))),
                pl.BlockSpec((d, BLOCK_FF), lambda j, c: (0, upper(j))),
                pl.BlockSpec((BLOCK_FF, d), lambda j, c: (lower(j), 0)),
                pl.BlockSpec((BLOCK_FF, d), lambda j, c: (upper(j), 0)),
                pl.BlockSpec((1, BLOCK_FF), lambda j, c: (0, lower(j))),
                pl.BlockSpec((1, BLOCK_FF), lambda j, c: (0, upper(j))),
                full(nv.shape),
            ],
            out_specs=[
                pl.BlockSpec((tokens, BLOCK_FF), lambda j, c: (0, j)),
                pl.BlockSpec((tokens, BLOCK_FF), lambda j, c: (0, j)),
                full((tokens, d)),
                full((tokens, d)),
                full((tokens, d)),
                full((tokens, d)),
                full((8, d)),
                pl.BlockSpec((tokens, d), lambda j, c: (c[0], 0)),
            ],
            scratch_shapes=[pltpu.VMEM((tokens, d), WIDE), pltpu.VMEM((tokens, BLOCK_FF), WIDE)],
        ),
        compiler_params=VMEM,
        name="ffn_fwd",
        cost_estimate=LONG,
    )(core, pre, grad_out, e0, e1, c0, c1, b0, b1, nv)


def reverse(value, count):
    out = value & 0
    for bit in range(count.bit_length() - 1):
        out = out * 2 + ((value >> bit) & 1)
    return out


def spot(apart, count):
    return (apart & 3) * (count // 4) + reverse(apart >> 2, count // 4)


def place_rows(out_ref, value, rank, count, left=0):
    rows = value.shape[0] // count
    cols = slice(left, left + value.shape[1])
    if rows % 16:
        out_ref[:, cols] = value
        return
    for i in range(count):
        at = spot(jnp.bitwise_xor(rank, i), count)
        there = pl.ds(pl.multiple_of(at * rows, 16), rows)
        out_ref[there, cols] = value[i * rows : (i + 1) * rows]


def placed(grad, rank, count):
    rows = grad.shape[0] // count
    if rows % 16 == 0:
        return grad
    blocks = grad.reshape(count, rows, -1)
    apart = jnp.arange(count)
    return jnp.zeros_like(blocks).at[spot(apart ^ rank, count)].set(blocks).reshape(grad.shape)


ANY = pl.BlockSpec(memory_space=pl.ANY)


def with_deps(body, lead, inputs, deps):
    def kernel(*refs):
        body(*refs[: lead + inputs], *refs[lead + inputs + len(deps) :])

    return kernel


def weight_kernel(count, place, left_ref, right_ref, out_ref):
    place_rows(out_ref, dot_tn(left_ref[...], right_ref[...]).astype(LOW), place[1], count)


def weight_grad(place, n_dp, left, right, first, count, block, deps=()):
    tokens = right.shape[0]
    d = left.shape[1]
    halves = left.shape[0] // tokens
    out = pl.pallas_call(
        with_deps(partial(weight_kernel, n_dp), 1, 2, deps),
        out_shape=jax.ShapeDtypeStruct((d, count * block), LOW),
        grid_spec=pltpu.PrefetchScalarGridSpec(
            num_scalar_prefetch=1,
            grid=(count,),
            in_specs=[
                pl.BlockSpec((tokens, d), lambda j, c: (c[0] if halves == 2 else 0, 0)),
                pl.BlockSpec((tokens, block), lambda j, c: (0, first + j)),
            ]
            + [ANY] * len(deps),
            out_specs=pl.BlockSpec((d, block), lambda j, c: (0, j)),
        ),
        compiler_params=VMEM,
        name="weight_grad",
        cost_estimate=LONG,
    )(place, left, right, *deps)
    return placed(out, place[1], n_dp)


def ffn_bwd_kernel(
    final, n_dp, place, low_ref, slope_ref, e_ref, c_ref, sofar_ref, pre_ref, hl_ref, ctx_ref, nv_ref,
    we_ref, bias_ref, one_ref, *rest,
):
    if final:
        ag_ref, sums_ref, wo_ref, acc_s, wg_s, wide_s = rest
    else:
        acc_s, wg_s, wide_s = rest
    j = pl.program_id(0)
    last = pl.num_programs(0) - 1
    tokens = low_ref.shape[0]

    @pl.when(j == 0)
    def _():
        acc_s[...] = sofar_ref[...]

    for top in range(0, tokens, ROWS):
        wide_s[top : top + ROWS] = dot_nt(low_ref[top : top + ROWS], c_ref[...])
    bias = jnp.zeros((8, BLOCK_FF), WIDE)
    for top in range(0, tokens, ROWS):
        for at in range(top, top + ROWS, 16):
            rows = slice(at, at + 16)
            wg = (wide_s[rows] * slope_ref[rows].astype(WIDE)).astype(LOW)
            wg_s[rows] = wg
            bias = bias + fold_rows(wg.astype(WIDE))
        acc_s[top : top + ROWS] += dot_nt(wg_s[top : top + ROWS], e_ref[...])
    bias_ref[...] = col_sum(bias)
    grad = dot_tn(hl_ref[...], wg_s[...]).astype(LOW)
    if final:
        for i in range(we_ref.shape[1] // BLOCK_FF):

            @pl.when(j == i)
            def _():
                place_rows(we_ref, grad, place[1], n_dp, i * BLOCK_FF)
    else:
        place_rows(we_ref, grad, place[1], n_dp)

    @pl.when(j == last)
    def _():
        if not final:
            one_ref[...] = acc_s[...]
            return

        def one(rows, sums):
            normed, inverse = norm_parts(pre_ref[rows])
            up = acc_s[rows]
            grad = norm_grad(up, normed, inverse, nv_ref[2:3])
            one_ref[rows] = grad
            ag_ref[rows] = grad.astype(LOW)
            new = (fold_rows(grad), fold_rows(up * normed), fold_rows(up))
            return tuple(a + b for a, b in zip(sums, new))

        zero = jnp.zeros((8, pre_ref.shape[1]), WIDE)
        sums = by_rows(tokens, one, (zero,) * 3, unroll=1)
        for i in range(3):
            sums_ref[i : i + 1] = col_sum(sums[i])
        sums_ref[3:8] = jnp.zeros((5, sums_ref.shape[1]), WIDE)
        half = wo_ref.shape[1]
        grad = dot_tn(ag_ref[...], ctx_ref[:, :half]).astype(LOW)
        place_rows(we_ref, grad, place[1], n_dp, we_ref.shape[1] - half)
        place_rows(wo_ref, dot_tn(ag_ref[...], ctx_ref[:, half:]).astype(LOW), place[1], n_dp)


def ffn_bwd(place, n_dp, final, low, slope, e, c, sofar, pre, hl, ctx, nv, deps=()):
    tokens, d = low.shape
    width = e.shape[1]
    steps = width // BLOCK_FF
    first = 0 if final else steps
    full = lambda shape: pl.BlockSpec(shape, lambda j, c: (0,) * len(shape))
    half = ctx.shape[1] // 2
    if final:
        both = (d, width + half)
        outs = [(jax.ShapeDtypeStruct(both, LOW), full(both))]
    else:
        outs = [
            (jax.ShapeDtypeStruct((d, width), LOW), pl.BlockSpec((d, BLOCK_FF), lambda j, c: (0, j)))
        ]
    outs += [
        (jax.ShapeDtypeStruct((1, width), WIDE), pl.BlockSpec((1, BLOCK_FF), lambda j, c: (0, j))),
        (jax.ShapeDtypeStruct((tokens, d), WIDE), full((tokens, d))),
    ]
    if final:
        outs += [
            (jax.ShapeDtypeStruct((tokens, d), LOW), full((tokens, d))),
            (jax.ShapeDtypeStruct((8, d), WIDE), full((8, d))),
            (jax.ShapeDtypeStruct((d, half), LOW), full((d, half))),
        ]
    out = pl.pallas_call(
        with_deps(partial(ffn_bwd_kernel, final, n_dp), 1, 9, deps),
        out_shape=tuple(o[0] for o in outs),
        grid_spec=pltpu.PrefetchScalarGridSpec(
            num_scalar_prefetch=1,
            grid=(steps,),
            in_specs=[
                full((tokens, d)),
                pl.BlockSpec((tokens, BLOCK_FF), lambda j, c: (0, first + j)),
                pl.BlockSpec((d, BLOCK_FF), lambda j, c: (0, j)),
                pl.BlockSpec((BLOCK_FF, d), lambda j, c: (j, 0)),
                full((tokens, d)),
                full((tokens, d)) if final else ANY,
                full((tokens, d)),
                full(ctx.shape) if final else ANY,
                full(nv.shape),
            ]
            + [ANY] * len(deps),
            out_specs=[o[1] for o in outs],
            scratch_shapes=[
                pltpu.VMEM((tokens, d), WIDE),
                pltpu.VMEM((tokens, BLOCK_FF), LOW),
                pltpu.VMEM((tokens, BLOCK_FF), WIDE),
            ],
        ),
        compiler_params=VMEM,
        name="ffn_bwd",
        cost_estimate=LONG,
    )(place, low, slope, e, c, sofar, pre, hl, ctx, nv, *deps)
    out = list(out)
    for i in (0, 5) if final else (0,):
        out[i] = placed(out[i], place[1], n_dp)
    return out


def attend_back_kernel(
    start, ag_ref, probs_ref, qkv_ref, o0_ref, o1_ref, sofar_ref, grad_ref, sums_ref,
    dp_s, ds_s, cg_s,
):
    @pl.when(pl.program_id(0) == 0)
    def _():
        sums_ref[...] = jnp.zeros_like(sums_ref) if start else sofar_ref[...]

    width = o0_ref.shape[0]
    pairs = width // 128
    scale = jnp.asarray(HEAD_DIM ** (-0.5), LOW)
    keep = [lane_half((ag_ref.shape[0], 128), e) for e in range(2)]
    side = lambda value, e: jnp.where(keep[e], value, jnp.zeros_like(value))
    for half, o_ref in enumerate((o0_ref, o1_ref)):
        cg_s[...] = dot_nt(ag_ref[...], o_ref[...]).astype(LOW)
        first = half * 2 * pairs
        for pair in range(pairs):
            at = 3 * width * half + 128 * pair
            do = cg_s[:, 128 * pair : 128 * pair + 128]
            vp = qkv_ref[:, at + 2 * width : at + 2 * width + 128]
            for e in range(2):
                dp_s[2 * pair + e] = dot_nt(side(vp, e), do)
            dv = dot(probs_ref[0, first + 2 * pair], side(do, 0))
            dv = (dv + dot(probs_ref[0, first + 2 * pair + 1], side(do, 1))).astype(LOW)
            grad_ref[:, at + 2 * width : at + 2 * width + 128] = dv
            to = half * width + 128 * pair
            sums_ref[1:2, to : to + 128] += col_sum(dv.astype(WIDE))
        for head in range(2 * pairs):
            for left in range(0, ag_ref.shape[0], 128):
                cols = slice(left, left + 128)
                dp = dp_s[head, :, cols]
                probs = probs_ref[0, first + head, :, cols].astype(WIDE)
                inner = jnp.sum(dp * probs, axis=0, keepdims=True)
                ds_s[head, :, cols] = (probs * (dp - inner)).astype(LOW)
        for pair in range(pairs):
            at = 3 * width * half + 128 * pair
            qp = qkv_ref[:, at : at + 128] * scale
            kp = qkv_ref[:, at + width : at + width + 128] * scale
            dk = dot(ds_s[2 * pair], side(qp, 0)) + dot(ds_s[2 * pair + 1], side(qp, 1))
            dq = dot_tn(ds_s[2 * pair], side(kp, 0)) + dot_tn(ds_s[2 * pair + 1], side(kp, 1))
            dq = dq.astype(LOW)
            grad_ref[:, at : at + 128] = dq
            grad_ref[:, at + width : at + width + 128] = dk.astype(LOW)
            to = half * width + 128 * pair
            sums_ref[0:1, to : to + 128] += col_sum(dq.astype(WIDE))


def attend_back(ag, probs, qkv, o0, o1, first, count, before=None, deps=()):
    seqs, heads, seq_len, _ = probs.shape
    tokens, d = ag.shape
    width = o0.shape[0]
    full = lambda shape: pl.BlockSpec(shape, lambda s: (0,) * len(shape))
    rows = lambda cols: pl.BlockSpec((seq_len, cols), lambda s: (first + s, 0))
    sums = (8, 2 * width)
    start = before is None
    if not start:
        deps = (before[0],) + tuple(deps)
    return pl.pallas_call(
        with_deps(partial(attend_back_kernel, start), 0, 6, deps),
        out_shape=(
            jax.ShapeDtypeStruct((tokens, 6 * width), LOW),
            jax.ShapeDtypeStruct(sums, WIDE),
        ),
        grid=(count,),
        in_specs=[
            rows(d),
            pl.BlockSpec((1, heads, seq_len, seq_len), lambda s: (first + s, 0, 0, 0)),
            rows(6 * width),
            full(o0.shape),
            full(o1.shape),
            ANY if start else full(sums),
        ]
        + [ANY] * len(deps),
        out_specs=[rows(6 * width), full(sums)],
        input_output_aliases={} if start else {6: 0},
        scratch_shapes=[
            pltpu.VMEM((heads // 2, seq_len, seq_len), WIDE),
            pltpu.VMEM((heads // 2, seq_len, seq_len), LOW),
            pltpu.VMEM((seq_len, width), LOW),
        ],
        compiler_params=VMEM,
        name="attend_back",
        cost_estimate=LONG,
    )(ag, probs, qkv, o0, o1, ag if start else before[1], *deps)


def input_kernel(place, grad_ref, w0_ref, w1_ref, one_ref, out_ref, whole_ref):
    width = w0_ref.shape[2]
    total = one_ref[...]
    for i in range(6):
        w = (w0_ref, w1_ref)[i // 3][i % 3]
        total = total + dot_nt(grad_ref[:, i * width : (i + 1) * width], w)
    out_ref[...] = total.astype(LOW)
    whole_ref[...] = total.astype(LOW).astype(WIDE)


def input_side(place, grad, w0, w1, one, deps=()):
    tokens, d = one.shape
    block = min(ROWS, tokens)
    full = lambda a: pl.BlockSpec(a.shape, lambda s, c: (0,) * a.ndim)
    rows = lambda cols: pl.BlockSpec((block, cols), lambda s, c: (s, 0))
    return pl.pallas_call(
        with_deps(input_kernel, 1, 4, deps),
        out_shape=(
            jax.ShapeDtypeStruct((tokens, d), LOW),
            jax.ShapeDtypeStruct((2 * tokens, d), WIDE),
        ),
        grid_spec=pltpu.PrefetchScalarGridSpec(
            num_scalar_prefetch=1,
            grid=(tokens // block,),
            in_specs=[rows(grad.shape[1]), full(w0), full(w1), rows(d)] + [ANY] * len(deps),
            out_specs=[
                rows(d),
                pl.BlockSpec((block, d), lambda s, c: (c[0] * (tokens // block) + s, 0)),
            ],
        ),
        compiler_params=VMEM,
        name="input_side",
        cost_estimate=LONG,
    )(place, grad, w0, w1, one, *deps)


def bundle_kernel(one_ref, two_ref, pair_ref, b0_ref, b1_ref, mine_ref, theirs_ref):
    half = pair_ref.shape[1] // 2
    d = one_ref.shape[1]
    for i, (ref, b_ref) in enumerate(((mine_ref, b0_ref), (theirs_ref, b1_ref))):
        ref[...] = jnp.zeros_like(ref)
        ref[0:8] = one_ref[...]
        ref[8:16] = two_ref[...]
        for j in range(2):
            ref[16:17, j * half : (j + 1) * half] = pair_ref[j : j + 1, i * half : (i + 1) * half]
        for j in range(b_ref.shape[1] // d):
            ref[17 + j : 18 + j] = b_ref[:, j * d : (j + 1) * d]


def bundle(one, two, pair, mine, theirs, deps=()):
    out = jax.ShapeDtypeStruct((24, one.shape[1]), WIDE)
    spec = lambda a: pl.BlockSpec(a.shape, lambda: (0, 0))
    return pl.pallas_call(
        with_deps(bundle_kernel, 0, 5, deps),
        out_shape=(out, out),
        in_specs=[spec(a) for a in (one, two, pair, mine, theirs)] + [ANY] * len(deps),
        out_specs=(spec(out), spec(out)),
        name="bundle",
    )(one, two, pair, mine, theirs, *deps)


def gather_kernel(count, layout, place, z_ref, x_ref, y_ref, da_ref, db_ref, *refs):
    outs, scratch = refs[: len(layout)], list(refs[len(layout) :])
    tos = [scratch.pop(0) if kind == "flip" else out for (kind, _, _), out in zip(layout, outs)]
    block = z_ref.shape[0] // (count // 4)
    for apart in range(count):
        at = jnp.bitwise_xor(place[1], apart)
        first = reverse(apart >> 2, count // 4) * block
        ref = (z_ref, x_ref, y_ref, da_ref)[apart & 3]
        if apart & 3 == 3 and first >= da_ref.shape[0]:
            ref, first = db_ref, first - da_ref.shape[0]
        for (kind, left, right), to in zip(layout, tos):
            if kind == "deep":
                rows = block // to.shape[0]
                for i in range(to.shape[0]):
                    here = slice(first + i * rows, first + i * rows + rows)
                    to[i, pl.ds(pl.multiple_of(at * rows, 16), rows)] = ref[here]
            else:
                there = pl.ds(pl.multiple_of(at * block, 16), block)
                to[there] = ref[first : first + block, left:right]
    for (kind, _, _), out, to in zip(layout, outs, tos):
        if kind == "flip":
            out[...] = to[...].T


def gather_place(place, n_dp, layout, z, x, y, da, db, deps=()):
    rows, cols = z.shape[0] * 4, z.shape[1]
    block = rows // n_dp
    deep = [right - left for kind, left, right in layout if kind == "deep"]
    shapes = []
    for kind, left, right in layout:
        wide = right - left
        if kind == "deep":
            shapes.append((wide // cols, rows * cols // wide, cols))
        else:
            shapes.append((wide, rows) if kind == "flip" else (rows, wide))
    if (block // (shapes[0][0] if deep else 1)) % 16:
        plane = jnp.stack([z, x, y, jnp.concatenate([da, db])])
        blocks = plane.reshape(n_dp, block, cols)[spot(jnp.arange(n_dp) ^ place[1], n_dp)]
        outs = []
        for (kind, left, right), shape in zip(layout, shapes):
            if kind == "deep":
                outs.append(blocks.reshape(n_dp, shape[0], -1, cols).transpose(1, 0, 2, 3).reshape(shape))
            else:
                whole = blocks.reshape(rows, cols)[:, left:right]
                outs.append(whole.T if kind == "flip" else whole)
        return outs
    spec = lambda a: pl.BlockSpec(a.shape, lambda s, c: (0, 0))
    return pl.pallas_call(
        with_deps(partial(gather_kernel, n_dp, layout), 1, 5, deps),
        out_shape=[jax.ShapeDtypeStruct(shape, LOW) for shape in shapes],
        grid_spec=pltpu.PrefetchScalarGridSpec(
            num_scalar_prefetch=1,
            grid=(1,),
            in_specs=[spec(a) for a in (z, x, y, da, db)] + [ANY] * len(deps),
            out_specs=[pl.BlockSpec(s, lambda i, c, n=len(s): (0,) * n) for s in shapes],
            scratch_shapes=[
                pltpu.VMEM(shape[::-1], LOW)
                for (kind, _, _), shape in zip(layout, shapes)
                if kind == "flip"
            ],
        ),
        compiler_params=VMEM,
        name="gather_place",
        cost_estimate=LONG,
    )(place, z, x, y, da, db, *deps)


def combine_kernel(plan, *refs):
    outs = refs[len(refs) - len(plan) :]
    for parts, out in zip(plan, outs):
        rows = out.shape[0] // len(parts)
        for i, terms in enumerate(parts):
            sides = []
            for inputs in terms:
                pieces = [refs[r][...].astype(WIDE) for r in inputs]
                sides.append(pieces[0] if not pieces[1:] else jnp.concatenate(pieces, axis=1))
            out[i * rows : (i + 1) * rows] = sum(sides[1:], sides[0]).astype(LOW)


def cut(terms, rows):
    take = lambda a, n: a[n * rows : (n + 1) * rows].astype(WIDE)
    sides = [jnp.concatenate([take(a, n) for a, n in term], axis=1) for term in terms]
    return sum(sides[1:], sides[0])


class Blocks:
    def __init__(self, rows):
        self.rows, self.arrays, self.specs = rows, [], []

    def add(self, terms):
        plan = []
        for term in terms:
            plan.append([])
            for array, number in term:
                plan[-1].append(len(self.arrays))
                self.arrays.append(array)
                self.specs.append(
                    pl.BlockSpec((self.rows, array.shape[1]), lambda i, number=number: (number, 0))
                )
        return plan


def combine(results, rows, deps=()):
    if rows % 16:
        return [
            jnp.concatenate([cut(terms, rows) for terms in parts]).astype(LOW) for parts in results
        ]
    blocks = Blocks(rows)
    plan = [[blocks.add(terms) for terms in parts] for parts in results]
    shapes = [
        (rows * len(parts), sum(a.shape[1] for a, _ in parts[0][0])) for parts in results
    ]
    return pl.pallas_call(
        with_deps(partial(combine_kernel, plan), 0, len(blocks.arrays), deps),
        out_shape=[jax.ShapeDtypeStruct(s, LOW) for s in shapes],
        grid=(1,),
        in_specs=blocks.specs + [ANY] * len(deps),
        out_specs=[pl.BlockSpec(s, lambda i: (0, 0)) for s in shapes],
        compiler_params=VMEM,
        name="combine",
        cost_estimate=NO_COST,
    )(*blocks.arrays, *deps)


def adamw_step(master, first_moment, second_moment, gradient, decay_rate):
    first_new = FIRST_DECAY * first_moment + (1.0 - FIRST_DECAY) * gradient
    second_new = SECOND_DECAY * second_moment + (1.0 - SECOND_DECAY) * gradient * gradient
    first_fixed = first_new / (1.0 - FIRST_DECAY**STEP)
    second_fixed = second_new / (1.0 - SECOND_DECAY**STEP)
    direction = first_fixed / (jnp.sqrt(second_fixed) + EPSILON)
    master_new = master - LEARN_RATE * (direction + decay_rate * master)
    return (master_new, first_new, second_new)


def update_kernel(plan, widths, deep, *refs):
    inputs, rest = refs[: len(refs) - 6 * len(widths) - 1], refs[len(refs) - 6 * len(widths) - 1 :]
    states, outs, copy_ref = rest[: 3 * len(widths)], rest[3 * len(widths) : -1], rest[-1]
    gradient = 0.0
    for term in plan:
        pieces = [inputs[r][...].astype(WIDE) for r in term]
        gradient = gradient + (pieces[0] if not pieces[1:] else jnp.concatenate(pieces, axis=1))
    rows, at = gradient.shape[0], 0
    for i, width in enumerate(widths):
        mine, to = states[3 * i : 3 * i + 3], outs[3 * i : 3 * i + 3]
        groups = deep or 1
        for j in range(groups):
            part = gradient[:, at : at + width // groups]
            old = [ref[j] if deep else ref[...] for ref in mine]
            new = adamw_step(*old, part, WEIGHT_DECAY)
            for ref, value in zip(to, new):
                if deep:
                    ref[j] = value
                else:
                    ref[...] = value
            if deep:
                copy_ref[j * rows : (j + 1) * rows] = new[0].astype(LOW)
            else:
                copy_ref[:, at : at + width] = new[0].astype(LOW)
            at += width // groups


def update(terms, rows, states, deep=0):
    count = lambda s: s[0].shape[0] * s[0].shape[2] if deep else s[0].shape[1]
    widths = [count(s) for s in states]
    total = sum(widths)
    if rows % 16:
        gradient, at, news = cut(terms, rows), 0, []
        for state, width in zip(states, widths):
            part = gradient[:, at : at + width]
            if deep:
                part = jnp.stack(jnp.split(part, deep, axis=1))
            news.append(adamw_step(*state, part, WEIGHT_DECAY))
            at += width
        copies = [n[0].astype(LOW) for n in news]
        if deep:
            return news, copies[0].reshape(-1, copies[0].shape[2])
        return news, jnp.concatenate(copies, axis=1)
    blocks = Blocks(rows)
    plan = blocks.add(terms)
    spec = lambda a: pl.BlockSpec(a.shape, lambda i: (0,) * a.ndim)
    flat = [a for state in states for a in state]
    copy = jax.ShapeDtypeStruct((rows * deep, total // deep) if deep else (rows, total), LOW)
    outs = [jax.ShapeDtypeStruct(a.shape, WIDE) for a in flat] + [copy]
    out = pl.pallas_call(
        partial(update_kernel, plan, widths, deep),
        out_shape=outs,
        grid=(1,),
        in_specs=blocks.specs + [spec(a) for a in flat],
        out_specs=[spec(a) for a in outs],
        compiler_params=VMEM,
        name="update",
        cost_estimate=NO_COST,
    )(*blocks.arrays, *flat)
    return [out[3 * i : 3 * i + 3] for i in range(len(states))], out[-1]


def put_kernel(place, other_ref, whole_ref, out_ref):
    out_ref[...] = other_ref[...].astype(out_ref.dtype)


def put_other(place, other, whole, deps=()):
    tokens, d = other.shape
    return pl.pallas_call(
        with_deps(put_kernel, 1, 2, deps),
        out_shape=jax.ShapeDtypeStruct(whole.shape, whole.dtype),
        grid_spec=pltpu.PrefetchScalarGridSpec(
            num_scalar_prefetch=1,
            grid=(1,),
            in_specs=[pl.BlockSpec((tokens, d), lambda s, c: (0, 0)), ANY] + [ANY] * len(deps),
            out_specs=pl.BlockSpec((tokens, d), lambda s, c: (1 - c[0], 0)),
        ),
        input_output_aliases={2: 0},
        compiler_params=VMEM,
        name="put_other",
        cost_estimate=LONG,
    )(place, other, whole, *deps)


def swap(value):
    return lax.ppermute(value, "tensor", [(0, 1), (1, 0)])


def across(value, apart, count):
    return lax.ppermute(value, "dp", [(i, i ^ apart) for i in range(count)])


def far_digits(count, direct):
    weights = [1 << bit for bit in range(2, count.bit_length() - 1)]
    size = 2 if direct else 1
    return [weights[i : i + size] for i in range(0, len(weights), size)]


def distances(digit):
    out = [0]
    for weight in digit:
        out = [d + e for d in out for e in (0, weight)]
    return out


def scatter_flow(mine, came, count, direct=False):
    rows, width = mine.shape
    block = rows // 8

    def part(y, x, half):
        at = (y * 2 + x) * 2 + half
        return [[(mine, at)], [(c, at) for c in came]]

    to_x, to_y = combine(
        [[part(0, 1, 0), part(1, 1, 0)], [part(1, 0, 1), part(1, 1, 1)]], block
    )
    send_both = lambda v: [across(v[0], 1, count), across(v[1], 2, count)]
    from_x, from_y = yield [to_x, to_y], send_both
    to_y, to_x = combine(
        [[part(1, 0, 0) + [[(from_x, 1)]]], [part(0, 1, 1) + [[(from_y, 1)]]]], block
    )
    last_x, last_y = yield [to_x, to_y], send_both
    upper = part(0, 0, 0) + [[(from_x, 0)], [(last_y, 0)]]
    lower = part(0, 0, 1) + [[(from_y, 0)], [(last_x, 0)]]

    half = block
    terms = None
    for digit in far_digits(count, direct):
        apart = distances(digit)
        if terms is None:
            half = half * 2 // len(apart)
            pieces = [upper, lower]
            if len(apart) == 4:
                pieces = [divide(p, 2, i) for p in pieces for i in range(2)]
        else:
            half = half // len(apart)
            pieces = [divide(terms, len(apart), i) for i in range(len(apart))]
        sends = combine([[piece] for piece in pieces[1:]], half)
        came = yield (
            sends,
            lambda v, apart=apart: [across(p, d, count) for p, d in zip(v, apart[1:])],
        )
        terms = pieces[0] + [[(c, 0)] for c in came]
    return terms, half


def divide(terms, members, number):
    return [[(a, n * members + number) for a, n in term] for term in terms]


def gather_flow(shard, count, direct=False):
    held = shard
    for digit in reversed(far_digits(count, direct)):
        apart = distances(digit)
        came = yield (
            [held],
            lambda v, apart=apart: [across(v[0], d, count) for d in apart[1:]],
        )
        (held,) = combine([[[[(h, 0)]] for h in [held] + list(came)]], held.shape[0])
    half = held.shape[0] // 2
    x, y = yield [held], lambda v: [across(v[0], 1, count), across(v[0], 2, count)]
    upper, lower = combine([[[[(x, 0)]]], [[[(y, 1)]]]], half)
    both = yield [upper, lower], lambda v: [across(v[0], 2, count), across(v[1], 1, count)]
    return held, x, y, both[0], both[1]


def total_flow(mine, others, count):
    (came,) = yield [others], lambda v: [swap(v[0])]
    total = mine + came
    apart = 1
    while apart < count:
        (came,) = yield [total], lambda v, apart=apart: [across(v[0], apart, count)]
        total = total + came
        apart *= 2
    return total


def behind(value, after):
    return lax.optimization_barrier((value, after))[0]


class Flow:
    def __init__(self, steps, then=None):
        self.steps, self.then = steps, then
        self.came, self.result, self.done = None, None, False
        self.sends = ()

    def advance(self, after=None):
        if after is not None and self.came is not None:
            self.came = behind(list(self.came), after)
        while not self.done:
            try:
                sends, send = self.steps.send(self.came)
            except StopIteration as stop:
                if self.then is None:
                    self.result, self.done = stop.value, True
                    return []
                self.steps, self.then = self.then(stop.value)
                self.came = None
                continue
            self.came, self.sends = send(sends), list(sends)
            return self.sends
        return []

    def finish(self):
        while not self.done:
            self.advance()
        return self.result


def local(
    n_dp,
    hidden_in,
    grad_out,
    lengths,
    key_mask,
    triple_weight,
    outward_weight,
    expand_weight,
    contract_weight,
    triple_master,
    triple_first,
    triple_second,
    outward_master,
    outward_first,
    outward_second,
    expand_master,
    expand_first,
    expand_second,
    contract_master,
    contract_first,
    contract_second,
    pair_bias,
    pair_first,
    pair_second,
    expand_bias,
    expand_bias_first,
    expand_bias_second,
    norm_vectors,
    vectors_first,
    vectors_second,
):
    core = lax.axis_index("tensor")
    rank = lax.axis_index("dp")

    own = pair_bias.shape[1]
    n_bias = expand_bias.shape[0]
    place = jnp.stack([core, rank]).astype(jnp.int32)
    bias_row = expand_bias[None]
    triple_other = swap(triple_weight)
    pair_other = swap(pair_bias)
    outward_other = swap(outward_weight)
    expand_here, contract_here, bias_here = behind(
        [expand_weight, contract_weight, bias_row], [triple_other, pair_other, outward_other]
    )
    bias_other = swap(bias_here)
    expand_other = swap(expand_here)
    contract_other = swap(contract_here)
    updates = {}

    def contract_then(summed):
        state = (contract_master.T, contract_first.T, contract_second.T)
        (updates["contract"],), copy = update(*summed, [state])
        return gather_flow(copy, n_dp), None

    def expand_then(summed):
        states = [
            (expand_master, expand_first, expand_second),
            (outward_master.T, outward_first.T, outward_second.T),
        ]
        (updates["expand"], updates["outward"]), copy = update(*summed, states)
        return gather_flow(copy, n_dp), None

    def triple_then(summed):
        state = (triple_master, triple_first, triple_second)
        (updates["triple"],), copy = update(*summed, [state], 3)
        return gather_flow(copy, n_dp), None

    qkv, probs, context, pre_one = attend(
        place, lengths, hidden_in, key_mask, triple_weight, triple_other, outward_weight,
        outward_other, pair_bias, pair_other, norm_vectors,
    )
    active, slope, layer_own, pre_two_grad, branch_grad, hidden_low, sums_two, layer_out = ffn_fwd(
        place, pre_one, grad_out, expand_weight, expand_other, contract_weight, contract_other,
        bias_row, bias_other, norm_vectors,
    )

    steps = n_bias // BLOCK_FF
    weight = partial(weight_grad, place, n_dp)
    contract_theirs = weight(branch_grad, active, steps, steps, BLOCK_FF)
    contract_mine = weight(branch_grad, active, 0, steps, BLOCK_FF, deps=(contract_theirs,))
    contract_flow = Flow(scatter_flow(contract_mine, [swap(contract_theirs)], n_dp, True), contract_then)
    sends = contract_flow.advance()
    expand_theirs, bias_theirs, hidden_sofar = ffn_bwd(
        place, n_dp, False, branch_grad, slope, expand_other, contract_other, pre_two_grad,
        pre_two_grad, hidden_low, context, norm_vectors, deps=sends,
    )
    sends = contract_flow.advance(bias_theirs)
    expand_came = swap(behind(expand_theirs, sends))
    expand_mine, bias_mine, pre_one_grad, attention_grad, sums_one, outward_theirs = ffn_bwd(
        place, n_dp, True, branch_grad, slope, expand_weight, contract_weight, hidden_sofar,
        pre_one, hidden_low, context, norm_vectors, deps=sends,
    )
    sends = contract_flow.advance(sums_one)
    outward_came = swap(behind(outward_theirs, sends))
    expand_flow = Flow(scatter_flow(expand_mine, [expand_came, outward_came], n_dp), expand_then)
    sends = sends + expand_flow.advance()
    projected_grad, sums_pair = attend_back(
        attention_grad, probs, qkv, outward_weight, outward_other, 0, lengths.shape[0] // 2,
        deps=sends,
    )
    layer_other = swap(behind(layer_own, sends))
    sends = contract_flow.advance(sums_pair)
    sends = sends + expand_flow.advance(sends)
    vectors = bundle(sums_one, sums_two, sums_pair, bias_mine, bias_theirs)
    vector_flow = Flow(total_flow(*vectors, n_dp))
    sends = sends + vector_flow.advance()
    triple_theirs = weight(hidden_in, projected_grad, 1, 1, 3 * own, deps=sends)
    sends = expand_flow.advance(triple_theirs) + vector_flow.advance(triple_theirs)
    sends = sends + contract_flow.advance(triple_theirs)
    triple_mine = weight(hidden_in, projected_grad, 0, 1, 3 * own, deps=sends)
    triple_came = swap(behind(triple_theirs, sends))
    triple_flow = Flow(scatter_flow(triple_mine, [triple_came], n_dp, True), triple_then)
    sends = triple_flow.advance()
    sends = sends + expand_flow.advance(triple_mine) + contract_flow.advance(triple_mine)
    input_own, input_grad = input_side(
        place, projected_grad, triple_weight, triple_other, pre_one_grad, deps=sends
    )
    triple_flow.advance(input_own)
    expand_flow.advance(triple_flow.sends)
    vector_flow.advance(triple_flow.sends)
    layer_out = put_other(place, layer_other, layer_out, deps=expand_flow.sends + vector_flow.sends)
    contract_flow.advance(layer_out)
    triple_flow.advance(contract_flow.sends)
    expand_flow.advance(triple_flow.sends)
    vector_flow.advance(expand_flow.sends)
    input_other = swap(behind(input_own, expand_flow.sends))
    input_grad = put_other(
        place, input_other, input_grad, deps=expand_flow.sends + vector_flow.sends
    )
    gather = partial(gather_place, place, n_dp)
    triple_flow.advance(input_grad)
    expand_flow.advance(triple_flow.sends)
    vector_flow.advance(input_grad)
    triple_flow.advance(expand_flow.sends)
    contract_flow.finish()
    (contract_copy,) = gather(
        (("flip", 0, n_bias),),
        *contract_flow.result,
        deps=triple_flow.sends + expand_flow.sends + vector_flow.sends,
    )
    triple_flow.advance(contract_copy)
    vector_flow.advance(contract_copy)
    expand_flow.advance(triple_flow.sends)
    triple_flow.advance(expand_flow.sends)
    expand_flow.finish()
    expand_copy, outward_copy = gather(
        (("plain", 0, n_bias), ("flip", n_bias, n_bias + own)),
        *expand_flow.result,
        deps=triple_flow.sends + vector_flow.sends,
    )
    vector_sum = vector_flow.finish()
    triple_flow.finish()
    (triple_copy,) = gather((("deep", 0, 3 * own),), *triple_flow.result, deps=(expand_copy,))
    vector_total = jnp.stack([vector_sum[i] for i in (0, 8, 1, 2, 9, 10)])
    pair_total = vector_sum[16].reshape(2, own)
    widen_total = vector_sum[17:].reshape(-1)[:n_bias]
    contract_new, expand_new = updates["contract"], updates["expand"]
    outward_new, triple_new = updates["outward"], updates["triple"]
    pair_new = adamw_step(pair_bias, pair_first, pair_second, pair_total, 0.0)
    widen_new = adamw_step(expand_bias, expand_bias_first, expand_bias_second, widen_total, 0.0)
    vectors_new = adamw_step(norm_vectors, vectors_first, vectors_second, vector_total, 0.0)
    return (
        layer_out,
        input_grad,
        triple_new[0],
        triple_new[1],
        triple_new[2],
        triple_copy,
        outward_new[0].T,
        outward_new[1].T,
        outward_new[2].T,
        outward_copy,
        expand_new[0],
        expand_new[1],
        expand_new[2],
        expand_copy,
        contract_new[0].T,
        contract_new[1].T,
        contract_new[2].T,
        contract_copy,
        pair_new[0],
        pair_new[1],
        pair_new[2],
        widen_new[0],
        widen_new[1],
        widen_new[2],
        vectors_new[0],
        vectors_new[1],
        vectors_new[2],
    )


def solution(mesh):
    matrix_specs = (
        P(None, "dp", "tensor"),
        P("tensor", "dp"),
        P("dp", "tensor"),
        P("tensor", "dp"),
    )
    copy_specs = (P(None, None, "tensor"), P("tensor", None), P(None, "tensor"), P("tensor", None))
    vector_specs = (P(None, "tensor"),) * 3 + (P("tensor"),) * 3 + (P(),) * 3
    in_specs = (
        (P("dp", None), P("dp", None), P("dp"), P("dp", None))
        + copy_specs
        + tuple(spec for spec in matrix_specs for _ in range(3))
        + vector_specs
    )
    out_specs = (P("dp", None), P("dp", None))
    for spec, copied in zip(matrix_specs, copy_specs):
        out_specs += (spec,) * 3 + (copied,)
    out_specs += vector_specs
    return jax.shard_map(
        partial(local, mesh.shape["dp"]),
        mesh=mesh,
        in_specs=in_specs,
        out_specs=out_specs,
        check_vma=False,
    )
```

```python
from functools import partial

import jax
import jax.numpy as jnp
from jax import lax
from jax.experimental import pallas as pl
from jax.experimental.pallas import tpu as pltpu
from jax.sharding import PartitionSpec as P

HEAD_DIM = 64
STEP = 7


MASK_FILL = -1e30
NORM_EPSILON = 1e-05
FIRST_DECAY = 0.5
SECOND_DECAY = 0.5
LEARN_RATE = 0.1
WEIGHT_DECAY = 0.01
EPSILON = 1e-08
LOW = jnp.bfloat16
WIDE = jnp.float32


BLOCK_FF = 512
NO_COST = pl.CostEstimate(flops=0, bytes_accessed=0, transcendentals=0)
LONG = pl.CostEstimate(flops=5 * 10**10, bytes_accessed=10**8, transcendentals=0)
VMEM = pltpu.CompilerParams(vmem_limit_bytes=64 * 2**20)
ROOT_HALF = 0.7071067811865476
BELL_TOP = 0.3989422804014327


def dot(left, right):
    return jnp.dot(left, right, preferred_element_type=WIDE)


def dot_nt(left, right):
    return lax.dot_general(left, right, (((1,), (1,)), ((), ())), preferred_element_type=WIDE)


def dot_tn(left, right):
    return lax.dot_general(left, right, (((0,), (0,)), ((), ())), preferred_element_type=WIDE)


def gelu_pair(x):
    cdf = 0.5 * lax.erf(x * ROOT_HALF) + 0.5
    return x * cdf, cdf + x * (jnp.exp(x * x * -0.5) * BELL_TOP)


def mean_rows(value):
    return jnp.mean(value, axis=-1, keepdims=True)


def norm_parts(pre):
    centred = pre - mean_rows(pre)
    inverse = lax.rsqrt(mean_rows(centred * centred) + NORM_EPSILON)
    return centred * inverse, inverse


def norm_grad(upstream, normed, inverse, gain):
    scaled = upstream * gain
    return inverse * (scaled - mean_rows(scaled) - normed * mean_rows(scaled * normed))


def col_sum(value):
    return jnp.sum(value, axis=0, keepdims=True)


def fold_rows(value):
    return jnp.sum(value.reshape(-1, 8, value.shape[1]), axis=0)


def by_rows(count, body, start, unroll=1):
    at = lambda r: pl.ds(pl.multiple_of(r * TILE, TILE), TILE)
    return lax.fori_loop(0, count // TILE, lambda r, c: body(at(r), c), start, unroll=unroll)


def lane_half(shape, e):
    lane = lax.broadcasted_iota(jnp.int32, shape, 1)
    return (lane < HEAD_DIM) if e == 0 else (lane >= HEAD_DIM)


TILE = 256


def attend_kernel(
    place, lengths, x_ref, mask_ref, w0_ref, w1_ref, o0_ref, o1_ref, p0_ref, p1_ref, nv_ref,
    qkv_ref, probs_ref, ctx_ref, pre_ref, score_s,
):
    x = x_ref[...]
    row = place[0] * pl.num_programs(0) + pl.program_id(0)
    slot = lax.broadcasted_iota(jnp.int32, (1, x.shape[0]), 1)
    present = (mask_ref[pl.ds(row, 1)] == 1) | (slot == 0)
    valid = jnp.where((slot < lengths[row]) & present, 1.0, 0.0)
    valid = jnp.broadcast_to(valid, (16, x.shape[0])).astype(LOW)
    bias = (1.0 - dot_tn(valid, jnp.full((16, 128), 0.0625, LOW))) * MASK_FILL
    width = w0_ref.shape[2]
    pairs = width // 128
    scale = jnp.asarray(HEAD_DIM ** (-0.5), LOW)
    for half, (w_ref, p_ref) in enumerate(((w0_ref, p0_ref), (w1_ref, p1_ref))):
        base = 3 * width * half
        q = dot(x, w_ref[0]) + p_ref[0:1]
        qkv_ref[:, base : base + width] = q.astype(LOW)
        qkv_ref[:, base + width : base + 2 * width] = dot(x, w_ref[1]).astype(LOW)
        v = dot(x, w_ref[2]) + p_ref[1:2]
        qkv_ref[:, base + 2 * width : base + 3 * width] = v.astype(LOW)
    for half in range(2):
        base = 3 * width * half
        for pair in range(pairs):
            at = base + 128 * pair
            kp = qkv_ref[:, at + width : at + width + 128] * scale
            for e in range(2):
                ke = jnp.where(lane_half(kp.shape, e), kp, jnp.zeros_like(kp))
                score_s[2 * pair + e] = dot_nt(ke, qkv_ref[:, at : at + 128])
        for head in range(2 * pairs):
            for left in range(0, x.shape[0], 128):
                masked = score_s[head, :, left : left + 128] + bias
                top = jnp.max(masked, axis=0, keepdims=True)
                ex = jnp.exp(masked - top)
                total = jnp.sum(ex, axis=0, keepdims=True)
                low = (ex * (1.0 / total)).astype(LOW)
                probs_ref[0, half * 2 * pairs + head, :, left : left + 128] = low
        vt = qkv_ref[:, base + 2 * width : base + 3 * width].T
        for pair in range(pairs):
            outs = []
            for e in range(2):
                low = 128 * pair + HEAD_DIM * e
                outs.append(
                    dot(vt[low : low + HEAD_DIM], probs_ref[0, half * 2 * pairs + 2 * pair + e])
                )
            ctx = jnp.concatenate(outs, axis=0).T.astype(LOW)
            ctx_ref[:, half * width + 128 * pair : half * width + 128 * pair + 128] = ctx
    attn = dot(ctx_ref[:, :width], o0_ref[...]) + dot(ctx_ref[:, width:], o1_ref[...])
    pre_ref[...] = x.astype(WIDE) + nv_ref[0:1] + attn


def attend(place, lengths, hidden_in, key_mask, w0, w1, o0, o1, p0, p1, nv):
    seqs, seq_len = key_mask.shape[0] // 2, key_mask.shape[1]
    d = hidden_in.shape[1]
    width = w0.shape[2]
    heads = 2 * width // HEAD_DIM
    tokens = seqs * seq_len
    full = lambda a: pl.BlockSpec(a.shape, lambda s, c, n: (0,) * a.ndim)
    rows = lambda cols: pl.BlockSpec((seq_len, cols), lambda s, c, n: (s, 0))
    return pl.pallas_call(
        attend_kernel,
        out_shape=(
            jax.ShapeDtypeStruct((tokens, 6 * width), LOW),
            jax.ShapeDtypeStruct((seqs, heads, seq_len, seq_len), LOW),
            jax.ShapeDtypeStruct((tokens, 2 * width), LOW),
            jax.ShapeDtypeStruct((tokens, d), WIDE),
        ),
        grid_spec=pltpu.PrefetchScalarGridSpec(
            num_scalar_prefetch=2,
            grid=(seqs,),
            in_specs=[
                pl.BlockSpec((seq_len, d), lambda s, c, n: (c[0] * seqs + s, 0)),
                *(full(a) for a in (key_mask, w0, w1, o0, o1, p0, p1, nv)),
            ],
            out_specs=[
                rows(6 * width),
                pl.BlockSpec((1, heads, seq_len, seq_len), lambda s, c, n: (s, 0, 0, 0)),
                rows(2 * width),
                rows(d),
            ],
            scratch_shapes=[pltpu.VMEM((heads // 2, seq_len, seq_len), WIDE)],
        ),
        compiler_params=VMEM,
        name="attend",
        cost_estimate=LONG,
    )(place, lengths, hidden_in, key_mask, w0, w1, o0, o1, p0, p1, nv)


ROWS = 512


def ffn_fwd_kernel(
    core, pre_ref, up_ref, e0_ref, e1_ref, c0_ref, c1_ref, b0_ref, b1_ref, nv_ref,
    act_ref, slope_ref, out_ref, grad_ref, low_ref, hl_ref, sums_ref, whole_ref,
    acc_s, wide_s,
):
    j = pl.program_id(0)
    last = pl.num_programs(0) - 1
    tokens = pre_ref.shape[0]

    @pl.when(j == 0)
    def _():
        def one(rows, _):
            normed, _ = norm_parts(pre_ref[rows])
            hidden_one = normed * nv_ref[2:3] + nv_ref[3:4]
            hl_ref[rows] = hidden_one.astype(LOW)
            acc_s[rows] = hidden_one + nv_ref[1:2]
            return 0

        by_rows(tokens, one, 0)

    def step(e_ref, c_ref, b_ref):
        for top in range(0, tokens, ROWS):
            wide_s[top : top + ROWS] = dot(hl_ref[top : top + ROWS], e_ref[...])
        for top in range(0, tokens, ROWS):
            for at in range(top, top + ROWS, 16):
                rows = slice(at, at + 16)
                act, slope = gelu_pair(wide_s[rows] + b_ref[...])
                act_ref[rows] = act.astype(LOW)
                slope_ref[rows] = slope.astype(LOW)
            acc_s[top : top + ROWS] += dot(act_ref[top : top + ROWS], c_ref[...])

    @pl.when(j < (last + 1) // 2)
    def _():
        step(e0_ref, c0_ref, b0_ref)

    @pl.when(j >= (last + 1) // 2)
    def _():
        step(e1_ref, c1_ref, b1_ref)

    @pl.when(j == last)
    def _():
        def one(rows, sums):
            normed, inverse = norm_parts(acc_s[rows])
            out = (normed * nv_ref[4:5] + nv_ref[5:6]).astype(LOW)
            out_ref[rows] = out
            whole_ref[rows] = out
            up = up_ref[rows].astype(WIDE)
            grad = norm_grad(up, normed, inverse, nv_ref[4:5])
            grad_ref[rows] = grad
            low_ref[rows] = grad.astype(LOW)
            new = (fold_rows(grad), fold_rows(up * normed), fold_rows(up))
            return tuple(a + b for a, b in zip(sums, new))

        zero = jnp.zeros((8, pre_ref.shape[1]), WIDE)
        sums = by_rows(tokens, one, (zero,) * 3, unroll=1)
        for i in range(3):
            sums_ref[i : i + 1] = col_sum(sums[i])
        sums_ref[3:8] = jnp.zeros((5, sums_ref.shape[1]), WIDE)


def ffn_fwd(core, pre, grad_out, e0, e1, c0, c1, b0, b1, nv):
    tokens, d = pre.shape
    width = e0.shape[1]
    steps = width // BLOCK_FF
    full = lambda shape: pl.BlockSpec(shape, lambda j, c: (0,) * len(shape))
    lower = lambda j: jnp.minimum(j, steps - 1)
    upper = lambda j: jnp.maximum(j - steps, 0)
    return pl.pallas_call(
        ffn_fwd_kernel,
        out_shape=(
            jax.ShapeDtypeStruct((tokens, 2 * width), LOW),
            jax.ShapeDtypeStruct((tokens, 2 * width), LOW),
            jax.ShapeDtypeStruct((tokens, d), LOW),
            jax.ShapeDtypeStruct((tokens, d), WIDE),
            jax.ShapeDtypeStruct((tokens, d), LOW),
            jax.ShapeDtypeStruct((tokens, d), LOW),
            jax.ShapeDtypeStruct((8, d), WIDE),
            jax.ShapeDtypeStruct((2 * tokens, d), LOW),
        ),
        grid_spec=pltpu.PrefetchScalarGridSpec(
            num_scalar_prefetch=1,
            grid=(2 * steps,),
            in_specs=[
                full((tokens, d)),
                pl.BlockSpec((tokens, d), lambda j, c: (c[0], 0)),
                pl.BlockSpec((d, BLOCK_FF), lambda j, c: (0, lower(j))),
                pl.BlockSpec((d, BLOCK_FF), lambda j, c: (0, upper(j))),
                pl.BlockSpec((BLOCK_FF, d), lambda j, c: (lower(j), 0)),
                pl.BlockSpec((BLOCK_FF, d), lambda j, c: (upper(j), 0)),
                pl.BlockSpec((1, BLOCK_FF), lambda j, c: (0, lower(j))),
                pl.BlockSpec((1, BLOCK_FF), lambda j, c: (0, upper(j))),
                full(nv.shape),
            ],
            out_specs=[
                pl.BlockSpec((tokens, BLOCK_FF), lambda j, c: (0, j)),
                pl.BlockSpec((tokens, BLOCK_FF), lambda j, c: (0, j)),
                full((tokens, d)),
                full((tokens, d)),
                full((tokens, d)),
                full((tokens, d)),
                full((8, d)),
                pl.BlockSpec((tokens, d), lambda j, c: (c[0], 0)),
            ],
            scratch_shapes=[pltpu.VMEM((tokens, d), WIDE), pltpu.VMEM((tokens, BLOCK_FF), WIDE)],
        ),
        compiler_params=VMEM,
        name="ffn_fwd",
        cost_estimate=LONG,
    )(core, pre, grad_out, e0, e1, c0, c1, b0, b1, nv)


def reverse(value, count):
    out = value & 0
    for bit in range(count.bit_length() - 1):
        out = out * 2 + ((value >> bit) & 1)
    return out


def spot(apart, count):
    return (apart & 3) * (count // 4) + reverse(apart >> 2, count // 4)


def place_rows(out_ref, value, rank, count, left=0):
    rows = value.shape[0] // count
    cols = slice(left, left + value.shape[1])
    if rows % 16:
        out_ref[:, cols] = value
        return
    for i in range(count):
        at = spot(jnp.bitwise_xor(rank, i), count)
        there = pl.ds(pl.multiple_of(at * rows, 16), rows)
        out_ref[there, cols] = value[i * rows : (i + 1) * rows]


def placed(grad, rank, count):
    rows = grad.shape[0] // count
    if rows % 16 == 0:
        return grad
    blocks = grad.reshape(count, rows, -1)
    apart = jnp.arange(count)
    return jnp.zeros_like(blocks).at[spot(apart ^ rank, count)].set(blocks).reshape(grad.shape)


ANY = pl.BlockSpec(memory_space=pl.ANY)


def with_deps(body, lead, inputs, deps):
    def kernel(*refs):
        body(*refs[: lead + inputs], *refs[lead + inputs + len(deps) :])

    return kernel


def weight_kernel(count, place, left_ref, right_ref, out_ref):
    place_rows(out_ref, dot_tn(left_ref[...], right_ref[...]).astype(LOW), place[1], count)


def weight_grad(place, n_dp, left, right, first, count, block, deps=()):
    tokens = right.shape[0]
    d = left.shape[1]
    halves = left.shape[0] // tokens
    out = pl.pallas_call(
        with_deps(partial(weight_kernel, n_dp), 1, 2, deps),
        out_shape=jax.ShapeDtypeStruct((d, count * block), LOW),
        grid_spec=pltpu.PrefetchScalarGridSpec(
            num_scalar_prefetch=1,
            grid=(count,),
            in_specs=[
                pl.BlockSpec((tokens, d), lambda j, c: (c[0] if halves == 2 else 0, 0)),
                pl.BlockSpec((tokens, block), lambda j, c: (0, first + j)),
            ]
            + [ANY] * len(deps),
            out_specs=pl.BlockSpec((d, block), lambda j, c: (0, j)),
        ),
        compiler_params=VMEM,
        name="weight_grad",
        cost_estimate=LONG,
    )(place, left, right, *deps)
    return placed(out, place[1], n_dp)


def ffn_bwd_kernel(
    final, n_dp, place, low_ref, slope_ref, e_ref, c_ref, sofar_ref, pre_ref, hl_ref, ctx_ref, nv_ref,
    we_ref, bias_ref, one_ref, *rest,
):
    if final:
        ag_ref, sums_ref, wo_ref, acc_s, wg_s, wide_s = rest
    else:
        acc_s, wg_s, wide_s = rest
    j = pl.program_id(0)
    last = pl.num_programs(0) - 1
    tokens = low_ref.shape[0]

    @pl.when(j == 0)
    def _():
        acc_s[...] = sofar_ref[...]

    for top in range(0, tokens, ROWS):
        wide_s[top : top + ROWS] = dot_nt(low_ref[top : top + ROWS], c_ref[...])
    bias = jnp.zeros((8, BLOCK_FF), WIDE)
    for top in range(0, tokens, ROWS):
        for at in range(top, top + ROWS, 16):
            rows = slice(at, at + 16)
            wg = (wide_s[rows] * slope_ref[rows].astype(WIDE)).astype(LOW)
            wg_s[rows] = wg
            bias = bias + fold_rows(wg.astype(WIDE))
        acc_s[top : top + ROWS] += dot_nt(wg_s[top : top + ROWS], e_ref[...])
    bias_ref[...] = col_sum(bias)
    grad = dot_tn(hl_ref[...], wg_s[...]).astype(LOW)
    if final:
        for i in range(we_ref.shape[1] // BLOCK_FF):

            @pl.when(j == i)
            def _():
                place_rows(we_ref, grad, place[1], n_dp, i * BLOCK_FF)
    else:
        place_rows(we_ref, grad, place[1], n_dp)

    @pl.when(j == last)
    def _():
        if not final:
            one_ref[...] = acc_s[...]
            return

        def one(rows, sums):
            normed, inverse = norm_parts(pre_ref[rows])
            up = acc_s[rows]
            grad = norm_grad(up, normed, inverse, nv_ref[2:3])
            one_ref[rows] = grad
            ag_ref[rows] = grad.astype(LOW)
            new = (fold_rows(grad), fold_rows(up * normed), fold_rows(up))
            return tuple(a + b for a, b in zip(sums, new))

        zero = jnp.zeros((8, pre_ref.shape[1]), WIDE)
        sums = by_rows(tokens, one, (zero,) * 3, unroll=1)
        for i in range(3):
            sums_ref[i : i + 1] = col_sum(sums[i])
        sums_ref[3:8] = jnp.zeros((5, sums_ref.shape[1]), WIDE)
        half = wo_ref.shape[1]
        grad = dot_tn(ag_ref[...], ctx_ref[:, :half]).astype(LOW)
        place_rows(we_ref, grad, place[1], n_dp, we_ref.shape[1] - half)
        place_rows(wo_ref, dot_tn(ag_ref[...], ctx_ref[:, half:]).astype(LOW), place[1], n_dp)


def ffn_bwd(place, n_dp, final, low, slope, e, c, sofar, pre, hl, ctx, nv, deps=()):
    tokens, d = low.shape
    width = e.shape[1]
    steps = width // BLOCK_FF
    first = 0 if final else steps
    full = lambda shape: pl.BlockSpec(shape, lambda j, c: (0,) * len(shape))
    half = ctx.shape[1] // 2
    if final:
        both = (d, width + half)
        outs = [(jax.ShapeDtypeStruct(both, LOW), full(both))]
    else:
        outs = [
            (jax.ShapeDtypeStruct((d, width), LOW), pl.BlockSpec((d, BLOCK_FF), lambda j, c: (0, j)))
        ]
    outs += [
        (jax.ShapeDtypeStruct((1, width), WIDE), pl.BlockSpec((1, BLOCK_FF), lambda j, c: (0, j))),
        (jax.ShapeDtypeStruct((tokens, d), WIDE), full((tokens, d))),
    ]
    if final:
        outs += [
            (jax.ShapeDtypeStruct((tokens, d), LOW), full((tokens, d))),
            (jax.ShapeDtypeStruct((8, d), WIDE), full((8, d))),
            (jax.ShapeDtypeStruct((d, half), LOW), full((d, half))),
        ]
    out = pl.pallas_call(
        with_deps(partial(ffn_bwd_kernel, final, n_dp), 1, 9, deps),
        out_shape=tuple(o[0] for o in outs),
        grid_spec=pltpu.PrefetchScalarGridSpec(
            num_scalar_prefetch=1,
            grid=(steps,),
            in_specs=[
                full((tokens, d)),
                pl.BlockSpec((tokens, BLOCK_FF), lambda j, c: (0, first + j)),
                pl.BlockSpec((d, BLOCK_FF), lambda j, c: (0, j)),
                pl.BlockSpec((BLOCK_FF, d), lambda j, c: (j, 0)),
                full((tokens, d)),
                full((tokens, d)) if final else ANY,
                full((tokens, d)),
                full(ctx.shape) if final else ANY,
                full(nv.shape),
            ]
            + [ANY] * len(deps),
            out_specs=[o[1] for o in outs],
            scratch_shapes=[
                pltpu.VMEM((tokens, d), WIDE),
                pltpu.VMEM((tokens, BLOCK_FF), LOW),
                pltpu.VMEM((tokens, BLOCK_FF), WIDE),
            ],
        ),
        compiler_params=VMEM,
        name="ffn_bwd",
        cost_estimate=LONG,
    )(place, low, slope, e, c, sofar, pre, hl, ctx, nv, *deps)
    out = list(out)
    for i in (0, 5) if final else (0,):
        out[i] = placed(out[i], place[1], n_dp)
    return out


def attend_back_kernel(
    start, ag_ref, probs_ref, qkv_ref, o0_ref, o1_ref, sofar_ref, grad_ref, sums_ref,
    dp_s, ds_s, cg_s,
):
    @pl.when(pl.program_id(0) == 0)
    def _():
        sums_ref[...] = jnp.zeros_like(sums_ref) if start else sofar_ref[...]

    width = o0_ref.shape[0]
    pairs = width // 128
    scale = jnp.asarray(HEAD_DIM ** (-0.5), LOW)
    keep = [lane_half((ag_ref.shape[0], 128), e) for e in range(2)]
    side = lambda value, e: jnp.where(keep[e], value, jnp.zeros_like(value))
    for half, o_ref in enumerate((o0_ref, o1_ref)):
        cg_s[...] = dot_nt(ag_ref[...], o_ref[...]).astype(LOW)
        first = half * 2 * pairs
        for pair in range(pairs):
            at = 3 * width * half + 128 * pair
            do = cg_s[:, 128 * pair : 128 * pair + 128]
            vp = qkv_ref[:, at + 2 * width : at + 2 * width + 128]
            for e in range(2):
                dp_s[2 * pair + e] = dot_nt(side(vp, e), do)
            dv = dot(probs_ref[0, first + 2 * pair], side(do, 0))
            dv = (dv + dot(probs_ref[0, first + 2 * pair + 1], side(do, 1))).astype(LOW)
            grad_ref[:, at + 2 * width : at + 2 * width + 128] = dv
            to = half * width + 128 * pair
            sums_ref[1:2, to : to + 128] += col_sum(dv.astype(WIDE))
        for head in range(2 * pairs):
            for left in range(0, ag_ref.shape[0], 128):
                cols = slice(left, left + 128)
                dp = dp_s[head, :, cols]
                probs = probs_ref[0, first + head, :, cols].astype(WIDE)
                inner = jnp.sum(dp * probs, axis=0, keepdims=True)
                ds_s[head, :, cols] = (probs * (dp - inner)).astype(LOW)
        for pair in range(pairs):
            at = 3 * width * half + 128 * pair
            qp = qkv_ref[:, at : at + 128] * scale
            kp = qkv_ref[:, at + width : at + width + 128] * scale
            dk = dot(ds_s[2 * pair], side(qp, 0)) + dot(ds_s[2 * pair + 1], side(qp, 1))
            dq = dot_tn(ds_s[2 * pair], side(kp, 0)) + dot_tn(ds_s[2 * pair + 1], side(kp, 1))
            dq = dq.astype(LOW)
            grad_ref[:, at : at + 128] = dq
            grad_ref[:, at + width : at + width + 128] = dk.astype(LOW)
            to = half * width + 128 * pair
            sums_ref[0:1, to : to + 128] += col_sum(dq.astype(WIDE))


def attend_back(ag, probs, qkv, o0, o1, first, count, before=None, deps=()):
    seqs, heads, seq_len, _ = probs.shape
    tokens, d = ag.shape
    width = o0.shape[0]
    full = lambda shape: pl.BlockSpec(shape, lambda s: (0,) * len(shape))
    rows = lambda cols: pl.BlockSpec((seq_len, cols), lambda s: (first + s, 0))
    sums = (8, 2 * width)
    start = before is None
    if not start:
        deps = (before[0],) + tuple(deps)
    return pl.pallas_call(
        with_deps(partial(attend_back_kernel, start), 0, 6, deps),
        out_shape=(
            jax.ShapeDtypeStruct((tokens, 6 * width), LOW),
            jax.ShapeDtypeStruct(sums, WIDE),
        ),
        grid=(count,),
        in_specs=[
            rows(d),
            pl.BlockSpec((1, heads, seq_len, seq_len), lambda s: (first + s, 0, 0, 0)),
            rows(6 * width),
            full(o0.shape),
            full(o1.shape),
            ANY if start else full(sums),
        ]
        + [ANY] * len(deps),
        out_specs=[rows(6 * width), full(sums)],
        input_output_aliases={} if start else {6: 0},
        scratch_shapes=[
            pltpu.VMEM((heads // 2, seq_len, seq_len), WIDE),
            pltpu.VMEM((heads // 2, seq_len, seq_len), LOW),
            pltpu.VMEM((seq_len, width), LOW),
        ],
        compiler_params=VMEM,
        name="attend_back",
        cost_estimate=LONG,
    )(ag, probs, qkv, o0, o1, ag if start else before[1], *deps)


def input_kernel(place, grad_ref, w0_ref, w1_ref, one_ref, out_ref, whole_ref):
    width = w0_ref.shape[2]
    total = one_ref[...]
    for i in range(6):
        w = (w0_ref, w1_ref)[i // 3][i % 3]
        total = total + dot_nt(grad_ref[:, i * width : (i + 1) * width], w)
    out_ref[...] = total.astype(LOW)
    whole_ref[...] = total.astype(LOW).astype(WIDE)


def input_side(place, grad, w0, w1, one, deps=()):
    tokens, d = one.shape
    block = min(ROWS, tokens)
    full = lambda a: pl.BlockSpec(a.shape, lambda s, c: (0,) * a.ndim)
    rows = lambda cols: pl.BlockSpec((block, cols), lambda s, c: (s, 0))
    return pl.pallas_call(
        with_deps(input_kernel, 1, 4, deps),
        out_shape=(
            jax.ShapeDtypeStruct((tokens, d), LOW),
            jax.ShapeDtypeStruct((2 * tokens, d), WIDE),
        ),
        grid_spec=pltpu.PrefetchScalarGridSpec(
            num_scalar_prefetch=1,
            grid=(tokens // block,),
            in_specs=[rows(grad.shape[1]), full(w0), full(w1), rows(d)] + [ANY] * len(deps),
            out_specs=[
                rows(d),
                pl.BlockSpec((block, d), lambda s, c: (c[0] * (tokens // block) + s, 0)),
            ],
        ),
        compiler_params=VMEM,
        name="input_side",
        cost_estimate=LONG,
    )(place, grad, w0, w1, one, *deps)


def bundle_kernel(one_ref, two_ref, pair_ref, b0_ref, b1_ref, mine_ref, theirs_ref):
    half = pair_ref.shape[1] // 2
    d = one_ref.shape[1]
    for i, (ref, b_ref) in enumerate(((mine_ref, b0_ref), (theirs_ref, b1_ref))):
        ref[...] = jnp.zeros_like(ref)
        ref[0:8] = one_ref[...]
        ref[8:16] = two_ref[...]
        for j in range(2):
            ref[16:17, j * half : (j + 1) * half] = pair_ref[j : j + 1, i * half : (i + 1) * half]
        for j in range(b_ref.shape[1] // d):
            ref[17 + j : 18 + j] = b_ref[:, j * d : (j + 1) * d]


def bundle(one, two, pair, mine, theirs, deps=()):
    out = jax.ShapeDtypeStruct((24, one.shape[1]), WIDE)
    spec = lambda a: pl.BlockSpec(a.shape, lambda: (0, 0))
    return pl.pallas_call(
        with_deps(bundle_kernel, 0, 5, deps),
        out_shape=(out, out),
        in_specs=[spec(a) for a in (one, two, pair, mine, theirs)] + [ANY] * len(deps),
        out_specs=(spec(out), spec(out)),
        name="bundle",
    )(one, two, pair, mine, theirs, *deps)


def gather_kernel(count, layout, place, z_ref, x_ref, y_ref, da_ref, db_ref, *refs):
    outs, scratch = refs[: len(layout)], list(refs[len(layout) :])
    tos = [scratch.pop(0) if kind == "flip" else out for (kind, _, _), out in zip(layout, outs)]
    block = z_ref.shape[0] // (count // 4)
    for apart in range(count):
        at = jnp.bitwise_xor(place[1], apart)
        first = reverse(apart >> 2, count // 4) * block
        ref = (z_ref, x_ref, y_ref, da_ref)[apart & 3]
        if apart & 3 == 3 and first >= da_ref.shape[0]:
            ref, first = db_ref, first - da_ref.shape[0]
        for (kind, left, right), to in zip(layout, tos):
            if kind == "deep":
                rows = block // to.shape[0]
                for i in range(to.shape[0]):
                    here = slice(first + i * rows, first + i * rows + rows)
                    to[i, pl.ds(pl.multiple_of(at * rows, 16), rows)] = ref[here]
            else:
                there = pl.ds(pl.multiple_of(at * block, 16), block)
                to[there] = ref[first : first + block, left:right]
    for (kind, _, _), out, to in zip(layout, outs, tos):
        if kind == "flip":
            out[...] = to[...].T


def gather_place(place, n_dp, layout, z, x, y, da, db, deps=()):
    rows, cols = z.shape[0] * 4, z.shape[1]
    block = rows // n_dp
    deep = [right - left for kind, left, right in layout if kind == "deep"]
    shapes = []
    for kind, left, right in layout:
        wide = right - left
        if kind == "deep":
            shapes.append((wide // cols, rows * cols // wide, cols))
        else:
            shapes.append((wide, rows) if kind == "flip" else (rows, wide))
    if (block // (shapes[0][0] if deep else 1)) % 16:
        plane = jnp.stack([z, x, y, jnp.concatenate([da, db])])
        blocks = plane.reshape(n_dp, block, cols)[spot(jnp.arange(n_dp) ^ place[1], n_dp)]
        outs = []
        for (kind, left, right), shape in zip(layout, shapes):
            if kind == "deep":
                outs.append(blocks.reshape(n_dp, shape[0], -1, cols).transpose(1, 0, 2, 3).reshape(shape))
            else:
                whole = blocks.reshape(rows, cols)[:, left:right]
                outs.append(whole.T if kind == "flip" else whole)
        return outs
    spec = lambda a: pl.BlockSpec(a.shape, lambda s, c: (0, 0))
    return pl.pallas_call(
        with_deps(partial(gather_kernel, n_dp, layout), 1, 5, deps),
        out_shape=[jax.ShapeDtypeStruct(shape, LOW) for shape in shapes],
        grid_spec=pltpu.PrefetchScalarGridSpec(
            num_scalar_prefetch=1,
            grid=(1,),
            in_specs=[spec(a) for a in (z, x, y, da, db)] + [ANY] * len(deps),
            out_specs=[pl.BlockSpec(s, lambda i, c, n=len(s): (0,) * n) for s in shapes],
            scratch_shapes=[
                pltpu.VMEM(shape[::-1], LOW)
                for (kind, _, _), shape in zip(layout, shapes)
                if kind == "flip"
            ],
        ),
        compiler_params=VMEM,
        name="gather_place",
        cost_estimate=LONG,
    )(place, z, x, y, da, db, *deps)


def combine_kernel(plan, *refs):
    outs = refs[len(refs) - len(plan) :]
    for parts, out in zip(plan, outs):
        rows = out.shape[0] // len(parts)
        for i, terms in enumerate(parts):
            sides = []
            for inputs in terms:
                pieces = [refs[r][...].astype(WIDE) for r in inputs]
                sides.append(pieces[0] if not pieces[1:] else jnp.concatenate(pieces, axis=1))
            out[i * rows : (i + 1) * rows] = sum(sides[1:], sides[0]).astype(LOW)


def cut(terms, rows):
    take = lambda a, n: a[n * rows : (n + 1) * rows].astype(WIDE)
    sides = [jnp.concatenate([take(a, n) for a, n in term], axis=1) for term in terms]
    return sum(sides[1:], sides[0])


class Blocks:
    def __init__(self, rows):
        self.rows, self.arrays, self.specs = rows, [], []

    def add(self, terms):
        plan = []
        for term in terms:
            plan.append([])
            for array, number in term:
                plan[-1].append(len(self.arrays))
                self.arrays.append(array)
                self.specs.append(
                    pl.BlockSpec((self.rows, array.shape[1]), lambda i, number=number: (number, 0))
                )
        return plan


def combine(results, rows, deps=()):
    if rows % 16:
        return [
            jnp.concatenate([cut(terms, rows) for terms in parts]).astype(LOW) for parts in results
        ]
    blocks = Blocks(rows)
    plan = [[blocks.add(terms) for terms in parts] for parts in results]
    shapes = [
        (rows * len(parts), sum(a.shape[1] for a, _ in parts[0][0])) for parts in results
    ]
    return pl.pallas_call(
        with_deps(partial(combine_kernel, plan), 0, len(blocks.arrays), deps),
        out_shape=[jax.ShapeDtypeStruct(s, LOW) for s in shapes],
        grid=(1,),
        in_specs=blocks.specs + [ANY] * len(deps),
        out_specs=[pl.BlockSpec(s, lambda i: (0, 0)) for s in shapes],
        compiler_params=VMEM,
        name="combine",
        cost_estimate=NO_COST,
    )(*blocks.arrays, *deps)


def adamw_step(master, first_moment, second_moment, gradient, decay_rate):
    first_new = FIRST_DECAY * first_moment + (1.0 - FIRST_DECAY) * gradient
    second_new = SECOND_DECAY * second_moment + (1.0 - SECOND_DECAY) * gradient * gradient
    first_fixed = first_new / (1.0 - FIRST_DECAY**STEP)
    second_fixed = second_new / (1.0 - SECOND_DECAY**STEP)
    direction = first_fixed / (jnp.sqrt(second_fixed) + EPSILON)
    master_new = master - LEARN_RATE * (direction + decay_rate * master)
    return (master_new, first_new, second_new)


def update_kernel(plan, widths, deep, *refs):
    inputs, rest = refs[: len(refs) - 6 * len(widths) - 1], refs[len(refs) - 6 * len(widths) - 1 :]
    states, outs, copy_ref = rest[: 3 * len(widths)], rest[3 * len(widths) : -1], rest[-1]
    gradient = 0.0
    for term in plan:
        pieces = [inputs[r][...].astype(WIDE) for r in term]
        gradient = gradient + (pieces[0] if not pieces[1:] else jnp.concatenate(pieces, axis=1))
    rows, at = gradient.shape[0], 0
    for i, width in enumerate(widths):
        mine, to = states[3 * i : 3 * i + 3], outs[3 * i : 3 * i + 3]
        groups = deep or 1
        for j in range(groups):
            part = gradient[:, at : at + width // groups]
            old = [ref[j] if deep else ref[...] for ref in mine]
            new = adamw_step(*old, part, WEIGHT_DECAY)
            for ref, value in zip(to, new):
                if deep:
                    ref[j] = value
                else:
                    ref[...] = value
            if deep:
                copy_ref[j * rows : (j + 1) * rows] = new[0].astype(LOW)
            else:
                copy_ref[:, at : at + width] = new[0].astype(LOW)
            at += width // groups


def update(terms, rows, states, deep=0):
    count = lambda s: s[0].shape[0] * s[0].shape[2] if deep else s[0].shape[1]
    widths = [count(s) for s in states]
    total = sum(widths)
    if rows % 16:
        gradient, at, news = cut(terms, rows), 0, []
        for state, width in zip(states, widths):
            part = gradient[:, at : at + width]
            if deep:
                part = jnp.stack(jnp.split(part, deep, axis=1))
            news.append(adamw_step(*state, part, WEIGHT_DECAY))
            at += width
        copies = [n[0].astype(LOW) for n in news]
        if deep:
            return news, copies[0].reshape(-1, copies[0].shape[2])
        return news, jnp.concatenate(copies, axis=1)
    blocks = Blocks(rows)
    plan = blocks.add(terms)
    spec = lambda a: pl.BlockSpec(a.shape, lambda i: (0,) * a.ndim)
    flat = [a for state in states for a in state]
    copy = jax.ShapeDtypeStruct((rows * deep, total // deep) if deep else (rows, total), LOW)
    outs = [jax.ShapeDtypeStruct(a.shape, WIDE) for a in flat] + [copy]
    out = pl.pallas_call(
        partial(update_kernel, plan, widths, deep),
        out_shape=outs,
        grid=(1,),
        in_specs=blocks.specs + [spec(a) for a in flat],
        out_specs=[spec(a) for a in outs],
        compiler_params=VMEM,
        name="update",
        cost_estimate=NO_COST,
    )(*blocks.arrays, *flat)
    return [out[3 * i : 3 * i + 3] for i in range(len(states))], out[-1]


def put_kernel(place, other_ref, whole_ref, out_ref):
    out_ref[...] = other_ref[...].astype(out_ref.dtype)


def put_other(place, other, whole, deps=()):
    tokens, d = other.shape
    return pl.pallas_call(
        with_deps(put_kernel, 1, 2, deps),
        out_shape=jax.ShapeDtypeStruct(whole.shape, whole.dtype),
        grid_spec=pltpu.PrefetchScalarGridSpec(
            num_scalar_prefetch=1,
            grid=(1,),
            in_specs=[pl.BlockSpec((tokens, d), lambda s, c: (0, 0)), ANY] + [ANY] * len(deps),
            out_specs=pl.BlockSpec((tokens, d), lambda s, c: (1 - c[0], 0)),
        ),
        input_output_aliases={2: 0},
        compiler_params=VMEM,
        name="put_other",
        cost_estimate=LONG,
    )(place, other, whole, *deps)


def swap(value):
    return lax.ppermute(value, "tensor", [(0, 1), (1, 0)])


def across(value, apart, count):
    return lax.ppermute(value, "dp", [(i, i ^ apart) for i in range(count)])


def far_digits(count, direct):
    weights = [1 << bit for bit in range(2, count.bit_length() - 1)]
    size = 2 if direct else 1
    return [weights[i : i + size] for i in range(0, len(weights), size)]


def distances(digit):
    out = [0]
    for weight in digit:
        out = [d + e for d in out for e in (0, weight)]
    return out


def scatter_flow(mine, came, count, direct=False):
    rows, width = mine.shape
    block = rows // 8

    def part(y, x, half):
        at = (y * 2 + x) * 2 + half
        return [[(mine, at)], [(c, at) for c in came]]

    to_x, to_y = combine(
        [[part(0, 1, 0), part(1, 1, 0)], [part(1, 0, 1), part(1, 1, 1)]], block
    )
    send_both = lambda v: [across(v[0], 1, count), across(v[1], 2, count)]
    from_x, from_y = yield [to_x, to_y], send_both
    to_y, to_x = combine(
        [[part(1, 0, 0) + [[(from_x, 1)]]], [part(0, 1, 1) + [[(from_y, 1)]]]], block
    )
    last_x, last_y = yield [to_x, to_y], send_both
    upper = part(0, 0, 0) + [[(from_x, 0)], [(last_y, 0)]]
    lower = part(0, 0, 1) + [[(from_y, 0)], [(last_x, 0)]]

    half = block
    terms = None
    for digit in far_digits(count, direct):
        apart = distances(digit)
        if terms is None:
            half = half * 2 // len(apart)
            pieces = [upper, lower]
            if len(apart) == 4:
                pieces = [divide(p, 2, i) for p in pieces for i in range(2)]
        else:
            half = half // len(apart)
            pieces = [divide(terms, len(apart), i) for i in range(len(apart))]
        sends = combine([[piece] for piece in pieces[1:]], half)
        came = yield (
            sends,
            lambda v, apart=apart: [across(p, d, count) for p, d in zip(v, apart[1:])],
        )
        terms = pieces[0] + [[(c, 0)] for c in came]
    return terms, half


def divide(terms, members, number):
    return [[(a, n * members + number) for a, n in term] for term in terms]


def gather_flow(shard, count, direct=False):
    held = shard
    for digit in reversed(far_digits(count, direct)):
        apart = distances(digit)
        came = yield (
            [held],
            lambda v, apart=apart: [across(v[0], d, count) for d in apart[1:]],
        )
        (held,) = combine([[[[(h, 0)]] for h in [held] + list(came)]], held.shape[0])
    half = held.shape[0] // 2
    x, y = yield [held], lambda v: [across(v[0], 1, count), across(v[0], 2, count)]
    upper, lower = combine([[[[(x, 0)]]], [[[(y, 1)]]]], half)
    both = yield [upper, lower], lambda v: [across(v[0], 2, count), across(v[1], 1, count)]
    return held, x, y, both[0], both[1]


def total_flow(mine, others, count):
    (came,) = yield [others], lambda v: [swap(v[0])]
    total = mine + came
    apart = 1
    while apart < count:
        (came,) = yield [total], lambda v, apart=apart: [across(v[0], apart, count)]
        total = total + came
        apart *= 2
    return total


def behind(value, after):
    return lax.optimization_barrier((value, after))[0]


class Flow:
    def __init__(self, steps, then=None):
        self.steps, self.then = steps, then
        self.came, self.result, self.done = None, None, False
        self.sends = ()

    def advance(self, after=None):
        if after is not None and self.came is not None:
            self.came = behind(list(self.came), after)
        while not self.done:
            try:
                sends, send = self.steps.send(self.came)
            except StopIteration as stop:
                if self.then is None:
                    self.result, self.done = stop.value, True
                    return []
                self.steps, self.then = self.then(stop.value)
                self.came = None
                continue
            self.came, self.sends = send(sends), list(sends)
            return self.sends
        return []

    def finish(self):
        while not self.done:
            self.advance()
        return self.result


def local(
    n_dp,
    hidden_in,
    grad_out,
    lengths,
    key_mask,
    triple_weight,
    outward_weight,
    expand_weight,
    contract_weight,
    triple_master,
    triple_first,
    triple_second,
    outward_master,
    outward_first,
    outward_second,
    expand_master,
    expand_first,
    expand_second,
    contract_master,
    contract_first,
    contract_second,
    pair_bias,
    pair_first,
    pair_second,
    expand_bias,
    expand_bias_first,
    expand_bias_second,
    norm_vectors,
    vectors_first,
    vectors_second,
):
    core = lax.axis_index("tensor")
    rank = lax.axis_index("dp")

    own = pair_bias.shape[1]
    n_bias = expand_bias.shape[0]
    place = jnp.stack([core, rank]).astype(jnp.int32)
    bias_row = expand_bias[None]
    triple_other = swap(triple_weight)
    pair_other = swap(pair_bias)
    outward_other = swap(outward_weight)
    expand_here, contract_here, bias_here = behind(
        [expand_weight, contract_weight, bias_row], [triple_other, pair_other, outward_other]
    )
    bias_other = swap(bias_here)
    expand_other = swap(expand_here)
    contract_other = swap(contract_here)
    updates = {}

    def contract_then(summed):
        state = (contract_master.T, contract_first.T, contract_second.T)
        (updates["contract"],), copy = update(*summed, [state])
        return gather_flow(copy, n_dp), None

    def expand_then(summed):
        states = [
            (expand_master, expand_first, expand_second),
            (outward_master.T, outward_first.T, outward_second.T),
        ]
        (updates["expand"], updates["outward"]), copy = update(*summed, states)
        return gather_flow(copy, n_dp), None

    def triple_then(summed):
        state = (triple_master, triple_first, triple_second)
        (updates["triple"],), copy = update(*summed, [state], 3)
        return gather_flow(copy, n_dp), None

    qkv, probs, context, pre_one = attend(
        place, lengths, hidden_in, key_mask, triple_weight, triple_other, outward_weight,
        outward_other, pair_bias, pair_other, norm_vectors,
    )
    active, slope, layer_own, pre_two_grad, branch_grad, hidden_low, sums_two, layer_out = ffn_fwd(
        place, pre_one, grad_out, expand_weight, expand_other, contract_weight, contract_other,
        bias_row, bias_other, norm_vectors,
    )

    weight = partial(weight_grad, place, n_dp)
    contract_theirs = weight(branch_grad, active, 2, 2, n_bias // 2)
    contract_mine = weight(branch_grad, active, 0, 2, n_bias // 2, deps=(contract_theirs,))
    contract_flow = Flow(scatter_flow(contract_mine, [swap(contract_theirs)], n_dp, True), contract_then)
    sends = contract_flow.advance()
    expand_theirs, bias_theirs, hidden_sofar = ffn_bwd(
        place, n_dp, False, branch_grad, slope, expand_other, contract_other, pre_two_grad,
        pre_two_grad, hidden_low, context, norm_vectors, deps=sends,
    )
    sends = contract_flow.advance(bias_theirs)
    expand_came = swap(behind(expand_theirs, sends))
    expand_mine, bias_mine, pre_one_grad, attention_grad, sums_one, outward_theirs = ffn_bwd(
        place, n_dp, True, branch_grad, slope, expand_weight, contract_weight, hidden_sofar,
        pre_one, hidden_low, context, norm_vectors, deps=sends,
    )
    sends = contract_flow.advance(sums_one)
    outward_came = swap(behind(outward_theirs, sends))
    expand_flow = Flow(scatter_flow(expand_mine, [expand_came, outward_came], n_dp), expand_then)
    sends = sends + expand_flow.advance()
    projected_grad, sums_pair = attend_back(
        attention_grad, probs, qkv, outward_weight, outward_other, 0, lengths.shape[0] // 2,
        deps=sends,
    )
    layer_other = swap(behind(layer_own, sends))
    sends = contract_flow.advance(sums_pair)
    sends = sends + expand_flow.advance(sends)
    vectors = bundle(sums_one, sums_two, sums_pair, bias_mine, bias_theirs)
    vector_flow = Flow(total_flow(*vectors, n_dp))
    sends = sends + vector_flow.advance()
    triple_theirs = weight(hidden_in, projected_grad, 1, 1, 3 * own, deps=sends)
    sends = expand_flow.advance(triple_theirs) + vector_flow.advance(triple_theirs)
    sends = sends + contract_flow.advance(triple_theirs)
    triple_mine = weight(hidden_in, projected_grad, 0, 1, 3 * own, deps=sends)
    triple_came = swap(behind(triple_theirs, sends))
    triple_flow = Flow(scatter_flow(triple_mine, [triple_came], n_dp, True), triple_then)
    sends = triple_flow.advance()
    sends = sends + expand_flow.advance(triple_mine) + contract_flow.advance(triple_mine)
    input_own, input_grad = input_side(
        place, projected_grad, triple_weight, triple_other, pre_one_grad, deps=sends
    )
    triple_flow.advance(input_own)
    expand_flow.advance(triple_flow.sends)
    vector_flow.advance(triple_flow.sends)
    layer_out = put_other(place, layer_other, layer_out, deps=expand_flow.sends + vector_flow.sends)
    contract_flow.advance(layer_out)
    triple_flow.advance(contract_flow.sends)
    expand_flow.advance(triple_flow.sends)
    vector_flow.advance(expand_flow.sends)
    input_other = swap(behind(input_own, expand_flow.sends))
    input_grad = put_other(
        place, input_other, input_grad, deps=expand_flow.sends + vector_flow.sends
    )
    gather = partial(gather_place, place, n_dp)
    triple_flow.advance(input_grad)
    expand_flow.advance(triple_flow.sends)
    vector_flow.advance(input_grad)
    triple_flow.advance(expand_flow.sends)
    contract_flow.finish()
    (contract_copy,) = gather(
        (("flip", 0, n_bias),),
        *contract_flow.result,
        deps=triple_flow.sends + expand_flow.sends + vector_flow.sends,
    )
    triple_flow.advance(contract_copy)
    vector_flow.advance(contract_copy)
    expand_flow.advance(triple_flow.sends)
    triple_flow.advance(expand_flow.sends)
    expand_flow.finish()
    expand_copy, outward_copy = gather(
        (("plain", 0, n_bias), ("flip", n_bias, n_bias + own)),
        *expand_flow.result,
        deps=triple_flow.sends + vector_flow.sends,
    )
    vector_sum = vector_flow.finish()
    triple_flow.finish()
    (triple_copy,) = gather((("deep", 0, 3 * own),), *triple_flow.result, deps=(expand_copy,))
    vector_total = jnp.stack([vector_sum[i] for i in (0, 8, 1, 2, 9, 10)])
    pair_total = vector_sum[16].reshape(2, own)
    widen_total = vector_sum[17:].reshape(-1)[:n_bias]
    contract_new, expand_new = updates["contract"], updates["expand"]
    outward_new, triple_new = updates["outward"], updates["triple"]
    pair_new = adamw_step(pair_bias, pair_first, pair_second, pair_total, 0.0)
    widen_new = adamw_step(expand_bias, expand_bias_first, expand_bias_second, widen_total, 0.0)
    vectors_new = adamw_step(norm_vectors, vectors_first, vectors_second, vector_total, 0.0)
    return (
        layer_out,
        input_grad,
        triple_new[0],
        triple_new[1],
        triple_new[2],
        triple_copy,
        outward_new[0].T,
        outward_new[1].T,
        outward_new[2].T,
        outward_copy,
        expand_new[0],
        expand_new[1],
        expand_new[2],
        expand_copy,
        contract_new[0].T,
        contract_new[1].T,
        contract_new[2].T,
        contract_copy,
        pair_new[0],
        pair_new[1],
        pair_new[2],
        widen_new[0],
        widen_new[1],
        widen_new[2],
        vectors_new[0],
        vectors_new[1],
        vectors_new[2],
    )


def solution(mesh):
    matrix_specs = (
        P(None, "dp", "tensor"),
        P("tensor", "dp"),
        P("dp", "tensor"),
        P("tensor", "dp"),
    )
    copy_specs = (P(None, None, "tensor"), P("tensor", None), P(None, "tensor"), P("tensor", None))
    vector_specs = (P(None, "tensor"),) * 3 + (P("tensor"),) * 3 + (P(),) * 3
    in_specs = (
        (P("dp", None), P("dp", None), P("dp"), P("dp", None))
        + copy_specs
        + tuple(spec for spec in matrix_specs for _ in range(3))
        + vector_specs
    )
    out_specs = (P("dp", None), P("dp", None))
    for spec, copied in zip(matrix_specs, copy_specs):
        out_specs += (spec,) * 3 + (copied,)
    out_specs += vector_specs
    return jax.shard_map(
        partial(local, mesh.shape["dp"]),
        mesh=mesh,
        in_specs=in_specs,
        out_specs=out_specs,
        check_vma=False,
    )
```
